128 devices in a mesh: wide: 32 (over z, y, x_lo), narrow: 4 (over x_hi, core).
Axes of the slice: x: 4 (x_hi: 2, x_lo: 2; x = x_hi * 2 + x_lo), y: 4, z: 4, core: 2. Of those that a mesh axis runs over, the one named last changes fastest.
Arguments:
- embedded: bfloat16 [16384, 4096], P('wide'), may hold values from -6 to 6
- cotangent: bfloat16 [16384, 4096], P('wide', 'narrow'), may hold values from -3 to 3
- cross_weight: bfloat16 [4096, 4096], P(None, 'narrow'), may hold values from -0.09375 to 0.09375
- cross_bias: float32 [4096], P('narrow'), may hold values from -6 to 6
- bag_size: int32 [16384, 32], P('wide'), may hold values from 1 to 2
- row_owner: int32 [4, 16384, 16, 1], P('narrow', 'wide'), may hold values from 0 to 31; in each aligned block of 8192 rows (0 to 8191, 8192 to 16383, ..., all dimensions but the last counted through in order) at most 512 rows name the same one
- row_id: int32 [4, 16384, 16], P('narrow', 'wide'), may hold values from 0 to 2047
- emb_table: float32 [65536, 128], P('wide'), may hold values from -6 to 6
- adagrad_state: float32 [65536], P('wide'), may hold values from 0.1 to 4
Outputs:
- weight_grad: float32 [4096, 4096], P('wide', 'narrow')
- bias_grad: float32 [4096], P('narrow')
- new_table: float32 [65536, 128], P('wide')
- new_state: float32 [65536], P('wide')
The draws below stay inside these ranges and needn't reach their ends.
Inputs may be any that keep to these rules, and one draw needn't show every extreme that they name: `row_owner`: within the entries of one device (one index n of the first dimension and 512 aligned samples), no owner is named more than 512 times, a bound that some block reaches.
All inputs are finite; a program needn't handle non-finite values.
Results may differ from the reference program's by a relative error of at most 0.007.
Values may be sent and summed in bfloat16 or wider, within the bound.
No kernel may reach another device: no remote copies, remote signals or barrier semaphores. Data moves between devices by JAX's collectives and lax.ppermute only.
A program may use at most 128 MiB of HBM per device.

```python
import math
import jax
import jax.numpy as jnp
import numpy as np
from jax import lax

E = 128
F = 32
BAG = 2
B_DEV = 512
ROWS_DEV = 2048
D = 4096
FP = 8
BATCH = 16384
ROWS = 65536
CAP = 512
N_WIDE = 32
N_NARROW = 4


def with_ends(drawn, own_key, smallest, largest):
    extent = drawn.shape
    place = [jax.random.randint(jax.random.fold_in(own_key, axis), (), 0, extent[axis]) for axis in range(len(extent))]
    drawn = drawn.at[tuple(place)].set(smallest)
    longest = extent.index(max(extent))
    place[longest] = (place[longest] + 1) % extent[longest]
    return drawn.at[tuple(place)].set(largest)


def raised(array, own_key, source, target, blocks, factor):
    def block_of(dim):
        return (jnp.arange(array.shape[dim]) // (array.shape[dim] // blocks)).reshape((-1,) + (1,) * (array.ndim - 1 - dim))

    near = jax.random.permutation(own_key, blocks)[block_of(target)]
    other_side = (block_of(target) + blocks // 2) % blocks
    return jnp.where((block_of(source) == near) | (block_of(source) == other_side), factor * array, array)


def levels(stream_key, extent, cuts, low, largest):
    factor_of, own = 1.0, jax.random.fold_in(stream_key, 6)
    for axis_at, blocks in cuts:
        steps = jnp.exp(jax.random.uniform(jax.random.fold_in(own, axis_at), (blocks,), jnp.float32, low / len(cuts), largest / len(cuts)))
        factor_of = factor_of * jnp.repeat(steps, extent[axis_at] // blocks).reshape([-1 if axis == axis_at else 1 for axis in range(len(extent))])
    return factor_of


def shared_out(own_key, own, number, rows, count, top, bound, slope):
    sequence = jax.random.permutation(own_key, count)
    heavy_load, ordinary = load_shares(count, rows * top, bound, slope, True), load_shares(count, rows * top, bound, slope, False)
    places = jnp.arange(count)

    def named(tallies, offset_by):
        used = int((tallies > 0).sum())
        fixed = max(1, used // 4)
        shifted = fixed + (places - fixed + offset_by * (used - fixed)) % max(1, count - fixed)
        return jnp.zeros((count,), jnp.int32).at[sequence[jnp.where(places < fixed, places, shifted)]].set(jnp.asarray(tallies, jnp.int32))

    tallies = jnp.where(number % 4 == 0, named(heavy_load, number // 4), named(ordinary, number - number // 4 - 1))
    mixed = jax.random.permutation(jax.random.fold_in(own, 3), count)
    giver, taker = mixed[0:count // 2 * 2:2], mixed[1:count // 2 * 2:2]
    slack = jnp.minimum(tallies[giver] - 1, bound - tallies[taker]) // 2
    slack = jnp.where((giver == sequence[0]) | (taker == sequence[0]) | (tallies[taker] == 0), 0, jnp.maximum(slack, 0))
    shifted = jax.random.randint(jax.random.fold_in(own, 4), (count // 2,), 0, 1 << 20) % (slack + 1)
    tallies = tallies.at[giver].add(-shifted).at[taker].add(shifted)
    items = jnp.searchsorted(jnp.cumsum(tallies), jnp.arange(rows * top), side="right").astype(jnp.int32)
    grid = items.reshape(top, rows).T
    grid = grid[jax.random.permutation(jax.random.fold_in(own, 1), rows)]
    offset_by = jax.random.randint(jax.random.fold_in(own, 2), (rows, 1), 0, top)
    return jnp.take_along_axis(grid, (jnp.arange(top)[None, :] + offset_by) % top, axis=1)


def load_shares(number_of, total, bound, skew, full):
    portions = [(1 << 20) // math.isqrt(standing ** skew) + 1 for standing in range(1, number_of + 1)]
    largest = bound if full else min(bound, max(-(-total // number_of), total * portions[0] // sum(portions)))
    least = 1 if total - largest >= number_of - 1 else 0
    holding, rest = [largest] + [least] * (number_of - 1), total - largest - least * (number_of - 1)
    while rest > 0:
        candidates = [i for i in range(1, number_of) if holding[i] < largest] or [i for i in range(1, number_of) if holding[i] < bound]
        whole, left = sum([portions[i] for i in candidates]), rest
        for i in candidates:
            more = min(bound - holding[i], max(1, left * portions[i] // whole), rest)
            holding[i] = holding[i] + more
            rest = rest - more
    return np.array(holding)


def scatter_about(own_key, dims, deviation, limit, cuts=(), kind=jnp.bfloat16):
    drawn = jax.random.normal(own_key, dims, jnp.float32) * deviation
    if len(cuts) > 0:
        drawn = levels(own_key, dims, cuts, -0.22, 0.18) * drawn
    return jnp.clip(drawn, min=-limit, max=limit).astype(kind)


def noise_with(key, shape, deviation, reach, cuts, heavy, kind=jnp.bfloat16):
    entries = deviation * jax.random.normal(key, shape, jnp.float32)
    if cuts:
        entries = entries * levels(key, shape, cuts, -0.22, 0.18)
    return jnp.clip(raised(entries, jax.random.fold_in(key, 3), *heavy), -reach, reach).astype(kind)


def setup_inputs(seed: int = 0) -> dict:
    arg_keys = jax.random.split(jax.random.key(seed), 10)
    embedded = noise_with(arg_keys[0], (BATCH, D), 1.0, 6.0, ((0, 32),), (0, 1, 32, 2.75))
    cotangent = scatter_about(arg_keys[1], (BATCH, D), 0.5, 3.0, ((0, 32), (1, 4)))
    cross_weight = scatter_about(arg_keys[2], (D, D), D ** -0.5, 0.09375, ((1, 4),))
    cross_bias = scatter_about(arg_keys[3], (D,), 1.0, 6.0, ((0, 4),), jnp.float32)
    bag_size = with_ends(jax.random.randint(arg_keys[4], (BATCH, F), 1, BAG + 1), jax.random.fold_in(arg_keys[4], 1), 1, BAG).astype(jnp.int32)
    row_owner_keys = jax.random.split(jax.random.fold_in(arg_keys[5], 1), N_NARROW * BATCH * (FP * BAG) // (B_DEV * FP * BAG))
    row_owner_turns = jax.random.permutation(jax.random.fold_in(arg_keys[5], 3), N_NARROW * BATCH * (FP * BAG) // (B_DEV * FP * BAG))
    row_owner = jax.vmap(lambda own, number: shared_out(jax.random.fold_in(arg_keys[5], 2), own, number, B_DEV * FP * BAG, N_WIDE, 1, CAP, 1))(row_owner_keys, row_owner_turns).reshape((N_NARROW, BATCH, FP * BAG, 1))
    row_id = with_ends(jax.random.randint(arg_keys[6], (N_NARROW, BATCH, FP * BAG), 0, ROWS_DEV), jax.random.fold_in(arg_keys[6], 1), 0, ROWS_DEV - 1).astype(jnp.int32)
    emb_table = scatter_about(arg_keys[7], (ROWS, E), 1.0, 6.0, ((0, 32),), jnp.float32)
    adagrad_state = jnp.clip(jnp.exp(math.log(4.0) - 3.6888794 * jax.random.uniform(arg_keys[8], (ROWS,), jnp.float32) ** levels(arg_keys[8], (ROWS,), ((0, 32),), -0.2, 0.2)), 0.1, 4.0)
    return {"embedded": embedded, "cotangent": cotangent, "cross_weight": cross_weight, "cross_bias": cross_bias, "bag_size": bag_size, "row_owner": row_owner, "row_id": row_id, "emb_table": emb_table, "adagrad_state": adagrad_state}


LEARN_RATE = 0.3

def reference(embedded, cotangent, cross_weight, cross_bias, bag_size, row_owner, row_id, emb_table, adagrad_state):
    cross_out = jnp.dot(embedded, cross_weight, preferred_element_type=jnp.float32) + cross_bias
    grad_out = cotangent.astype(jnp.float32)
    scaled = (grad_out * embedded.astype(jnp.float32)).astype(jnp.bfloat16)
    norm_factor = 1.0 / math.sqrt(BATCH)
    weight_grad = lax.dot_general(embedded, scaled, (((0,), (0,)), ((), ())), preferred_element_type=jnp.float32) * norm_factor
    bias_grad = lax.optimization_barrier(jnp.sum(scaled.astype(jnp.float32), axis=0)) * norm_factor
    backward = lax.dot_general(scaled, cross_weight, (((1,), (1,)), ((), ())), preferred_element_type=jnp.float32)
    pooled = (grad_out + backward + grad_out * cross_out).astype(jnp.bfloat16)
    features = pooled.reshape(BATCH, F, E)
    row_grad = jnp.zeros((ROWS, E), jnp.float32)
    for group in range(N_NARROW):
        grads = features[:, group * FP:(group + 1) * FP, :]
        bag_len = bag_size[:, group * FP:(group + 1) * FP]
        is_live = jnp.arange(BAG, dtype=jnp.int32)[None, None, :] < bag_len[:, :, None]
        values = jnp.where(is_live[:, :, :, None], grads[:, :, None, :], jnp.zeros((), jnp.bfloat16)).reshape(-1, E)
        targets = row_owner[group].reshape(-1) * ROWS_DEV + row_id[group].reshape(-1)
        row_grad = row_grad + jax.ops.segment_sum(values.astype(jnp.float32), targets.astype(jnp.int32), num_segments=ROWS)
    new_state = adagrad_state + lax.optimization_barrier(jnp.mean(row_grad * row_grad, axis=1))
    new_table = emb_table - LEARN_RATE * row_grad / jnp.sqrt(new_state)[:, None]
    return (weight_grad, bias_grad, new_table, new_state)
```

```python
import math

import jax
import jax.numpy as jnp
from jax import lax
from jax.experimental import pallas as pl
from jax.experimental.pallas import tpu as pltpu
from jax.sharding import PartitionSpec as P

LEARN_RATE = 0.3
E = 128
N_WIDE = 32
CAP = 512
ID_ROWS = 16
BLOCK = CAP + ID_ROWS
N_ROWS = 2048
HI = 4
LO = N_ROWS // HI
F32 = jnp.float32
BF16 = jnp.bfloat16


def z_perm(d):
    return [(i, ((i // 8 + d) % 4) * 8 + i % 8) for i in range(N_WIDE)]


def y_perm(d):
    return [(i, (i // 8) * 8 + (((i // 2) % 4 + d) % 4) * 2 + i % 2) for i in range(N_WIDE)]


X_LO = [(i, i ^ 1) for i in range(N_WIDE)]
CORE = [(i, i ^ 1) for i in range(4)]
X_HI = [(i, i ^ 2) for i in range(4)]


def slot_positions(onehot):
    entries, n_wide = onehot.shape
    block_len = 512
    block_count = entries // block_len
    blocked = onehot.reshape(block_count, block_len, n_wide)
    lower = (jnp.arange(block_len)[:, None] > jnp.arange(block_len)[None, :]).astype(BF16)
    within = jnp.einsum("ij,bjn->bin", lower, blocked, preferred_element_type=F32)
    block_total = jnp.sum(blocked.astype(F32), axis=1)
    before = jnp.cumsum(block_total, axis=0) - block_total
    counted = (within + before[:, None, :]) * blocked.astype(F32)
    position = jnp.sum(counted, axis=2).reshape(entries).astype(jnp.int32)
    return position, jnp.sum(block_total, axis=0)


def scatter_kernel(slots_ref, base_ref, far_ref, ids_ref, out_ref, rows):
    dump = N_WIDE * CAP

    def clear(i, _):
        rows[pl.ds(pl.multiple_of(i * 64, 64), 64), :] = jnp.zeros((64, E), F32)
        return 0

    lax.fori_loop(0, dump // 64, clear, 0)

    def place(i, _):
        first = pl.multiple_of(i * 16, 16)
        for f in range(8):
            cols = slice(f * E, (f + 1) * E)
            tile = base_ref[pl.ds(first, 16), cols] + far_ref[pl.ds(first, 16), cols].astype(F32)
            for b in range(16):
                row = tile[b : b + 1, :]
                for j in range(2):
                    slot = slots_ref[(first + b) * 16 + 2 * f + j]
                    rows[pl.ds(slot, 1), :] = row
        return 0

    lax.fori_loop(0, base_ref.shape[0] // 16, place, 0)

    def narrow_down(w, _):
        out_ref[w, :CAP, :] = rows[pl.ds(pl.multiple_of(w * CAP, CAP), CAP), :].astype(BF16)
        out_ref[w, CAP:, :] = ids_ref[w]
        return 0

    lax.fori_loop(0, N_WIDE, narrow_down, 0)


def scatter_entries(slots, base, far, ids):
    vmem = pl.BlockSpec(memory_space=pltpu.VMEM)
    return pl.pallas_call(
        scatter_kernel,
        out_shape=jax.ShapeDtypeStruct((N_WIDE, BLOCK, E), BF16),
        in_specs=[pl.BlockSpec(memory_space=pltpu.SMEM), vmem, vmem, vmem],
        out_specs=vmem,
        scratch_shapes=[pltpu.VMEM((N_WIDE * CAP + 8, E), F32)],
        compiler_params=pltpu.CompilerParams(vmem_limit_bytes=40 << 20),
        cost_estimate=pl.CostEstimate(flops=0, bytes_accessed=40 << 20, transcendentals=0),
        name="place_entries",
    )(slots, base, far, ids)


def sums_kernel(count_ref, recv_ref, out_ref, total):
    total[...] = jnp.zeros_like(total)
    lane_rows = lax.broadcasted_iota(jnp.int32, (LO, E), 0)

    def add_half(w, half):
        ids = recv_ref[w, CAP:, :].astype(F32)
        row = (ids[0:4, :] * 64.0 + ids[4:8, :]).astype(jnp.int32) - 1
        hi = row // LO
        lo = row - hi * LO
        hi = jnp.where(row < 0, -1, hi)
        hi_col = jnp.transpose(jnp.concatenate([hi, hi], axis=0).astype(F32), (1, 0))
        left, right = [], []
        for j in range(half * 2, half * 2 + 2):
            left.append(jnp.where(lane_rows == lo[j : j + 1, :], 1.0, 0.0).astype(BF16))
            v = recv_ref[w, j * E : (j + 1) * E, :]
            own = jnp.broadcast_to(hi_col[:, j : j + 1], (E, E)).astype(BF16)
            right.append(
                jnp.concatenate(
                    [jnp.where(own == BF16(h), v, BF16(0)) for h in range(HI)], axis=1
                )
            )
        total[...] += jnp.dot(
            jnp.concatenate(left, axis=1),
            jnp.concatenate(right, axis=0),
            preferred_element_type=F32,
        )

    def source(w, _):
        count = count_ref[w]
        for half in range(2):

            @pl.when(count > half * 2 * E)
            def _():
                add_half(w, half)

        return 0

    lax.fori_loop(0, N_WIDE, source, 0)
    for h in range(HI):
        out_ref[h * LO : (h + 1) * LO, :] = total[:, h * E : (h + 1) * E].astype(BF16)


def owned_sums(counts, recv):
    vmem = pl.BlockSpec(memory_space=pltpu.VMEM)
    return pl.pallas_call(
        sums_kernel,
        out_shape=jax.ShapeDtypeStruct((N_ROWS, E), BF16),
        in_specs=[pl.BlockSpec(memory_space=pltpu.SMEM), vmem],
        out_specs=vmem,
        scratch_shapes=[pltpu.VMEM((LO, HI * E), F32)],
        compiler_params=pltpu.CompilerParams(vmem_limit_bytes=40 << 20),
        cost_estimate=pl.CostEstimate(flops=8 << 30, bytes_accessed=5 << 20, transcendentals=0),
        name="owned_sums",
    )(counts, recv)


def summed(own, others):
    total = own.astype(F32)
    for other in others:
        total = total + other.astype(F32)
    return total


def weight_grad_owned(embedded, scaled, z, y, x_lo):
    half = scaled.shape[1] // 2
    left, right = scaled[:, :half], scaled[:, half:]
    dims = (((0,), (0,)), ((), ()))

    def term_z(d):
        rows = lax.dynamic_slice_in_dim(embedded, ((z + d) % 4) * 1024, 1024, 1)
        return lax.dot_general(rows, left, dims, preferred_element_type=F32).astype(BF16)

    def term_y(d):
        start = ((y + d) % 4) * 256
        rows = jnp.concatenate(
            [lax.dynamic_slice_in_dim(embedded, k * 1024 + start, 256, 1) for k in range(4)], axis=1
        )
        return lax.dot_general(rows, right, dims, preferred_element_type=F32).astype(BF16)

    got_z = [lax.ppermute(term_z(d), "wide", z_perm(d)) for d in (2, 1, 3)]
    got_y = [lax.ppermute(term_y(d), "wide", y_perm(d)) for d in (2, 1, 3)]
    by_z = summed(term_z(0), got_z).astype(BF16)
    by_y = summed(term_y(0), got_y).astype(BF16)

    def piece(array, at):
        return lax.dynamic_slice_in_dim(array, (at % 4) * 256, 256, 0)

    got_zy = [lax.ppermute(piece(by_z, y + d), "wide", y_perm(d)) for d in (2, 1, 3)]
    got_yz = [lax.ppermute(piece(by_y, z + d), "wide", z_perm(d)) for d in (2, 1, 3)]
    pair = jnp.concatenate(
        [summed(piece(by_z, y), got_zy), summed(piece(by_y, z), got_yz)], axis=1
    ).astype(BF16)
    got = lax.ppermute(lax.dynamic_slice_in_dim(pair, (1 - x_lo) * E, E, 0), "wide", X_LO)
    return summed(lax.dynamic_slice_in_dim(pair, x_lo * E, E, 0), [got])


def over_narrow(part, core):
    rows = part.shape[0] // 2
    keep = lax.dynamic_slice_in_dim(part, core * rows, rows, 0)
    send = lax.dynamic_slice_in_dim(part, (1 - core) * rows, rows, 0)
    chip = summed(keep, [lax.ppermute(send, "narrow", CORE)]).astype(BF16)
    mine = summed(chip, [lax.ppermute(chip, "narrow", X_HI)])
    mate = lax.ppermute(mine, "narrow", CORE)
    low = jnp.where(core == 0, mine, mate)
    high = jnp.where(core == 0, mate, mine)
    return jnp.concatenate([low, high], axis=0)


def body(
    embedded,
    cotangent,
    cross_weight,
    cross_bias,
    bag_size,
    row_owner,
    row_id,
    emb_table,
    adagrad_state,
):
    panel = lax.axis_index("narrow")
    wide = lax.axis_index("wide")
    z, y, x_lo = wide // 8, (wide // 2) % 4, wide % 2
    core = panel % 2
    batch_rows, width = cotangent.shape
    feats = width // E
    norm_factor = 1.0 / math.sqrt(batch_rows * N_WIDE)

    x_panel = lax.dynamic_slice_in_dim(embedded, panel * width, width, 1)
    grad_out = cotangent.astype(F32)
    scaled = (grad_out * x_panel.astype(F32)).astype(BF16)

    def backward_part(k):
        rows = lax.dynamic_slice_in_dim(cross_weight, (panel ^ k) * width, width, 0)
        return lax.dot_general(scaled, rows, (((1,), (1,)), ((), ())), preferred_element_type=F32)

    from_mate_far = lax.ppermute(backward_part(3).astype(BF16), "narrow", CORE)
    chip_far = (backward_part(2) + from_mate_far.astype(F32)).astype(BF16)
    far = lax.ppermute(chip_far, "narrow", X_HI)
    from_mate = lax.ppermute(backward_part(1).astype(BF16), "narrow", CORE)
    cross_out = jnp.dot(embedded, cross_weight, preferred_element_type=F32) + cross_bias
    base = grad_out + grad_out * cross_out + backward_part(0) + from_mate.astype(F32)

    bag_len = lax.dynamic_slice_in_dim(bag_size, panel * feats, feats, 1)
    bag_depth = row_id.shape[2] // feats
    is_live = (jnp.arange(bag_depth, dtype=jnp.int32)[None, None, :] < bag_len[:, :, None]).reshape(-1)
    target = jnp.where(is_live, row_owner.reshape(-1), N_WIDE)
    is_target = target[:, None] == jnp.arange(N_WIDE, dtype=jnp.int32)[None, :]
    onehot = is_target.astype(BF16)
    position, counts = slot_positions(onehot)
    slots = jnp.where(is_live, target * CAP + position, N_WIDE * CAP)
    marked = row_id.reshape(-1) + 1
    halves = jnp.concatenate(
        [
            jnp.where(is_target, (marked // 64)[:, None], 0),
            jnp.where(is_target, (marked % 64)[:, None], 0),
        ],
        axis=1,
    ).astype(BF16)
    at_position = (position[:, None] == jnp.arange(CAP, dtype=jnp.int32)[None, :]).astype(BF16)
    ids = lax.dot_general(halves, at_position, (((0,), (0,)), ((), ())), preferred_element_type=F32)
    ids = ids.astype(BF16).reshape(2, N_WIDE, CAP // E, E).transpose(1, 0, 2, 3)
    ids = jnp.pad(ids.reshape(N_WIDE, 2 * CAP // E, E), ((0, 0), (0, ID_ROWS - 2 * CAP // E), (0, 0)))

    bias_part = jnp.sum(scaled, axis=0, dtype=F32)
    shared = lax.all_gather(jnp.concatenate([bias_part, counts]), "wide")
    bias_grad = jnp.sum(shared[:, :width], axis=0) * norm_factor
    recv_counts = lax.dynamic_slice_in_dim(shared, width + wide, 1, 1).reshape(-1).astype(jnp.int32)

    payload = scatter_entries(slots, base, far, ids)
    recv = lax.all_to_all(payload, "wide", split_axis=0, concat_axis=0, tiled=True)
    row_grad = over_narrow(owned_sums(recv_counts, recv), core)
    new_state = adagrad_state + jnp.mean(row_grad * row_grad, axis=1)
    new_table = emb_table - LEARN_RATE * row_grad / jnp.sqrt(new_state)[:, None]

    weight_grad = weight_grad_owned(embedded, scaled, z, y, x_lo) * norm_factor
    return (weight_grad, bias_grad, new_table, new_state)


def solution(mesh):
    in_specs = (
        P("wide", None),
        P("wide", "narrow"),
        P(None, "narrow"),
        P("narrow"),
        P("wide", None),
        P("narrow", "wide", None, None),
        P("narrow", "wide", None),
        P("wide", None),
        P("wide"),
    )
    out_specs = (P("wide", "narrow"), P("narrow"), P("wide", None), P("wide"))
    return jax.shard_map(body, mesh=mesh, in_specs=in_specs, out_specs=out_specs, check_vma=False)
```

```python
import math

import jax
import jax.numpy as jnp
from jax import lax
from jax.experimental import pallas as pl
from jax.experimental.pallas import tpu as pltpu
from jax.sharding import PartitionSpec as P

LEARN_RATE = 0.3
E = 128
N_WIDE = 32
CAP = 512
TAIL = 32
BLOCK = CAP + TAIL
N_ROWS = 2048
HI = 4
LO = N_ROWS // HI
F32 = jnp.float32
BF16 = jnp.bfloat16


def z_perm(d):
    return [(i, ((i // 8 + d) % 4) * 8 + i % 8) for i in range(N_WIDE)]


def y_perm(d):
    return [(i, (i // 8) * 8 + (((i // 2) % 4 + d) % 4) * 2 + i % 2) for i in range(N_WIDE)]


X_LO = [(i, i ^ 1) for i in range(N_WIDE)]
CORE = [(i, i ^ 1) for i in range(4)]
X_HI = [(i, i ^ 2) for i in range(4)]


def slot_positions(onehot):
    entries, n_wide = onehot.shape
    block_len = 512
    block_count = entries // block_len
    blocked = onehot.reshape(block_count, block_len, n_wide)
    lower = (jnp.arange(block_len)[:, None] > jnp.arange(block_len)[None, :]).astype(BF16)
    within = jnp.einsum("ij,bjn->bin", lower, blocked, preferred_element_type=F32)
    block_total = jnp.sum(blocked.astype(F32), axis=1)
    before = jnp.cumsum(block_total, axis=0) - block_total
    counted = (within + before[:, None, :]) * blocked.astype(F32)
    position = jnp.sum(counted, axis=2).reshape(entries).astype(jnp.int32)
    return position, jnp.sum(block_total, axis=0).astype(jnp.int32)


def scatter_kernel(slots_ref, base_ref, far_ref, tail_ref, out_ref, rows):
    dump = N_WIDE * CAP

    def clear(i, _):
        rows[pl.ds(pl.multiple_of(i * 64, 64), 64), :] = jnp.zeros((64, E), F32)
        return 0

    lax.fori_loop(0, dump // 64, clear, 0)

    def place(i, _):
        first = pl.multiple_of(i * 16, 16)
        for f in range(8):
            cols = slice(f * E, (f + 1) * E)
            tile = base_ref[pl.ds(first, 16), cols] + far_ref[pl.ds(first, 16), cols].astype(F32)
            for b in range(16):
                row = tile[b : b + 1, :]
                for j in range(2):
                    slot = slots_ref[(first + b) * 16 + 2 * f + j]
                    rows[pl.ds(slot, 1), :] = row
        return 0

    lax.fori_loop(0, base_ref.shape[0] // 16, place, 0)

    def narrow_down(w, _):
        out_ref[w, :CAP, :] = rows[pl.ds(pl.multiple_of(w * CAP, CAP), CAP), :].astype(BF16)
        out_ref[w, CAP:, :] = tail_ref[w]
        return 0

    lax.fori_loop(0, N_WIDE, narrow_down, 0)


def scatter_entries(slots, base, far, tail):
    vmem = pl.BlockSpec(memory_space=pltpu.VMEM)
    return pl.pallas_call(
        scatter_kernel,
        out_shape=jax.ShapeDtypeStruct((N_WIDE, BLOCK, E), BF16),
        in_specs=[pl.BlockSpec(memory_space=pltpu.SMEM), vmem, vmem, vmem],
        out_specs=vmem,
        scratch_shapes=[pltpu.VMEM((N_WIDE * CAP + 8, E), F32)],
        compiler_params=pltpu.CompilerParams(vmem_limit_bytes=40 << 20),
        cost_estimate=pl.CostEstimate(flops=0, bytes_accessed=40 << 20, transcendentals=0),
        name="place_entries",
    )(slots, base, far, tail)


def sums_kernel(count_ref, recv_ref, out_ref, bias_ref, total):
    total[...] = jnp.zeros_like(total)
    bias_ref[...] = jnp.zeros_like(bias_ref)
    lane_rows = lax.broadcasted_iota(jnp.int32, (LO, E), 0)

    def add_half(w, half):
        ids = recv_ref[w, CAP : CAP + 16, :].astype(F32)
        row = (ids[0:4, :] * 64.0 + ids[4:8, :]).astype(jnp.int32) - 1
        hi = row // LO
        lo = row - hi * LO
        hi = jnp.where(row < 0, -1, hi)
        hi_col = jnp.transpose(jnp.concatenate([hi, hi], axis=0).astype(F32), (1, 0))
        left, right = [], []
        for j in range(half * 2, half * 2 + 2):
            left.append(jnp.where(lane_rows == lo[j : j + 1, :], 1.0, 0.0).astype(BF16))
            v = recv_ref[w, j * E : (j + 1) * E, :]
            own = jnp.broadcast_to(hi_col[:, j : j + 1], (E, E)).astype(BF16)
            right.append(
                jnp.concatenate(
                    [jnp.where(own == BF16(h), v, BF16(0)) for h in range(HI)], axis=1
                )
            )
        total[...] += jnp.dot(
            jnp.concatenate(left, axis=1),
            jnp.concatenate(right, axis=0),
            preferred_element_type=F32,
        )

    def source(w, _):
        count = count_ref[w]
        sums = recv_ref[w, CAP:, :].astype(F32)
        bias_ref[...] += sums[8:16, :] + sums[16:24, :]
        for half in range(2):

            @pl.when(count > half * 2 * E)
            def _():
                add_half(w, half)

        return 0

    lax.fori_loop(0, N_WIDE, source, 0)
    for h in range(HI):
        out_ref[h * LO : (h + 1) * LO, :] = total[:, h * E : (h + 1) * E].astype(BF16)


def owned_sums(counts, recv):
    vmem = pl.BlockSpec(memory_space=pltpu.VMEM)
    return pl.pallas_call(
        sums_kernel,
        out_shape=(jax.ShapeDtypeStruct((N_ROWS, E), BF16), jax.ShapeDtypeStruct((8, E), F32)),
        in_specs=[pl.BlockSpec(memory_space=pltpu.SMEM), vmem],
        out_specs=(vmem, vmem),
        scratch_shapes=[pltpu.VMEM((LO, HI * E), F32)],
        compiler_params=pltpu.CompilerParams(vmem_limit_bytes=40 << 20),
        cost_estimate=pl.CostEstimate(flops=8 << 30, bytes_accessed=5 << 20, transcendentals=0),
        name="owned_sums",
    )(counts, recv)


def summed(own, others):
    total = own.astype(F32)
    for other in others:
        total = total + other.astype(F32)
    return total


def terms_kernel(block_ref, embedded_ref, scaled_ref, *out_refs):
    step = pl.program_id(0)
    term = lax.dot_general(
        embedded_ref[...], scaled_ref[...], (((0,), (0,)), ((), ())), preferred_element_type=F32
    ).astype(BF16)
    for q, out_ref in enumerate(out_refs):

        @pl.when(step // 4 == q)
        def _():
            out_ref[...] = term


def sent_terms(embedded, scaled, blocks):
    samples, half = scaled.shape[0], scaled.shape[1] // 2

    def out_map(q):
        return lambda s, blocks: (jnp.clip(s - 4 * q, 0, 3), 0)

    return pl.pallas_call(
        terms_kernel,
        out_shape=[jax.ShapeDtypeStruct((1024, half), BF16)] * 6,
        grid_spec=pltpu.PrefetchScalarGridSpec(
            num_scalar_prefetch=1,
            grid=(24,),
            in_specs=[
                pl.BlockSpec((samples, 256), lambda s, blocks: (0, blocks[s])),
                pl.BlockSpec((samples, half), lambda s, blocks: (0, s // 12)),
            ],
            out_specs=[pl.BlockSpec((256, half), out_map(q)) for q in range(6)],
        ),
        compiler_params=pltpu.CompilerParams(vmem_limit_bytes=32 << 20),
        cost_estimate=pl.CostEstimate(flops=3 << 30, bytes_accessed=14 << 20, transcendentals=0),
        name="sent_terms",
    )(blocks, embedded, scaled)


def weight_grad_owned(embedded, scaled, sent, z, y, x_lo):
    half = scaled.shape[1] // 2
    left, right = scaled[:, :half], scaled[:, half:]
    dims = (((0,), (0,)), ((), ()))

    def term_z():
        rows = lax.dynamic_slice_in_dim(embedded, z * 1024, 1024, 1)
        return lax.dot_general(rows, left, dims, preferred_element_type=F32)

    def term_y():
        rows = jnp.concatenate(
            [lax.dynamic_slice_in_dim(embedded, k * 1024 + y * 256, 256, 1) for k in range(4)], axis=1
        )
        return lax.dot_general(rows, right, dims, preferred_element_type=F32)

    got_z = [lax.ppermute(sent[q], "wide", z_perm(d)) for q, d in enumerate((2, 1, 3))]
    got_y = [lax.ppermute(sent[3 + q], "wide", y_perm(d)) for q, d in enumerate((2, 1, 3))]
    by_z = summed(term_z(), got_z).astype(BF16)
    by_y = summed(term_y(), got_y).astype(BF16)

    def piece(array, at):
        return lax.dynamic_slice_in_dim(array, (at % 4) * 256, 256, 0)

    got_zy = [lax.ppermute(piece(by_z, y + d), "wide", y_perm(d)) for d in (2, 1, 3)]
    got_yz = [lax.ppermute(piece(by_y, z + d), "wide", z_perm(d)) for d in (2, 1, 3)]
    pair = jnp.concatenate(
        [summed(piece(by_z, y), got_zy), summed(piece(by_y, z), got_yz)], axis=1
    ).astype(BF16)
    got = lax.ppermute(lax.dynamic_slice_in_dim(pair, (1 - x_lo) * E, E, 0), "wide", X_LO)
    return summed(lax.dynamic_slice_in_dim(pair, x_lo * E, E, 0), [got])


def over_narrow(part, core):
    rows = part.shape[0] // 2
    keep = lax.dynamic_slice_in_dim(part, core * rows, rows, 0)
    send = lax.dynamic_slice_in_dim(part, (1 - core) * rows, rows, 0)
    chip = summed(keep, [lax.ppermute(send, "narrow", CORE)]).astype(BF16)
    mine = summed(chip, [lax.ppermute(chip, "narrow", X_HI)])
    mate = lax.ppermute(mine, "narrow", CORE)
    low = jnp.where(core == 0, mine, mate)
    high = jnp.where(core == 0, mate, mine)
    return jnp.concatenate([low, high], axis=0)


def body(
    embedded,
    cotangent,
    cross_weight,
    cross_bias,
    bag_size,
    row_owner,
    row_id,
    emb_table,
    adagrad_state,
):
    panel = lax.axis_index("narrow")
    wide = lax.axis_index("wide")
    z, y, x_lo = wide // 8, (wide // 2) % 4, wide % 2
    core = panel % 2
    batch_rows, width = cotangent.shape
    feats = width // E
    norm_factor = 1.0 / math.sqrt(batch_rows * N_WIDE)

    x_panel = lax.dynamic_slice_in_dim(embedded, panel * width, width, 1)
    grad_out = cotangent.astype(F32)
    scaled = (grad_out * x_panel.astype(F32)).astype(BF16)

    def backward_part(k):
        rows = lax.dynamic_slice_in_dim(cross_weight, (panel ^ k) * width, width, 0)
        return lax.dot_general(scaled, rows, (((1,), (1,)), ((), ())), preferred_element_type=F32)

    from_mate_far = lax.ppermute(backward_part(3).astype(BF16), "narrow", CORE)
    chip_far = (backward_part(2) + from_mate_far.astype(F32)).astype(BF16)
    chip_far, scaled, embedded = lax.optimization_barrier((chip_far, scaled, embedded))
    far = lax.ppermute(chip_far, "narrow", X_HI)
    column_blocks = jnp.stack(
        [((z + d) % 4) * 4 + k for d in (2, 1, 3) for k in range(4)]
        + [k * 4 + (y + d) % 4 for d in (2, 1, 3) for k in range(4)]
    )
    sent = sent_terms(embedded, scaled, column_blocks)
    embedded, *sent = lax.optimization_barrier((embedded, *sent))
    from_mate = lax.ppermute(backward_part(1).astype(BF16), "narrow", CORE)
    cross_out = jnp.dot(embedded, cross_weight, preferred_element_type=F32) + cross_bias
    base = grad_out + grad_out * cross_out + backward_part(0) + from_mate.astype(F32)

    bag_len = lax.dynamic_slice_in_dim(bag_size, panel * feats, feats, 1)
    bag_depth = row_id.shape[2] // feats
    is_live = (jnp.arange(bag_depth, dtype=jnp.int32)[None, None, :] < bag_len[:, :, None]).reshape(-1)
    target = jnp.where(is_live, row_owner.reshape(-1), N_WIDE)
    is_target = target[:, None] == jnp.arange(N_WIDE, dtype=jnp.int32)[None, :]
    onehot = is_target.astype(BF16)
    position, counts = slot_positions(onehot)
    slots = jnp.where(is_live, target * CAP + position, N_WIDE * CAP)
    marked = row_id.reshape(-1) + 1
    halves = jnp.concatenate(
        [
            jnp.where(is_target, (marked // 64)[:, None], 0),
            jnp.where(is_target, (marked % 64)[:, None], 0),
        ],
        axis=1,
    ).astype(BF16)
    at_position = (position[:, None] == jnp.arange(CAP, dtype=jnp.int32)[None, :]).astype(BF16)
    ids = lax.dot_general(halves, at_position, (((0,), (0,)), ((), ())), preferred_element_type=F32)
    ids = ids.astype(BF16).reshape(2, N_WIDE, CAP // E, E).transpose(1, 0, 2, 3)

    bias_part = jnp.sum(scaled, axis=0, dtype=F32)
    bias_top = lax.reduce_precision(bias_part, 8, 7)
    bias_parts = jnp.stack([bias_top, bias_part - bias_top]).astype(BF16).reshape(1, 16, E)
    count_parts = jnp.stack([counts // 64, counts % 64], axis=1).astype(BF16)
    tail = jnp.concatenate(
        [
            ids.reshape(N_WIDE, 8, E),
            jnp.broadcast_to(bias_parts, (N_WIDE, 16, E)),
            jnp.broadcast_to(jnp.repeat(count_parts, 4, axis=1)[:, :, None], (N_WIDE, 8, E)),
        ],
        axis=1,
    )

    payload = scatter_entries(slots, base, far, tail)
    recv = lax.all_to_all(payload, "wide", split_axis=0, concat_axis=0, tiled=True)
    recv_counts = (recv[:, CAP + 24, 0].astype(F32) * 64.0 + recv[:, CAP + 28, 0].astype(F32)).astype(jnp.int32)
    sums, bias_sums = owned_sums(recv_counts, recv)
    bias_grad = bias_sums.reshape(-1) * norm_factor
    row_grad = over_narrow(sums, core)
    new_state = adagrad_state + jnp.mean(row_grad * row_grad, axis=1)
    new_table = emb_table - LEARN_RATE * row_grad / jnp.sqrt(new_state)[:, None]

    weight_grad = weight_grad_owned(embedded, scaled, sent, z, y, x_lo) * norm_factor
    return (weight_grad, bias_grad, new_table, new_state)


def solution(mesh):
    in_specs = (
        P("wide", None),
        P("wide", "narrow"),
        P(None, "narrow"),
        P("narrow"),
        P("wide", None),
        P("narrow", "wide", None, None),
        P("narrow", "wide", None),
        P("wide", None),
        P("wide"),
    )
    out_specs = (P("wide", "narrow"), P("narrow"), P("wide", None), P("wide"))
    return jax.shard_map(body, mesh=mesh, in_specs=in_specs, out_specs=out_specs, check_vma=False)
```

```python
import math

import jax
import jax.numpy as jnp
from jax import lax
from jax.experimental import pallas as pl
from jax.experimental.pallas import tpu as pltpu
from jax.sharding import PartitionSpec as P

LEARN_RATE = 0.3
E = 128
N_WIDE = 32
CAP = 512
TAIL = 32
BLOCK = CAP + TAIL
N_ROWS = 2048
HI = 4
LO = N_ROWS // HI
F32 = jnp.float32
BF16 = jnp.bfloat16
LIGHT = pl.CostEstimate(flops=1, bytes_accessed=1, transcendentals=0)
APART = (2, 1, 3)


def z_perm(d):
    return [(i, ((i // 8 + d) % 4) * 8 + i % 8) for i in range(N_WIDE)]


def y_perm(d):
    return [(i, (i // 8) * 8 + (((i // 2) % 4 + d) % 4) * 2 + i % 2) for i in range(N_WIDE)]


X_LO = [(i, i ^ 1) for i in range(N_WIDE)]
CORE = [(i, i ^ 1) for i in range(4)]
X_HI = [(i, i ^ 2) for i in range(4)]


def slot_positions(onehot):
    entries, n_wide = onehot.shape
    block_len = 512
    block_count = entries // block_len
    blocked = onehot.reshape(block_count, block_len, n_wide)
    lower = (jnp.arange(block_len)[:, None] > jnp.arange(block_len)[None, :]).astype(BF16)
    within = jnp.einsum("ij,bjn->bin", lower, blocked, preferred_element_type=F32)
    block_total = jnp.sum(blocked.astype(F32), axis=1)
    before = jnp.cumsum(block_total, axis=0) - block_total
    counted = (within + before[:, None, :]) * blocked.astype(F32)
    position = jnp.sum(counted, axis=2).reshape(entries).astype(jnp.int32)
    return position, jnp.sum(block_total, axis=0).astype(jnp.int32)


def scatter_kernel(slots_ref, base_ref, far_ref, tail_ref, out_ref, rows, blocks, sems):
    dump = N_WIDE * CAP

    def clear(i, _):
        rows[pl.ds(pl.multiple_of(i * 64, 64), 64), :] = jnp.zeros((64, E), F32)
        return 0

    lax.fori_loop(0, dump // 64, clear, 0)

    def place(i, _):
        first = pl.multiple_of(i * 16, 16)
        for f in range(8):
            cols = slice(f * E, (f + 1) * E)
            tile = base_ref[pl.ds(first, 16), cols] + far_ref[pl.ds(first, 16), cols].astype(F32)
            for b in range(16):
                row = tile[b : b + 1, :]
                for j in range(2):
                    slot = slots_ref[(first + b) * 16 + 2 * f + j]
                    rows[pl.ds(slot, 1), :] = row
        return 0

    lax.fori_loop(0, base_ref.shape[0] // 16, place, 0)

    def copy_out(w):
        return pltpu.make_async_copy(blocks.at[w], out_ref.at[w], sems.at[w])

    def narrow_down(w, _):
        blocks[w, :CAP, :] = rows[pl.ds(pl.multiple_of(w * CAP, CAP), CAP), :].astype(BF16)
        blocks[w, CAP:, :] = tail_ref[w]
        copy_out(w).start()
        return 0

    lax.fori_loop(0, N_WIDE, narrow_down, 0)

    def finish(w, _):
        copy_out(w).wait()
        return 0

    lax.fori_loop(0, N_WIDE, finish, 0)


def scatter_entries(slots, base, far, tail):
    vmem = pl.BlockSpec(memory_space=pltpu.VMEM)
    return pl.pallas_call(
        scatter_kernel,
        out_shape=jax.ShapeDtypeStruct((N_WIDE, BLOCK, E), BF16),
        in_specs=[pl.BlockSpec(memory_space=pltpu.SMEM), vmem, vmem, vmem],
        out_specs=pl.BlockSpec(memory_space=pl.ANY),
        scratch_shapes=[
            pltpu.VMEM((N_WIDE * CAP + 8, E), F32),
            pltpu.VMEM((N_WIDE, BLOCK, E), BF16),
            pltpu.SemaphoreType.DMA((N_WIDE,)),
        ],
        compiler_params=pltpu.CompilerParams(vmem_limit_bytes=40 << 20),
        cost_estimate=LIGHT,
        name="place_entries",
    )(slots, base, far, tail)


def sums_kernel(count_ref, recv_ref, out_ref, bias_ref, total, left, right, todo):
    lane_rows = lax.broadcasted_iota(jnp.int32, (LO, E), 0)

    def listing(w, n):
        todo[n] = 2 * w
        n = n + jnp.where(count_ref[w] > 0, 1, 0)
        todo[n] = 2 * w + 1
        return n + jnp.where(count_ref[w] > CAP // 2, 1, 0)

    n = lax.fori_loop(0, N_WIDE, listing, 0)
    for k in range(6):
        todo[n + k] = -1
    total[...] = jnp.zeros_like(total)
    bias_ref[...] = jnp.sum(
        recv_ref[:, CAP + 8 : CAP + 16, :].astype(F32) + recv_ref[:, CAP + 16 : CAP + 24, :].astype(F32),
        axis=0,
    )

    def build(i, buf):
        for p in range(2):
            item = todo[i * 2 + p]
            w = jnp.maximum(item, 0) // 2
            half = jnp.maximum(item, 0) % 2
            ids = recv_ref[w, CAP : CAP + 16, :].astype(F32)
            row = (ids[0:4, :] * 64.0 + ids[4:8, :]).astype(jnp.int32) - 1
            row = jnp.where(half == 0, row[0:2, :], row[2:4, :])
            row = jnp.where(item < 0, -1, row)
            hi = row >> (LO.bit_length() - 1)
            lo = jnp.where(row < 0, -1, row & (LO - 1))
            hi_col = jnp.transpose(jnp.concatenate([hi] * 4, axis=0).astype(F32), (1, 0))
            for j in range(2):
                at = (2 * p + j) * E
                left[buf, :, at : at + E] = jnp.where(lane_rows == lo[j : j + 1, :], 1.0, 0.0).astype(BF16)
                v = recv_ref[w, pl.ds(pl.multiple_of(half * (CAP // 2), CAP // 2) + j * E, E), :]
                own = jnp.broadcast_to(hi_col[:, j : j + 1], (E, E)).astype(BF16)
                for h in range(HI):
                    right[buf, at : at + E, h * E : (h + 1) * E] = jnp.where(own == BF16(h), v, BF16(0))

    build(0, 0)

    def step(i, _):
        for b in range(2):
            build(2 * i + b + 1, 1 - b)
            total[...] += jnp.dot(left[b], right[b], preferred_element_type=F32)
        return 0

    lax.fori_loop(0, (n + 3) // 4, step, 0)
    for h in range(HI):
        out_ref[h * LO : (h + 1) * LO, :] = total[:, h * E : (h + 1) * E].astype(BF16)


def owned_sums(counts, recv):
    vmem = pl.BlockSpec(memory_space=pltpu.VMEM)
    return pl.pallas_call(
        sums_kernel,
        out_shape=(jax.ShapeDtypeStruct((N_ROWS, E), BF16), jax.ShapeDtypeStruct((8, E), F32)),
        in_specs=[pl.BlockSpec(memory_space=pltpu.SMEM), vmem],
        out_specs=(vmem, vmem),
        scratch_shapes=[
            pltpu.VMEM((LO, HI * E), F32),
            pltpu.VMEM((2, LO, CAP), BF16),
            pltpu.VMEM((2, CAP, HI * E), BF16),
            pltpu.SMEM((2 * N_WIDE + 16,), jnp.int32),
        ],
        compiler_params=pltpu.CompilerParams(vmem_limit_bytes=40 << 20),
        cost_estimate=LIGHT,
        name="owned_sums",
    )(counts, recv)


def summed(own, others):
    total = own.astype(F32)
    for other in others:
        total = total + other.astype(F32)
    return total


def far_kernel(block_ref, scaled_ref, embedded_ref, *refs):
    sent, turned, columns, terms, sems_in, sems_out = refs[:4], refs[4], *refs[5:]

    def copy_in(c):
        at = pl.multiple_of(block_ref[c] * 256, 256)
        return pltpu.make_async_copy(embedded_ref.at[:, pl.ds(at, 256)], columns.at[c], sems_in.at[c])

    def copy_out(q):
        return pltpu.make_async_copy(terms.at[q], sent[q], sems_out.at[q])

    for c in range(8):
        copy_in(c).start()
    turned[...] = jnp.transpose(scaled_ref[...], (1, 0))
    for route in range(2):
        part = turned[route * 512 : (route + 1) * 512, :]
        for k in range(4):
            copy_in(4 * route + k).wait()
            term = jnp.dot(part, columns[4 * route + k], preferred_element_type=F32).astype(BF16)
            for way in range(2):
                terms[2 * route + way, :, k * 256 : (k + 1) * 256] = term[way * 256 : (way + 1) * 256, :]
        for way in range(2):
            copy_out(2 * route + way).start()
    for q in range(4):
        copy_out(q).wait()


def far_terms(embedded, scaled, blocks):
    hbm = pl.BlockSpec(memory_space=pl.ANY)
    vmem = pl.BlockSpec(memory_space=pltpu.VMEM)
    return pl.pallas_call(
        far_kernel,
        out_shape=[jax.ShapeDtypeStruct((256, 1024), BF16)] * 4 + [jax.ShapeDtypeStruct((1024, 512), BF16)],
        in_specs=[pl.BlockSpec(memory_space=pltpu.SMEM), vmem, hbm],
        out_specs=[hbm] * 4 + [vmem],
        scratch_shapes=[
            pltpu.VMEM((8, 512, 256), BF16),
            pltpu.VMEM((4, 256, 1024), BF16),
            pltpu.SemaphoreType.DMA((8,)),
            pltpu.SemaphoreType.DMA((4,)),
        ],
        compiler_params=pltpu.CompilerParams(vmem_limit_bytes=40 << 20),
        cost_estimate=LIGHT,
        name="far_terms",
    )(blocks, scaled, embedded)


def near_kernel(block_ref, turned_ref, embedded_ref, *refs):
    passed, sent, columns, terms, sems_in, sems_out = refs[:4], refs[4:8], *refs[8:]

    def copy_in(c):
        at = pl.multiple_of(block_ref[c] * 256, 256)
        return pltpu.make_async_copy(embedded_ref.at[:, pl.ds(at, 256)], columns.at[c], sems_in.at[c])

    def copy_out(q):
        return pltpu.make_async_copy(terms.at[q], sent[q], sems_out.at[q])

    for c in range(16):
        copy_in(c).start()
    for q in range(4):
        route, way = q // 2, q % 2
        part = turned_ref[route * 512 : (route + 1) * 512, :]
        mine, other = slice(way * 256, (way + 1) * 256), slice((1 - way) * 256, (2 - way) * 256)
        for k in range(4):
            copy_in(4 * q + k).wait()
            at = slice(k * 256, (k + 1) * 256)
            term = jnp.dot(part, columns[4 * q + k], preferred_element_type=F32)
            terms[q, mine, at] = (term[mine, :] + passed[q][:, at].astype(F32)).astype(BF16)
            terms[q, other, at] = term[other, :].astype(BF16)
        copy_out(q).start()
    for q in range(4):
        copy_out(q).wait()


def near_terms(embedded, turned, passed, blocks):
    hbm = pl.BlockSpec(memory_space=pl.ANY)
    vmem = pl.BlockSpec(memory_space=pltpu.VMEM)
    return pl.pallas_call(
        near_kernel,
        out_shape=[jax.ShapeDtypeStruct((512, 1024), BF16)] * 4,
        in_specs=[pl.BlockSpec(memory_space=pltpu.SMEM), vmem, hbm] + [vmem] * 4,
        out_specs=[hbm] * 4,
        scratch_shapes=[
            pltpu.VMEM((16, 512, 256), BF16),
            pltpu.VMEM((4, 512, 1024), BF16),
            pltpu.SemaphoreType.DMA((16,)),
            pltpu.SemaphoreType.DMA((4,)),
        ],
        compiler_params=pltpu.CompilerParams(vmem_limit_bytes=40 << 20),
        cost_estimate=LIGHT,
        name="near_terms",
    )(blocks, turned, embedded, *passed)


def own_kernel(block_ref, turned_ref, embedded_ref, *refs):
    got, pieces, columns, sems = refs[:4], refs[4:12], *refs[12:]

    def copy_in(q):
        at = pl.multiple_of(block_ref[q] * 256, 256)
        return pltpu.make_async_copy(embedded_ref.at[:, pl.ds(at, 256)], columns.at[q], sems.at[q])

    for q in range(8):
        copy_in(q).start()
    for q in range(8):
        copy_in(q).wait()
        route = q // 4
        total = jnp.dot(
            turned_ref[route * 512 : (route + 1) * 512, :], columns[q], preferred_element_type=F32
        )
        at = pl.multiple_of(block_ref[8 + q] * 256, 256)
        for other in got[2 * route : 2 * route + 2]:
            total += other[:, pl.ds(at, 256)].astype(F32)
        pieces[q][...] = total.astype(BF16)


def own_terms(embedded, turned, got, blocks):
    hbm = pl.BlockSpec(memory_space=pl.ANY)
    vmem = pl.BlockSpec(memory_space=pltpu.VMEM)
    return pl.pallas_call(
        own_kernel,
        out_shape=[jax.ShapeDtypeStruct((512, 256), BF16)] * 8,
        in_specs=[pl.BlockSpec(memory_space=pltpu.SMEM), vmem, hbm] + [vmem] * 4,
        out_specs=[vmem] * 8,
        scratch_shapes=[pltpu.VMEM((8, 512, 256), BF16), pltpu.SemaphoreType.DMA((8,))],
        compiler_params=pltpu.CompilerParams(vmem_limit_bytes=40 << 20),
        cost_estimate=LIGHT,
        name="own_terms",
    )(blocks, turned, embedded, *got)


def weight_grad_owned(pieces, x_lo):
    got_zy = [lax.ppermute(pieces[q], "wide", y_perm(d)) for q, d in enumerate(APART)]
    got_yz = [lax.ppermute(pieces[4 + q], "wide", z_perm(d)) for q, d in enumerate(APART)]
    pair = jnp.concatenate([summed(pieces[3], got_zy), summed(pieces[7], got_yz)], axis=0).astype(BF16)
    got = lax.ppermute(lax.dynamic_slice_in_dim(pair, (1 - x_lo) * E, E, 1), "wide", X_LO)
    return summed(lax.dynamic_slice_in_dim(pair, x_lo * E, E, 1), [got]).T


def base_kernel(
    panel_ref, embedded_ref, weight_ref, bias_ref, cot_ref, scaled_ref, rows_ref, mate_ref, out_ref
):
    cross = jnp.dot(embedded_ref[...], weight_ref[...], preferred_element_type=F32) + bias_ref[...]
    backward = lax.dot_general(
        scaled_ref[...], rows_ref[...], (((1,), (1,)), ((), ())), preferred_element_type=F32
    )
    grad = cot_ref[...].astype(F32)
    out_ref[...] = grad + grad * cross + backward + mate_ref[...].astype(F32)


def base_terms(panel, embedded, weight, bias, cotangent, scaled, from_mate):
    samples, width = cotangent.shape
    tile = 256
    steps = width // tile
    return pl.pallas_call(
        base_kernel,
        out_shape=jax.ShapeDtypeStruct((samples, width), F32),
        grid_spec=pltpu.PrefetchScalarGridSpec(
            num_scalar_prefetch=1,
            grid=(steps,),
            in_specs=[
                pl.BlockSpec(embedded.shape, lambda i, p: (0, 0)),
                pl.BlockSpec((weight.shape[0], tile), lambda i, p: (0, i)),
                pl.BlockSpec((1, tile), lambda i, p: (0, i)),
                pl.BlockSpec((samples, tile), lambda i, p: (0, i)),
                pl.BlockSpec((samples, width), lambda i, p: (0, 0)),
                pl.BlockSpec((tile, width), lambda i, p: (p[0] * steps + i, 0)),
                pl.BlockSpec((samples, tile), lambda i, p: (0, i)),
            ],
            out_specs=pl.BlockSpec((samples, tile), lambda i, p: (0, i)),
        ),
        compiler_params=pltpu.CompilerParams(vmem_limit_bytes=40 << 20),
        cost_estimate=LIGHT,
        name="base_terms",
    )(panel.reshape(1), embedded, weight, bias.reshape(1, -1), cotangent, scaled, weight, from_mate)


def over_narrow(part, core):
    rows = part.shape[0] // 2
    keep = lax.dynamic_slice_in_dim(part, core * rows, rows, 0)
    send = lax.dynamic_slice_in_dim(part, (1 - core) * rows, rows, 0)
    chip = summed(keep, [lax.ppermute(send, "narrow", CORE)]).astype(BF16)
    mine = summed(chip, [lax.ppermute(chip, "narrow", X_HI)])
    mate = lax.ppermute(mine, "narrow", CORE)
    low = jnp.where(core == 0, mine, mate)
    high = jnp.where(core == 0, mate, mine)
    return jnp.concatenate([low, high], axis=0)


def body(
    embedded,
    cotangent,
    cross_weight,
    cross_bias,
    bag_size,
    row_owner,
    row_id,
    emb_table,
    adagrad_state,
):
    panel = lax.axis_index("narrow")
    wide = lax.axis_index("wide")
    z, y, x_lo = wide // 8, (wide // 2) % 4, wide % 2
    core = panel % 2
    batch_rows, width = cotangent.shape
    feats = width // E
    norm_factor = 1.0 / math.sqrt(batch_rows * N_WIDE)

    x_panel = lax.dynamic_slice_in_dim(embedded, panel * width, width, 1)
    grad_out = cotangent.astype(F32)
    scaled = (grad_out * x_panel.astype(F32)).astype(BF16)

    def backward_part(k):
        rows = lax.dynamic_slice_in_dim(cross_weight, (panel ^ k) * width, width, 0)
        return lax.dot_general(scaled, rows, (((1,), (1,)), ((), ())), preferred_element_type=F32)

    from_mate_far = lax.ppermute(backward_part(3).astype(BF16), "narrow", CORE)
    from_mate = lax.ppermute(backward_part(1).astype(BF16), "narrow", CORE)
    chip_far = (backward_part(2) + from_mate_far.astype(F32)).astype(BF16)
    chip_far, embedded, from_mate = lax.optimization_barrier((chip_far, embedded, from_mate))
    far = lax.ppermute(chip_far, "narrow", X_HI)

    far_blocks = jnp.stack([((z + 2) % 4) * 4 + k for k in range(4)] + [k * 4 + (y + 2) % 4 for k in range(4)])
    near_blocks = jnp.stack(
        [((z + d) % 4) * 4 + k for d in (1, 3) for k in range(4)]
        + [k * 4 + (y + d) % 4 for d in (1, 3) for k in range(4)]
    )
    ways = [z_perm(1), z_perm(3), y_perm(1), y_perm(3)]
    *sent, turned = far_terms(embedded, scaled, far_blocks)
    passed = [lax.ppermute(sent[q], "wide", ways[q]) for q in range(4)]
    embedded, turned = lax.optimization_barrier((embedded, turned))
    base = base_terms(panel, embedded, cross_weight, cross_bias, cotangent, scaled, from_mate)
    embedded, base, far = lax.optimization_barrier((embedded, base, far))
    sent = near_terms(embedded, turned, passed, near_blocks)
    got = [lax.ppermute(sent[q], "wide", ways[q]) for q in range(4)]
    row_owner, row_id, *_ = lax.optimization_barrier((row_owner, row_id, sent[0]))

    bag_len = lax.dynamic_slice_in_dim(bag_size, panel * feats, feats, 1)
    bag_depth = row_id.shape[2] // feats
    is_live = (jnp.arange(bag_depth, dtype=jnp.int32)[None, None, :] < bag_len[:, :, None]).reshape(-1)
    target = jnp.where(is_live, row_owner.reshape(-1), N_WIDE)
    is_target = target[:, None] == jnp.arange(N_WIDE, dtype=jnp.int32)[None, :]
    onehot = is_target.astype(BF16)
    position, counts = slot_positions(onehot)
    slots = jnp.where(is_live, target * CAP + position, N_WIDE * CAP)
    marked = row_id.reshape(-1) + 1
    halves = jnp.concatenate(
        [
            jnp.where(is_target, (marked // 64)[:, None], 0),
            jnp.where(is_target, (marked % 64)[:, None], 0),
        ],
        axis=1,
    ).astype(BF16)
    at_position = (position[:, None] == jnp.arange(CAP, dtype=jnp.int32)[None, :]).astype(BF16)
    ids = lax.dot_general(halves, at_position, (((0,), (0,)), ((), ())), preferred_element_type=F32)
    ids = ids.astype(BF16).reshape(2, N_WIDE, CAP // E, E).transpose(1, 0, 2, 3)

    bias_part = jnp.sum(scaled, axis=0, dtype=F32)
    bias_top = lax.reduce_precision(bias_part, 8, 7)
    bias_parts = jnp.stack([bias_top, bias_part - bias_top]).astype(BF16).reshape(1, 16, E)
    count_parts = jnp.stack([counts // 64, counts % 64], axis=1).astype(BF16)
    tail = jnp.concatenate(
        [
            ids.reshape(N_WIDE, 8, E),
            jnp.broadcast_to(bias_parts, (N_WIDE, 16, E)),
            jnp.broadcast_to(jnp.repeat(count_parts, 4, axis=1)[:, :, None], (N_WIDE, 8, E)),
        ],
        axis=1,
    )

    payload = scatter_entries(slots, base, far, tail)
    payload, *got = lax.optimization_barrier((payload, *got))
    recv = lax.all_to_all(payload, "wide", split_axis=0, concat_axis=0, tiled=True)
    recv_counts = (recv[:, CAP + 24, 0].astype(F32) * 64.0 + recv[:, CAP + 28, 0].astype(F32)).astype(jnp.int32)
    sums, bias_sums = owned_sums(recv_counts, recv)
    bias_grad = bias_sums.reshape(-1) * norm_factor
    row_grad = over_narrow(sums, core)
    new_state = adagrad_state + jnp.mean(row_grad * row_grad, axis=1)
    new_table = emb_table - LEARN_RATE * row_grad / jnp.sqrt(new_state)[:, None]

    later = APART + (0,)
    own_blocks = jnp.stack(
        [z * 4 + (y + d) % 4 for d in later]
        + [((z + d) % 4) * 4 + y for d in later]
        + [(y + d) % 4 for d in later]
        + [(z + d) % 4 for d in later]
    )
    weight_grad = weight_grad_owned(own_terms(embedded, turned, got, own_blocks), x_lo) * norm_factor
    return (weight_grad, bias_grad, new_table, new_state)


def solution(mesh):
    in_specs = (
        P("wide", None),
        P("wide", "narrow"),
        P(None, "narrow"),
        P("narrow"),
        P("wide", None),
        P("narrow", "wide", None, None),
        P("narrow", "wide", None),
        P("wide", None),
        P("wide"),
    )
    out_specs = (P("wide", "narrow"), P("narrow"), P("wide", None), P("wide"))
    return jax.shard_map(body, mesh=mesh, in_specs=in_specs, out_specs=out_specs, check_vma=False)
```

```python
import math

import jax
import jax.numpy as jnp
from jax import lax
from jax.experimental import pallas as pl
from jax.experimental.pallas import tpu as pltpu
from jax.sharding import PartitionSpec as P

LEARN_RATE = 0.3
E = 128
N_WIDE = 32
CAP = 512
TAIL = 32
BLOCK = CAP + TAIL
N_ROWS = 2048
HI = 4
LO = N_ROWS // HI
F32 = jnp.float32
BF16 = jnp.bfloat16
LIGHT = pl.CostEstimate(flops=1, bytes_accessed=1, transcendentals=0)
VMEM_BYTES = 56 << 20
APART = (2, 1, 3)


def z_perm(d):
    return [(i, ((i // 8 + d) % 4) * 8 + i % 8) for i in range(N_WIDE)]


def y_perm(d):
    return [(i, (i // 8) * 8 + (((i // 2) % 4 + d) % 4) * 2 + i % 2) for i in range(N_WIDE)]


X_LO = [(i, i ^ 1) for i in range(N_WIDE)]
CORE = [(i, i ^ 1) for i in range(4)]
X_HI = [(i, i ^ 2) for i in range(4)]


def slots_kernel(panel_ref, owner_ref, row_ref, bag_ref, slots_ref, ids_ref, count_ref, onehots):
    depth, samples = owner_ref.shape
    feats = depth // 2
    bag = bag_ref[pl.ds(pl.multiple_of(panel_ref[0] * feats, feats), feats), :]
    bag = jnp.concatenate([bag[k // 2 : k // 2 + 1, :] for k in range(depth)], axis=0)
    live = (lax.broadcasted_iota(jnp.int32, (depth, samples), 0) & 1) < bag
    owner = jnp.where(live, owner_ref[...], N_WIDE)
    for t in range(N_WIDE):
        onehots[t * depth : (t + 1) * depth, :] = jnp.where(owner == t, 1.0, 0.0).astype(BF16)

    size = N_WIDE * depth
    first = lax.broadcasted_iota(jnp.int32, (samples, samples), 0)
    second = lax.broadcasted_iota(jnp.int32, (samples, samples), 1)
    before = jnp.where(first < second, 1.0, 0.0).astype(BF16)
    within = jnp.dot(onehots[...], before, preferred_element_type=F32)
    in_row = jnp.dot(onehots[...], jnp.ones((samples, E), BF16), preferred_element_type=F32)
    top = jnp.floor(in_row * (1.0 / 16.0))
    low = (in_row - 16.0 * top).astype(BF16)
    top = top.astype(BF16)
    r = lax.broadcasted_iota(jnp.int32, (size, size), 0)
    c = lax.broadcasted_iota(jnp.int32, (size, size), 1)
    shift = depth.bit_length() - 1
    earlier = jnp.where((r >> shift == c >> shift) & (c < r), 1.0, 0.0).astype(BF16)
    rows_before = 16.0 * jnp.dot(earlier, top, preferred_element_type=F32) + jnp.dot(
        earlier, low, preferred_element_type=F32
    )
    t_rows = lax.broadcasted_iota(jnp.int32, (N_WIDE, size), 0)
    t_cols = lax.broadcasted_iota(jnp.int32, (N_WIDE, size), 1)
    members = jnp.where(t_rows == t_cols >> shift, 1.0, 0.0).astype(BF16)
    count_ref[...] = 16.0 * jnp.dot(members, top, preferred_element_type=F32) + jnp.dot(
        members, low, preferred_element_type=F32
    )
    place = jnp.zeros((depth, samples), F32)
    for t in range(N_WIDE):
        at = slice(t * depth, (t + 1) * depth)
        ahead = jnp.concatenate([rows_before[at, :]] * (samples // E), axis=1)
        place = place + jnp.where(owner == t, within[at, :] + ahead, 0.0)
    place = place.astype(jnp.int32)
    slots_ref[...] = jnp.where(live, owner * CAP + place, N_WIDE * CAP)

    marked = row_ref[...] + 1
    top = (marked >> 6).astype(F32)
    low = (marked & 63).astype(F32)
    owners = lax.broadcasted_iota(jnp.int32, (N_WIDE, samples), 0)
    places = lax.broadcasted_iota(jnp.int32, (CAP, samples), 0)
    ids = jnp.zeros((2 * N_WIDE, CAP), F32)
    for k in range(depth):
        at = slice(k, k + 1)
        mine = owners == owner[at, :]
        marks = jnp.concatenate([jnp.where(mine, top[at, :], 0.0), jnp.where(mine, low[at, :], 0.0)], axis=0)
        there = jnp.where(places == place[at, :], 1.0, 0.0).astype(BF16)
        ids = ids + lax.dot_general(
            marks.astype(BF16), there, (((1,), (1,)), ((), ())), preferred_element_type=F32
        )
    ids_ref[...] = ids.astype(BF16)


def entry_slots(panel, owner, row, bag):
    vmem = pl.BlockSpec(memory_space=pltpu.VMEM)
    depth, samples = owner.shape
    return pl.pallas_call(
        slots_kernel,
        out_shape=(
            jax.ShapeDtypeStruct((depth, samples), jnp.int32),
            jax.ShapeDtypeStruct((2 * N_WIDE, CAP), BF16),
            jax.ShapeDtypeStruct((N_WIDE, E), F32),
        ),
        in_specs=[pl.BlockSpec(memory_space=pltpu.SMEM), vmem, vmem, vmem],
        out_specs=(vmem, vmem, vmem),
        scratch_shapes=[pltpu.VMEM((N_WIDE * depth, samples), BF16)],
        compiler_params=pltpu.CompilerParams(vmem_limit_bytes=VMEM_BYTES),
        cost_estimate=LIGHT,
        name="entry_slots",
    )(panel.reshape(1), owner, row, bag)


def scatter_kernel(slots_ref, base_ref, far_ref, tail_ref, out_ref, rows, blocks, sems):
    dump = N_WIDE * CAP

    def clear(i, _):
        rows[pl.ds(pl.multiple_of(i * 64, 64), 64), :] = jnp.zeros((64, E), F32)
        return 0

    lax.fori_loop(0, dump // 64, clear, 0)

    def place(i, _):
        first = pl.multiple_of(i * 16, 16)
        for f in range(8):
            cols = slice(f * E, (f + 1) * E)
            tile = base_ref[pl.ds(first, 16), cols] + far_ref[pl.ds(first, 16), cols].astype(F32)
            for b in range(16):
                row = tile[b : b + 1, :]
                for j in range(2):
                    slot = slots_ref[2 * f + j, first + b]
                    rows[pl.ds(slot, 1), :] = row
        return 0

    lax.fori_loop(0, base_ref.shape[0] // 16, place, 0)

    def copy_out(w):
        return pltpu.make_async_copy(blocks.at[w], out_ref.at[w], sems.at[w])

    def narrow_down(w, _):
        blocks[w, :CAP, :] = rows[pl.ds(pl.multiple_of(w * CAP, CAP), CAP), :].astype(BF16)
        blocks[w, CAP:, :] = tail_ref[w]
        copy_out(w).start()
        return 0

    lax.fori_loop(0, N_WIDE, narrow_down, 0)

    def finish(w, _):
        copy_out(w).wait()
        return 0

    lax.fori_loop(0, N_WIDE, finish, 0)


def scatter_entries(slots, base, far, tail):
    vmem = pl.BlockSpec(memory_space=pltpu.VMEM)
    return pl.pallas_call(
        scatter_kernel,
        out_shape=jax.ShapeDtypeStruct((N_WIDE, BLOCK, E), BF16),
        in_specs=[pl.BlockSpec(memory_space=pltpu.SMEM), vmem, vmem, vmem],
        out_specs=pl.BlockSpec(memory_space=pltpu.HBM),
        scratch_shapes=[
            pltpu.VMEM((N_WIDE * CAP + 8, E), F32),
            pltpu.VMEM((N_WIDE, BLOCK, E), BF16),
            pltpu.SemaphoreType.DMA((N_WIDE,)),
        ],
        compiler_params=pltpu.CompilerParams(vmem_limit_bytes=VMEM_BYTES),
        cost_estimate=LIGHT,
        name="place_entries",
    )(slots, base, far, tail)


def sums_kernel(count_ref, recv_ref, out_ref, bias_ref, total, left, right, todo):
    lane_rows = lax.broadcasted_iota(jnp.int32, (LO, E), 0)

    def listing(w, n):
        todo[n] = 2 * w
        n = n + jnp.where(count_ref[w] > 0, 1, 0)
        todo[n] = 2 * w + 1
        return n + jnp.where(count_ref[w] > CAP // 2, 1, 0)

    n = lax.fori_loop(0, N_WIDE, listing, 0)
    for k in range(6):
        todo[n + k] = -1
    total[...] = jnp.zeros_like(total)
    bias_ref[...] = jnp.sum(
        recv_ref[:, CAP + 8 : CAP + 16, :].astype(F32) + recv_ref[:, CAP + 16 : CAP + 24, :].astype(F32),
        axis=0,
    )

    def build(i, buf):
        for p in range(2):
            item = todo[i * 2 + p]
            w = jnp.maximum(item, 0) // 2
            half = jnp.maximum(item, 0) % 2
            ids = recv_ref[w, CAP : CAP + 16, :].astype(F32)
            row = (ids[0:4, :] * 64.0 + ids[4:8, :]).astype(jnp.int32) - 1
            row = jnp.where(half == 0, row[0:2, :], row[2:4, :])
            row = jnp.where(item < 0, -1, row)
            hi = row >> (LO.bit_length() - 1)
            lo = jnp.where(row < 0, -1, row & (LO - 1))
            hi_col = jnp.transpose(jnp.concatenate([hi] * 4, axis=0).astype(F32), (1, 0))
            for j in range(2):
                at = (2 * p + j) * E
                left[buf, :, at : at + E] = jnp.where(lane_rows == lo[j : j + 1, :], 1.0, 0.0).astype(BF16)
                v = recv_ref[w, pl.ds(pl.multiple_of(half * (CAP // 2), CAP // 2) + j * E, E), :]
                own = jnp.broadcast_to(hi_col[:, j : j + 1], (E, E)).astype(BF16)
                for h in range(HI):
                    right[buf, at : at + E, h * E : (h + 1) * E] = jnp.where(own == BF16(h), v, BF16(0))

    build(0, 0)

    def step(i, _):
        for b in range(2):
            build(2 * i + b + 1, 1 - b)
            total[...] += jnp.dot(left[b], right[b], preferred_element_type=F32)
        return 0

    lax.fori_loop(0, (n + 3) // 4, step, 0)
    for h in range(HI):
        out_ref[h * LO : (h + 1) * LO, :] = total[:, h * E : (h + 1) * E].astype(BF16)


def owned_sums(counts, recv):
    vmem = pl.BlockSpec(memory_space=pltpu.VMEM)
    return pl.pallas_call(
        sums_kernel,
        out_shape=(jax.ShapeDtypeStruct((N_ROWS, E), BF16), jax.ShapeDtypeStruct((8, E), F32)),
        in_specs=[pl.BlockSpec(memory_space=pltpu.SMEM), vmem],
        out_specs=(vmem, vmem),
        scratch_shapes=[
            pltpu.VMEM((LO, HI * E), F32),
            pltpu.VMEM((2, LO, CAP), BF16),
            pltpu.VMEM((2, CAP, HI * E), BF16),
            pltpu.SMEM((2 * N_WIDE + 16,), jnp.int32),
        ],
        compiler_params=pltpu.CompilerParams(vmem_limit_bytes=VMEM_BYTES),
        cost_estimate=LIGHT,
        name="owned_sums",
    )(counts, recv)


def summed(own, others):
    total = own.astype(F32)
    for other in others:
        total = total + other.astype(F32)
    return total


def far_kernel(block_ref, scaled_ref, embedded_ref, *refs):
    sent, turned, columns, terms, sems_in, sems_out = refs[:4], refs[4], *refs[5:]

    def copy_in(c):
        at = pl.multiple_of(block_ref[c] * 256, 256)
        part = columns.at[c // 4, :, pl.ds((c % 4) * 256, 256)]
        return pltpu.make_async_copy(embedded_ref.at[:, pl.ds(at, 256)], part, sems_in.at[c])

    def copy_out(q):
        return pltpu.make_async_copy(terms.at[q], sent[q], sems_out.at[q])

    for c in range(8):
        copy_in(c).start()
    turned[...] = jnp.transpose(scaled_ref[...], (1, 0))
    for route in range(2):
        for k in range(4):
            copy_in(4 * route + k).wait()
        term = jnp.dot(
            turned[route * 512 : (route + 1) * 512, :], columns[route], preferred_element_type=F32
        ).astype(BF16)
        for way in range(2):
            terms[2 * route + way] = term[way * 256 : (way + 1) * 256, :]
            copy_out(2 * route + way).start()
    for q in range(4):
        copy_out(q).wait()


def far_terms(embedded, scaled, blocks):
    hbm = pl.BlockSpec(memory_space=pltpu.HBM)
    vmem = pl.BlockSpec(memory_space=pltpu.VMEM)
    return pl.pallas_call(
        far_kernel,
        out_shape=[jax.ShapeDtypeStruct((256, 1024), BF16)] * 4 + [jax.ShapeDtypeStruct((1024, 512), BF16)],
        in_specs=[pl.BlockSpec(memory_space=pltpu.SMEM), vmem, hbm],
        out_specs=[hbm] * 4 + [vmem],
        scratch_shapes=[
            pltpu.VMEM((2, 512, 1024), BF16),
            pltpu.VMEM((4, 256, 1024), BF16),
            pltpu.SemaphoreType.DMA((8,)),
            pltpu.SemaphoreType.DMA((4,)),
        ],
        compiler_params=pltpu.CompilerParams(vmem_limit_bytes=VMEM_BYTES),
        cost_estimate=LIGHT,
        name="far_terms",
    )(blocks, scaled, embedded)


def near_kernel(block_ref, turned_ref, embedded_ref, *refs):
    passed, sent, columns, terms, sems_in, sems_out = refs[:4], refs[4:8], *refs[8:]

    def copy_in(c):
        at = pl.multiple_of(block_ref[c] * 256, 256)
        part = columns.at[c // 4, :, pl.ds((c % 4) * 256, 256)]
        return pltpu.make_async_copy(embedded_ref.at[:, pl.ds(at, 256)], part, sems_in.at[c])

    def copy_out(q):
        return pltpu.make_async_copy(terms.at[q], sent[q], sems_out.at[q])

    for c in range(16):
        copy_in(c).start()
    for q in range(4):
        route, way = q // 2, q % 2
        mine, other = slice(way * 256, (way + 1) * 256), slice((1 - way) * 256, (2 - way) * 256)
        for k in range(4):
            copy_in(4 * q + k).wait()
        term = jnp.dot(
            turned_ref[route * 512 : (route + 1) * 512, :], columns[q], preferred_element_type=F32
        )
        terms[q, mine, :] = (term[mine, :] + passed[q][...].astype(F32)).astype(BF16)
        terms[q, other, :] = term[other, :].astype(BF16)
        copy_out(q).start()
    for q in range(4):
        copy_out(q).wait()


def near_terms(embedded, turned, passed, blocks):
    hbm = pl.BlockSpec(memory_space=pltpu.HBM)
    vmem = pl.BlockSpec(memory_space=pltpu.VMEM)
    return pl.pallas_call(
        near_kernel,
        out_shape=[jax.ShapeDtypeStruct((512, 1024), BF16)] * 4,
        in_specs=[pl.BlockSpec(memory_space=pltpu.SMEM), vmem, hbm] + [vmem] * 4,
        out_specs=[hbm] * 4,
        scratch_shapes=[
            pltpu.VMEM((4, 512, 1024), BF16),
            pltpu.VMEM((4, 512, 1024), BF16),
            pltpu.SemaphoreType.DMA((16,)),
            pltpu.SemaphoreType.DMA((4,)),
        ],
        compiler_params=pltpu.CompilerParams(vmem_limit_bytes=VMEM_BYTES),
        cost_estimate=LIGHT,
        name="near_terms",
    )(blocks, turned, embedded, *passed)


def own_kernel(block_ref, turned_ref, embedded_ref, *refs):
    got, pieces, columns, sems = refs[:4], refs[4:12], *refs[12:]

    def copy_in(q):
        at = pl.multiple_of(block_ref[q] * 256, 256)
        part = columns.at[q // 4, :, pl.ds((q % 4) * 256, 256)]
        return pltpu.make_async_copy(embedded_ref.at[:, pl.ds(at, 256)], part, sems.at[q])

    for q in range(8):
        copy_in(q).start()
    for route in range(2):
        for k in range(4):
            copy_in(4 * route + k).wait()
        term = jnp.dot(
            turned_ref[route * 512 : (route + 1) * 512, :], columns[route], preferred_element_type=F32
        )
        for k in range(4):
            q = 4 * route + k
            at = pl.multiple_of(block_ref[8 + q] * 256, 256)
            total = term[:, k * 256 : (k + 1) * 256]
            for other in got[2 * route : 2 * route + 2]:
                total += other[:, pl.ds(at, 256)].astype(F32)
            pieces[q][...] = total.astype(BF16)


def own_terms(embedded, turned, got, blocks):
    hbm = pl.BlockSpec(memory_space=pltpu.HBM)
    vmem = pl.BlockSpec(memory_space=pltpu.VMEM)
    return pl.pallas_call(
        own_kernel,
        out_shape=[jax.ShapeDtypeStruct((512, 256), BF16)] * 8,
        in_specs=[pl.BlockSpec(memory_space=pltpu.SMEM), vmem, hbm] + [vmem] * 4,
        out_specs=[vmem] * 8,
        scratch_shapes=[pltpu.VMEM((2, 512, 1024), BF16), pltpu.SemaphoreType.DMA((8,))],
        compiler_params=pltpu.CompilerParams(vmem_limit_bytes=VMEM_BYTES),
        cost_estimate=LIGHT,
        name="own_terms",
    )(blocks, turned, embedded, *got)


def weight_grad_owned(pieces, x_lo):
    got_zy = [lax.ppermute(pieces[q], "wide", y_perm(d)) for q, d in enumerate(APART)]
    got_yz = [lax.ppermute(pieces[4 + q], "wide", z_perm(d)) for q, d in enumerate(APART)]
    pair = jnp.concatenate([summed(pieces[3], got_zy), summed(pieces[7], got_yz)], axis=0).astype(BF16)
    got = lax.ppermute(lax.dynamic_slice_in_dim(pair, (1 - x_lo) * E, E, 1), "wide", X_LO)
    return summed(lax.dynamic_slice_in_dim(pair, x_lo * E, E, 1), [got]).T


def base_kernel(
    panel_ref, embedded_ref, weight_ref, bias_ref, cot_ref, scaled_ref, rows_ref, mate_ref, out_ref
):
    cross = jnp.dot(embedded_ref[...], weight_ref[...], preferred_element_type=F32) + bias_ref[...]
    backward = lax.dot_general(
        scaled_ref[...], rows_ref[...], (((1,), (1,)), ((), ())), preferred_element_type=F32
    )
    grad = cot_ref[...].astype(F32)
    out_ref[...] = grad + grad * cross + backward + mate_ref[...].astype(F32)


def base_terms(panel, embedded, weight, bias, cotangent, scaled, from_mate):
    samples, width = cotangent.shape
    tile = 256
    steps = width // tile
    return pl.pallas_call(
        base_kernel,
        out_shape=jax.ShapeDtypeStruct((samples, width), F32),
        grid_spec=pltpu.PrefetchScalarGridSpec(
            num_scalar_prefetch=1,
            grid=(steps,),
            in_specs=[
                pl.BlockSpec(embedded.shape, lambda i, p: (0, 0)),
                pl.BlockSpec((weight.shape[0], tile), lambda i, p: (0, i)),
                pl.BlockSpec((1, tile), lambda i, p: (0, i)),
                pl.BlockSpec((samples, tile), lambda i, p: (0, i)),
                pl.BlockSpec((samples, width), lambda i, p: (0, 0)),
                pl.BlockSpec((tile, width), lambda i, p: (p[0] * steps + i, 0)),
                pl.BlockSpec((samples, tile), lambda i, p: (0, i)),
            ],
            out_specs=pl.BlockSpec((samples, tile), lambda i, p: (0, i)),
        ),
        compiler_params=pltpu.CompilerParams(vmem_limit_bytes=VMEM_BYTES),
        cost_estimate=LIGHT,
        name="base_terms",
    )(panel.reshape(1), embedded, weight, bias.reshape(1, -1), cotangent, scaled, weight, from_mate)


def over_narrow(part, core):
    rows = part.shape[0] // 2
    keep = lax.dynamic_slice_in_dim(part, core * rows, rows, 0)
    send = lax.dynamic_slice_in_dim(part, (1 - core) * rows, rows, 0)
    chip = summed(keep, [lax.ppermute(send, "narrow", CORE)]).astype(BF16)
    mine = summed(chip, [lax.ppermute(chip, "narrow", X_HI)])
    mate = lax.ppermute(mine, "narrow", CORE)
    low = jnp.where(core == 0, mine, mate)
    high = jnp.where(core == 0, mate, mine)
    return jnp.concatenate([low, high], axis=0)


def body(
    embedded,
    cotangent,
    cross_weight,
    cross_bias,
    bag_size,
    row_owner,
    row_id,
    emb_table,
    adagrad_state,
):
    panel = lax.axis_index("narrow")
    wide = lax.axis_index("wide")
    z, y, x_lo = wide // 8, (wide // 2) % 4, wide % 2
    core = panel % 2
    batch_rows, width = cotangent.shape
    feats = width // E
    norm_factor = 1.0 / math.sqrt(batch_rows * N_WIDE)

    x_panel = lax.dynamic_slice_in_dim(embedded, panel * width, width, 1)
    grad_out = cotangent.astype(F32)
    scaled = (grad_out * x_panel.astype(F32)).astype(BF16)

    def backward_part(k):
        rows = lax.dynamic_slice_in_dim(cross_weight, (panel ^ k) * width, width, 0)
        return lax.dot_general(scaled, rows, (((1,), (1,)), ((), ())), preferred_element_type=F32)

    from_mate_far = lax.ppermute(backward_part(3).astype(BF16), "narrow", CORE)
    from_mate = lax.ppermute(backward_part(1).astype(BF16), "narrow", CORE)
    chip_far = (backward_part(2) + from_mate_far.astype(F32)).astype(BF16)
    chip_far, embedded, from_mate = lax.optimization_barrier((chip_far, embedded, from_mate))
    far = lax.ppermute(chip_far, "narrow", X_HI)

    far_blocks = jnp.stack([((z + 2) % 4) * 4 + k for k in range(4)] + [k * 4 + (y + 2) % 4 for k in range(4)])
    near_blocks = jnp.stack(
        [((z + d) % 4) * 4 + k for d in (1, 3) for k in range(4)]
        + [k * 4 + (y + d) % 4 for d in (1, 3) for k in range(4)]
    )
    ways = [z_perm(1), z_perm(3), y_perm(1), y_perm(3)]
    *sent, turned = far_terms(embedded, scaled, far_blocks)
    passed = [lax.ppermute(sent[q], "wide", ways[q]) for q in range(4)]
    embedded, turned = lax.optimization_barrier((embedded, turned))
    base = base_terms(panel, embedded, cross_weight, cross_bias, cotangent, scaled, from_mate)
    embedded, base, far = lax.optimization_barrier((embedded, base, far))
    sent = near_terms(embedded, turned, passed, near_blocks)
    got = [lax.ppermute(sent[q], "wide", ways[q]) for q in range(4)]
    row_owner, row_id, bag_size, *_ = lax.optimization_barrier((row_owner, row_id, bag_size, sent[0]))

    slots, ids, counts = entry_slots(
        panel, row_owner.reshape(row_owner.shape[1:3]).T, row_id.reshape(row_id.shape[1:]).T, bag_size.T
    )
    ids = ids.reshape(2, N_WIDE, CAP // E, E).transpose(1, 0, 2, 3)
    counts = counts[:, 0].astype(jnp.int32)

    bias_part = jnp.sum(scaled, axis=0, dtype=F32)
    bias_top = lax.reduce_precision(bias_part, 8, 7)
    bias_parts = jnp.stack([bias_top, bias_part - bias_top]).astype(BF16).reshape(1, 16, E)
    count_parts = jnp.stack([counts // 64, counts % 64], axis=1).astype(BF16)
    tail = jnp.concatenate(
        [
            ids.reshape(N_WIDE, 8, E),
            jnp.broadcast_to(bias_parts, (N_WIDE, 16, E)),
            jnp.broadcast_to(jnp.repeat(count_parts, 4, axis=1)[:, :, None], (N_WIDE, 8, E)),
        ],
        axis=1,
    )

    payload = scatter_entries(slots, base, far, tail)
    payload, *got = lax.optimization_barrier((payload, *got))
    recv = lax.all_to_all(payload, "wide", split_axis=0, concat_axis=0, tiled=True)
    later = APART + (0,)
    own_blocks = jnp.stack(
        [z * 4 + (y + d) % 4 for d in later]
        + [((z + d) % 4) * 4 + y for d in later]
        + [(y + d) % 4 for d in later]
        + [(z + d) % 4 for d in later]
    )
    weight_grad = weight_grad_owned(own_terms(embedded, turned, got, own_blocks), x_lo) * norm_factor
    recv, weight_grad = lax.optimization_barrier((recv, weight_grad))

    recv_counts = (recv[:, CAP + 24, 0].astype(F32) * 64.0 + recv[:, CAP + 28, 0].astype(F32)).astype(jnp.int32)
    sums, bias_sums = owned_sums(recv_counts, recv)
    bias_grad = bias_sums.reshape(-1) * norm_factor
    row_grad = over_narrow(sums, core)
    new_state = adagrad_state + jnp.mean(row_grad * row_grad, axis=1)
    new_table = emb_table - LEARN_RATE * row_grad / jnp.sqrt(new_state)[:, None]
    return (weight_grad, bias_grad, new_table, new_state)


def solution(mesh):
    in_specs = (
        P("wide", None),
        P("wide", "narrow"),
        P(None, "narrow"),
        P("narrow"),
        P("wide", None),
        P("narrow", "wide", None, None),
        P("narrow", "wide", None),
        P("wide", None),
        P("wide"),
    )
    out_specs = (P("wide", "narrow"), P("narrow"), P("wide", None), P("wide"))
    return jax.shard_map(body, mesh=mesh, in_specs=in_specs, out_specs=out_specs, check_vma=False)
```

```python
import math

import jax
import jax.numpy as jnp
from jax import lax
from jax.experimental import pallas as pl
from jax.experimental.pallas import tpu as pltpu
from jax.sharding import PartitionSpec as P

LEARN_RATE = 0.3
E = 128
N_WIDE = 32
CAP = 512
TAIL = 32
BLOCK = CAP + TAIL
N_ROWS = 2048
HI = 4
LO = N_ROWS // HI
F32 = jnp.float32
BF16 = jnp.bfloat16
LIGHT = pl.CostEstimate(flops=1, bytes_accessed=1, transcendentals=0)
VMEM_BYTES = 56 << 20
NT = (((1,), (1,)), ((), ()))


def z_perm(d):
    return [(i, ((i // 8 + d) % 4) * 8 + i % 8) for i in range(N_WIDE)]


def y_perm(d):
    return [(i, (i // 8) * 8 + (((i // 2) % 4 + d) % 4) * 2 + i % 2) for i in range(N_WIDE)]


def y_flip(m):
    return [(i, i ^ (2 * m)) for i in range(N_WIDE)]


def z_flip(m):
    return [(i, i ^ (8 * m)) for i in range(N_WIDE)]


X_LO = [(i, i ^ 1) for i in range(N_WIDE)]
CORE = [(i, i ^ 1) for i in range(4)]
X_HI = [(i, i ^ 2) for i in range(4)]


def slots_kernel(panel_ref, owner_ref, row_ref, bag_ref, slots_ref, ids_ref, count_ref, onehots):
    depth, samples = owner_ref.shape
    feats = depth // 2
    bag = bag_ref[pl.ds(pl.multiple_of(panel_ref[0] * feats, feats), feats), :]
    bag = jnp.concatenate([bag[k // 2 : k // 2 + 1, :] for k in range(depth)], axis=0)
    live = (lax.broadcasted_iota(jnp.int32, (depth, samples), 0) & 1) < bag
    owner = jnp.where(live, owner_ref[...], N_WIDE)
    for t in range(N_WIDE):
        onehots[t * depth : (t + 1) * depth, :] = jnp.where(owner == t, 1.0, 0.0).astype(BF16)

    size = N_WIDE * depth
    first = lax.broadcasted_iota(jnp.int32, (samples, samples), 0)
    second = lax.broadcasted_iota(jnp.int32, (samples, samples), 1)
    before = jnp.where(first < second, 1.0, 0.0).astype(BF16)
    within = jnp.dot(onehots[...], before, preferred_element_type=F32)
    in_row = jnp.dot(onehots[...], jnp.ones((samples, E), BF16), preferred_element_type=F32)
    top = jnp.floor(in_row * (1.0 / 16.0))
    low = (in_row - 16.0 * top).astype(BF16)
    top = top.astype(BF16)
    r = lax.broadcasted_iota(jnp.int32, (size, size), 0)
    c = lax.broadcasted_iota(jnp.int32, (size, size), 1)
    shift = depth.bit_length() - 1
    earlier = jnp.where((r >> shift == c >> shift) & (c < r), 1.0, 0.0).astype(BF16)
    rows_before = 16.0 * jnp.dot(earlier, top, preferred_element_type=F32) + jnp.dot(
        earlier, low, preferred_element_type=F32
    )
    t_rows = lax.broadcasted_iota(jnp.int32, (N_WIDE, size), 0)
    t_cols = lax.broadcasted_iota(jnp.int32, (N_WIDE, size), 1)
    members = jnp.where(t_rows == t_cols >> shift, 1.0, 0.0).astype(BF16)
    count_ref[...] = 16.0 * jnp.dot(members, top, preferred_element_type=F32) + jnp.dot(
        members, low, preferred_element_type=F32
    )
    place = jnp.zeros((depth, samples), F32)
    for t in range(N_WIDE):
        at = slice(t * depth, (t + 1) * depth)
        ahead = jnp.concatenate([rows_before[at, :]] * (samples // E), axis=1)
        place = place + jnp.where(owner == t, within[at, :] + ahead, 0.0)
    place = place.astype(jnp.int32)
    slots = jnp.where(live, owner * CAP + place, N_WIDE * CAP)
    for k in range(samples // E):
        slots_ref[k * depth : (k + 1) * depth, :] = slots[:, k * E : (k + 1) * E]

    marked = row_ref[...] + 1
    top = (marked >> 6).astype(F32)
    low = (marked & 63).astype(F32)
    owners = lax.broadcasted_iota(jnp.int32, (N_WIDE, samples), 0)
    places = lax.broadcasted_iota(jnp.int32, (CAP, samples), 0)
    ids = jnp.zeros((2 * N_WIDE, CAP), F32)
    for k in range(depth):
        at = slice(k, k + 1)
        mine = owners == owner[at, :]
        marks = jnp.concatenate([jnp.where(mine, top[at, :], 0.0), jnp.where(mine, low[at, :], 0.0)], axis=0)
        there = jnp.where(places == place[at, :], 1.0, 0.0).astype(BF16)
        ids = ids + lax.dot_general(
            marks.astype(BF16), there, (((1,), (1,)), ((), ())), preferred_element_type=F32
        )
    ids_ref[...] = ids


def entry_slots(panel, owner, row, bag):
    vmem = pl.BlockSpec(memory_space=pltpu.VMEM)
    depth, samples = owner.shape
    return pl.pallas_call(
        slots_kernel,
        out_shape=(
            jax.ShapeDtypeStruct((depth * samples // E, E), jnp.int32),
            jax.ShapeDtypeStruct((2 * N_WIDE, CAP), F32),
            jax.ShapeDtypeStruct((N_WIDE, E), F32),
        ),
        in_specs=[pl.BlockSpec(memory_space=pltpu.SMEM), vmem, vmem, vmem],
        out_specs=(vmem, vmem, vmem),
        scratch_shapes=[pltpu.VMEM((N_WIDE * depth, samples), BF16)],
        compiler_params=pltpu.CompilerParams(vmem_limit_bytes=VMEM_BYTES),
        cost_estimate=LIGHT,
        name="entry_slots",
    )(panel.reshape(1), owner, row, bag)


def place_kernel(
    slots_ref, base_hbm, mate_hbm, far_hbm, ids_ref, count_ref, bias_ref, out_ref, base, mate, far, rows, blocks, sems, sems_in
):
    depth = 16
    dump = N_WIDE * CAP
    loads = [
        pltpu.make_async_copy(src, dst, sems_in.at[k])
        for k, (src, dst) in enumerate(((base_hbm, base), (mate_hbm, mate), (far_hbm, far)))
    ]
    for load in loads:
        load.start()

    def clear(i, _):
        rows[pl.ds(pl.multiple_of(i * 256, 256), 256), :] = jnp.zeros((256, E), F32)
        return 0

    lax.fori_loop(0, dump // 256, clear, 0)
    for load in loads:
        load.wait()

    def place(i, _):
        first = pl.multiple_of(i * 16, 16)
        at = (first // E) * (depth * E) + first % E
        for f in range(8):
            cols = slice(f * E, (f + 1) * E)
            tile = base[pl.ds(first, 16), cols] + (
                mate[pl.ds(first, 16), cols].astype(F32) + far[pl.ds(first, 16), cols].astype(F32)
            )
            for b in range(16):
                row = tile[b : b + 1, :]
                for j in range(2):
                    slot = slots_ref[at + (2 * f + j) * E + b]
                    rows[pl.ds(slot, 1), :] = row
        return 0

    lax.fori_loop(0, base.shape[0] // 16, place, 0)

    bias_top = bias_ref[...].astype(BF16)
    bias_low = (bias_ref[...] - bias_top.astype(F32)).astype(BF16)

    def copy_out(w):
        return pltpu.make_async_copy(blocks.at[w], out_ref.at[w], sems.at[w])

    def narrow_down(w, _):
        blocks[w, :CAP, :] = rows[pl.ds(pl.multiple_of(w * CAP, CAP), CAP), :].astype(BF16)
        top = ids_ref[pl.ds(w, 1), :]
        low = ids_ref[pl.ds(N_WIDE + w, 1), :]
        count = count_ref[pl.ds(w, 1), :]
        count_top = jnp.floor(count * (1.0 / 64.0))
        parts = [top[:, k * E : (k + 1) * E] for k in range(4)] + [low[:, k * E : (k + 1) * E] for k in range(4)]
        ends = [count_top] * 4 + [count - 64.0 * count_top] * 4
        blocks[w, CAP:, :] = jnp.concatenate(
            [
                jnp.concatenate(parts, axis=0).astype(BF16),
                bias_top,
                bias_low,
                jnp.concatenate(ends, axis=0).astype(BF16),
            ],
            axis=0,
        )
        copy_out(w).start()
        return 0

    lax.fori_loop(0, N_WIDE, narrow_down, 0)

    def finish(w, _):
        copy_out(w).wait()
        return 0

    lax.fori_loop(0, N_WIDE, finish, 0)


def place_entries(slots, base, mate, far, ids, counts, bias):
    vmem = pl.BlockSpec(memory_space=pltpu.VMEM)
    hbm = pl.BlockSpec(memory_space=pltpu.HBM)
    return pl.pallas_call(
        place_kernel,
        out_shape=jax.ShapeDtypeStruct((N_WIDE, BLOCK, E), BF16),
        in_specs=[pl.BlockSpec(memory_space=pltpu.SMEM), hbm, hbm, hbm, vmem, vmem, vmem],
        out_specs=hbm,
        scratch_shapes=[
            pltpu.VMEM(base.shape, F32),
            pltpu.VMEM(base.shape, BF16),
            pltpu.VMEM(base.shape, BF16),
            pltpu.VMEM((N_WIDE * CAP + 8, E), F32),
            pltpu.VMEM((N_WIDE, BLOCK, E), BF16),
            pltpu.SemaphoreType.DMA((N_WIDE,)),
            pltpu.SemaphoreType.DMA((3,)),
        ],
        compiler_params=pltpu.CompilerParams(vmem_limit_bytes=VMEM_BYTES),
        cost_estimate=LIGHT,
        name="place_entries",
    )(slots, base, mate, far, ids, counts, bias)


def sums_kernel(count_ref, recv_ref, out_ref, bias_ref, total, left, right, todo):
    lane_rows = lax.broadcasted_iota(jnp.int32, (LO, E), 0)

    def listing(w, n):
        todo[n] = 2 * w
        n = n + jnp.where(count_ref[w] > 0, 1, 0)
        todo[n] = 2 * w + 1
        return n + jnp.where(count_ref[w] > CAP // 2, 1, 0)

    n = lax.fori_loop(0, N_WIDE, listing, 0)
    for k in range(12):
        todo[n + k] = -1
    total[...] = jnp.zeros_like(total)
    bias_ref[...] = jnp.sum(
        recv_ref[:, CAP + 8 : CAP + 16, :].astype(F32) + recv_ref[:, CAP + 16 : CAP + 24, :].astype(F32),
        axis=0,
    )

    def build(i, buf):
        for p in range(4):
            item = todo[i * 4 + p]
            w = jnp.maximum(item, 0) // 2
            half = jnp.maximum(item, 0) % 2
            ids = recv_ref[w, CAP : CAP + 16, :].astype(F32)
            row = (ids[0:4, :] * 64.0 + ids[4:8, :]).astype(jnp.int32) - 1
            row = jnp.where(half == 0, row[0:2, :], row[2:4, :])
            row = jnp.where(item < 0, -1, row)
            hi = row >> (LO.bit_length() - 1)
            lo = jnp.where(row < 0, -1, row & (LO - 1))
            hi_col = jnp.transpose(jnp.concatenate([hi] * 4, axis=0).astype(F32), (1, 0))
            for j in range(2):
                at = (2 * p + j) * E
                left[buf, :, at : at + E] = jnp.where(lane_rows == lo[j : j + 1, :], 1.0, 0.0).astype(BF16)
                v = recv_ref[w, pl.ds(pl.multiple_of(half * (CAP // 2), CAP // 2) + j * E, E), :]
                own = jnp.broadcast_to(hi_col[:, j : j + 1], (E, E)).astype(BF16)
                for h in range(HI):
                    right[buf, at : at + E, h * E : (h + 1) * E] = jnp.where(own == BF16(h), v, BF16(0))

    build(0, 0)

    def step(i, _):
        for b in range(2):
            build(2 * i + b + 1, 1 - b)
            total[...] += jnp.dot(left[b], right[b], preferred_element_type=F32)
        return 0

    lax.fori_loop(0, (n + 7) // 8, step, 0)
    for h in range(HI):
        out_ref[h * LO : (h + 1) * LO, :] = total[:, h * E : (h + 1) * E].astype(BF16)


def owned_sums(counts, recv):
    vmem = pl.BlockSpec(memory_space=pltpu.VMEM)
    return pl.pallas_call(
        sums_kernel,
        out_shape=(jax.ShapeDtypeStruct((N_ROWS, E), BF16), jax.ShapeDtypeStruct((8, E), F32)),
        in_specs=[pl.BlockSpec(memory_space=pltpu.SMEM), vmem],
        out_specs=(vmem, vmem),
        scratch_shapes=[
            pltpu.VMEM((LO, HI * E), F32),
            pltpu.VMEM((2, LO, 2 * CAP), BF16),
            pltpu.VMEM((2, 2 * CAP, HI * E), BF16),
            pltpu.SMEM((2 * N_WIDE + 16,), jnp.int32),
        ],
        compiler_params=pltpu.CompilerParams(vmem_limit_bytes=VMEM_BYTES),
        cost_estimate=LIGHT,
        name="owned_sums",
    )(counts, recv)


def summed(own, others):
    total = own.astype(F32)
    for other in others:
        total = total + other.astype(F32)
    return total


def own_chunk(a):
    return pl.multiple_of(a * 1024, 1024)


def ring_term(route, turned, embedded, z, y, d):
    part = turned[route * 512 : (route + 1) * 512, :]
    if route == 0:
        rows = embedded[:, pl.ds(own_chunk((z + d) % 4), 1024)]
        return jnp.dot(part, rows, preferred_element_type=F32)
    start = ((y + d) % 4) * 256
    blocks = [embedded[:, pl.ds(pl.multiple_of(k * 1024 + start, 256), 256)] for k in range(4)]
    return jnp.concatenate([jnp.dot(part, rows, preferred_element_type=F32) for rows in blocks], axis=1)


def sent_kernel(n_ref, z_ref, y_ref, cot_hbm, embedded_hbm, weight_hbm, *refs):
    parts_hbm, first_hbm, second_hbm, (scaled_hbm, turned_hbm, bias_ref) = refs[:3], refs[3:7], refs[7:11], refs[11:14]
    cot, embedded, weight, scaled, turned, parts, first, second, sems, sems_out = refs[14:]
    n, z, y = n_ref[0], z_ref[0], y_ref[0]

    def columns(q):
        at = pl.ds(own_chunk(n ^ q), 1024)
        return pltpu.make_async_copy(embedded_hbm.at[:, at], embedded.at[:, at], sems.at[q])

    def rows(q):
        at = pl.ds(own_chunk(n ^ q), 1024)
        return pltpu.make_async_copy(weight_hbm.at[at, :], weight.at[q - 1], sems.at[3 + q])

    outs = [(parts.at[q], parts_hbm[q]) for q in range(3)]
    outs += [(first.at[q], first_hbm[q]) for q in range(4)] + [(second.at[q], second_hbm[q]) for q in range(4)]
    outs += [(scaled, scaled_hbm), (turned, turned_hbm)]
    outs = [pltpu.make_async_copy(src, dst, sems_out.at[k]) for k, (src, dst) in enumerate(outs)]

    get_cot = pltpu.make_async_copy(cot_hbm, cot, sems.at[7])
    get_cot.start()
    columns(0).start()
    rows(3).start()
    get_cot.wait()
    columns(0).wait()
    for q in (1, 2):
        rows(q).start()
    for q in (1, 2, 3):
        columns(q).start()
    grads = (cot[...].astype(F32) * embedded[:, pl.ds(own_chunk(n), 1024)].astype(F32)).astype(BF16)
    scaled[...] = grads
    turned[...] = jnp.transpose(grads, (1, 0))
    sums = jnp.sum(grads.astype(F32), axis=0, keepdims=True)
    bias_ref[...] = jnp.concatenate([sums[:, k * E : (k + 1) * E] for k in range(8)], axis=0)
    outs[11].start()
    outs[12].start()
    for k, q in enumerate((3, 1, 2)):
        rows(q).wait()
        part = lax.dot_general(scaled[...], weight[q - 1], NT, preferred_element_type=F32)
        parts[k] = part.astype(BF16)
        outs[k].start()
    for q in (1, 2, 3):
        columns(q).wait()
    for route in range(2):
        term = ring_term(route, turned, embedded, z, y, 2).astype(BF16)
        for way in range(2):
            first[2 * route + way, :256, :] = term[way * 256 : (way + 1) * 256, :]
        for way in range(2):
            q = 2 * route + way
            term = ring_term(route, turned, embedded, z, y, 3 if way else 1).astype(BF16)
            first[q, 256:, :] = term[(1 - way) * 256 : (2 - way) * 256, :]
            second[q] = term[way * 256 : (way + 1) * 256, :]
            outs[3 + q].start()
            outs[7 + q].start()
    for copy in outs:
        copy.wait()


def sent_terms(n, z, y, cotangent, embedded, weight):
    hbm = pl.BlockSpec(memory_space=pltpu.HBM)
    smem = pl.BlockSpec(memory_space=pltpu.SMEM)
    samples, width = cotangent.shape
    shape = jax.ShapeDtypeStruct
    full, half = shape((samples, width), BF16), shape((256, 1024), BF16)
    results = pl.pallas_call(
        sent_kernel,
        out_shape=[full] * 3 + [shape((512, 1024), BF16)] * 4 + [half] * 4
        + [full, shape((width, samples), BF16), shape((8, E), F32)],
        in_specs=[smem] * 3 + [hbm] * 3,
        out_specs=[hbm] * 13 + [pl.BlockSpec(memory_space=pltpu.VMEM)],
        scratch_shapes=[
            pltpu.VMEM(cotangent.shape, BF16),
            pltpu.VMEM(embedded.shape, BF16),
            pltpu.VMEM((3, 1024, 1024), BF16),
            pltpu.VMEM((samples, width), BF16),
            pltpu.VMEM((width, samples), BF16),
            pltpu.VMEM((3, samples, width), BF16),
            pltpu.VMEM((4, 512, 1024), BF16),
            pltpu.VMEM((4, 256, 1024), BF16),
            pltpu.SemaphoreType.DMA((8,)),
            pltpu.SemaphoreType.DMA((13,)),
        ],
        compiler_params=pltpu.CompilerParams(vmem_limit_bytes=VMEM_BYTES),
        cost_estimate=LIGHT,
        name="sent_terms",
    )(n, z, y, cotangent, embedded, weight)
    return results[:3], results[3:7], results[7:11], *results[11:]


def kept_kernel(n_ref, z_ref, y_ref, cot_hbm, embedded_hbm, weight_hbm, bias_ref, scaled_hbm, turned_hbm, *refs):
    base_hbm, own_hbm, (cot, embedded, weight, scaled, turned, cross, base, own, sems, sems_out) = refs[0], refs[1:3], refs[3:]
    n, z, y = n_ref[0], z_ref[0], y_ref[0]

    def columns(q):
        at = pl.ds(own_chunk(n ^ q), 1024)
        return pltpu.make_async_copy(embedded_hbm.at[:, at], embedded.at[:, at], sems.at[q])

    def rows(q):
        at = pl.ds(own_chunk(n ^ q), 1024)
        return pltpu.make_async_copy(weight_hbm.at[at, :], weight.at[q], sems.at[4 + q])

    others = [(scaled_hbm, scaled), (cot_hbm, cot), (turned_hbm, turned)]
    others = [pltpu.make_async_copy(src, dst, sems.at[8 + k]) for k, (src, dst) in enumerate(others)]
    outs = [(base, base_hbm), (own.at[0], own_hbm[0]), (own.at[1], own_hbm[1])]
    outs = [pltpu.make_async_copy(src, dst, sems_out.at[k]) for k, (src, dst) in enumerate(outs)]
    rows(0).start()
    columns(0).start()
    others[0].start()
    rows(0).wait()
    columns(0).wait()
    for q in (1, 2, 3):
        rows(q).start()
        columns(q).start()
    others[1].start()
    others[2].start()
    cross[...] = jnp.dot(embedded[:, pl.ds(own_chunk(n), 1024)], weight[0], preferred_element_type=F32)
    others[0].wait()
    base[...] = lax.dot_general(scaled[...], weight[0], NT, preferred_element_type=F32)
    for q in (1, 2):
        rows(q).wait()
        columns(q).wait()
        cross[...] += jnp.dot(embedded[:, pl.ds(own_chunk(n ^ q), 1024)], weight[q], preferred_element_type=F32)
    rows(3).wait()
    columns(3).wait()
    others[1].wait()
    grad = cot[...].astype(F32)
    last = jnp.dot(embedded[:, pl.ds(own_chunk(n ^ 3), 1024)], weight[3], preferred_element_type=F32)
    base[...] += grad + grad * (cross[...] + last + bias_ref[...])
    outs[0].start()
    others[2].wait()
    for route in range(2):
        own[route] = ring_term(route, turned, embedded, z, y, 0).astype(BF16)
        outs[1 + route].start()
    for copy in outs:
        copy.wait()


def kept_terms(n, z, y, cotangent, embedded, weight, bias, scaled, turned):
    hbm = pl.BlockSpec(memory_space=pltpu.HBM)
    smem = pl.BlockSpec(memory_space=pltpu.SMEM)
    samples, width = cotangent.shape
    return pl.pallas_call(
        kept_kernel,
        out_shape=[jax.ShapeDtypeStruct((samples, width), F32)] + [jax.ShapeDtypeStruct((512, 1024), BF16)] * 2,
        in_specs=[smem] * 3 + [hbm] * 3 + [pl.BlockSpec(memory_space=pltpu.VMEM)] + [hbm] * 2,
        out_specs=[hbm] * 3,
        scratch_shapes=[
            pltpu.VMEM(cotangent.shape, BF16),
            pltpu.VMEM(embedded.shape, BF16),
            pltpu.VMEM((4, 1024, 1024), BF16),
            pltpu.VMEM((samples, width), BF16),
            pltpu.VMEM((width, samples), BF16),
            pltpu.VMEM((samples, width), F32),
            pltpu.VMEM((samples, width), F32),
            pltpu.VMEM((2, 512, 1024), BF16),
            pltpu.SemaphoreType.DMA((11,)),
            pltpu.SemaphoreType.DMA((3,)),
        ],
        compiler_params=pltpu.CompilerParams(vmem_limit_bytes=VMEM_BYTES),
        cost_estimate=LIGHT,
        name="kept_terms",
    )(n, z, y, cotangent, embedded, weight, bias.reshape(1, -1), scaled, turned)


def halves_of(array, bit, axis):
    size = array.shape[axis] // 2
    return (
        lax.dynamic_slice_in_dim(array, bit * size, size, axis),
        lax.dynamic_slice_in_dim(array, (1 - bit) * size, size, axis),
    )


def over_narrow(part, core):
    rows = part.shape[0] // 2
    keep = lax.dynamic_slice_in_dim(part, core * rows, rows, 0)
    send = lax.dynamic_slice_in_dim(part, (1 - core) * rows, rows, 0)
    chip = summed(keep, [lax.ppermute(send, "narrow", CORE)]).astype(BF16)
    mine = summed(chip, [lax.ppermute(chip, "narrow", X_HI)])
    mate = lax.ppermute(mine, "narrow", CORE)
    low = jnp.where(core == 0, mine, mate)
    high = jnp.where(core == 0, mate, mine)
    return jnp.concatenate([low, high], axis=0)


def body(
    embedded,
    cotangent,
    cross_weight,
    cross_bias,
    bag_size,
    row_owner,
    row_id,
    emb_table,
    adagrad_state,
):
    panel = lax.axis_index("narrow")
    wide = lax.axis_index("wide")
    z, y, x_lo = wide // 8, (wide // 2) % 4, wide % 2
    core = panel % 2
    batch_rows = cotangent.shape[0]
    norm_factor = 1.0 / math.sqrt(batch_rows * N_WIDE)

    at = (panel.reshape(1), z.reshape(1), y.reshape(1))

    parts, first, second, scaled, turned, bias_part = sent_terms(*at, cotangent, embedded, cross_weight)
    from_mate_far = lax.ppermute(parts[0], "narrow", CORE)
    from_mate = lax.ppermute(parts[1], "narrow", CORE)
    ways = [z_perm(1), z_perm(3), y_perm(1), y_perm(3)]
    first = [lax.ppermute(first[q], "wide", ways[q]) for q in range(4)]
    chip_far = (parts[2].astype(F32) + from_mate_far.astype(F32)).astype(BF16)
    chip_far, scaled, from_mate = lax.optimization_barrier((chip_far, scaled, from_mate))
    far = lax.ppermute(chip_far, "narrow", X_HI)

    base, *own = kept_terms(*at, cotangent, embedded, cross_weight, cross_bias, scaled, turned)
    row_owner, row_id, bag_size, base = lax.optimization_barrier((row_owner, row_id, bag_size, base))
    slots, ids, counts = entry_slots(
        panel, row_owner.reshape(row_owner.shape[1:3]).T, row_id.reshape(row_id.shape[1:]).T, bag_size.T
    )
    slots, ids, counts, far, *first = lax.optimization_barrier((slots, ids, counts, far, *first))
    second = [(second[q].astype(F32) + first[q][:256].astype(F32)).astype(BF16) for q in range(4)]
    slots, *second = lax.optimization_barrier((slots, *second))
    second = [lax.ppermute(second[q], "wide", ways[q]) for q in range(4)]

    payload = place_entries(slots.reshape(-1), base, from_mate, far, ids, counts, bias_part)
    payload, *second = lax.optimization_barrier((payload, *second))
    recv = lax.all_to_all(payload, "wide", split_axis=0, concat_axis=0, tiled=True)

    kept = []
    for route, (place, flip) in enumerate(((y, y_flip), (z, z_flip))):
        up, down = 2 * route, 2 * route + 1
        total = own[route].astype(F32) + jnp.concatenate(
            [second[up].astype(F32) + first[down][256:].astype(F32), second[down].astype(F32) + first[up][256:].astype(F32)],
            axis=0,
        )
        keep, send = halves_of(total, place // 2, 1)
        kept.append(keep + lax.ppermute(send.astype(BF16), "wide", flip(2)).astype(F32))
    quarters = []
    for total, place in zip(kept, (y, z)):
        keep, send = halves_of(total, place % 2, 1)
        quarters.append((keep.astype(BF16), send.astype(BF16)))
    recv, *sends = lax.optimization_barrier((recv, quarters[0][1], quarters[1][1]))
    pair = jnp.concatenate(
        [
            summed(quarters[0][0], [lax.ppermute(sends[0], "wide", y_flip(1))]),
            summed(quarters[1][0], [lax.ppermute(sends[1], "wide", z_flip(1))]),
        ],
        axis=0,
    ).astype(BF16)
    keep, send = halves_of(pair, x_lo, 1)
    weight_grad = summed(keep, [lax.ppermute(send, "wide", X_LO)]).T * norm_factor

    recv_counts = (recv[:, CAP + 24, 0].astype(F32) * 64.0 + recv[:, CAP + 28, 0].astype(F32)).astype(jnp.int32)
    sums, bias_sums = owned_sums(recv_counts, recv)
    bias_grad = bias_sums.reshape(-1) * norm_factor
    row_grad = over_narrow(sums, core)
    new_state = adagrad_state + jnp.mean(row_grad * row_grad, axis=1)
    new_table = emb_table - LEARN_RATE * row_grad / jnp.sqrt(new_state)[:, None]
    return (weight_grad, bias_grad, new_table, new_state)


def solution(mesh):
    in_specs = (
        P("wide", None),
        P("wide", "narrow"),
        P(None, "narrow"),
        P("narrow"),
        P("wide", None),
        P("narrow", "wide", None, None),
        P("narrow", "wide", None),
        P("wide", None),
        P("wide"),
    )
    out_specs = (P("wide", "narrow"), P("narrow"), P("wide", None), P("wide"))
    return jax.shard_map(body, mesh=mesh, in_specs=in_specs, out_specs=out_specs, check_vma=False)
```

```python
import math

import jax
import jax.numpy as jnp
from jax import lax
from jax.experimental import pallas as pl
from jax.experimental.pallas import tpu as pltpu
from jax.sharding import PartitionSpec as P

LEARN_RATE = 0.3
E = 128
N_WIDE = 32
CAP = 512
TAIL = 32
BLOCK = CAP + TAIL
N_ROWS = 2048
HI = 4
LO = N_ROWS // HI
F32 = jnp.float32
BF16 = jnp.bfloat16
LIGHT = pl.CostEstimate(flops=1, bytes_accessed=1, transcendentals=0)
VMEM_BYTES = 56 << 20
NT = (((1,), (1,)), ((), ()))


def z_perm(d):
    return [(i, ((i // 8 + d) % 4) * 8 + i % 8) for i in range(N_WIDE)]


def y_perm(d):
    return [(i, (i // 8) * 8 + (((i // 2) % 4 + d) % 4) * 2 + i % 2) for i in range(N_WIDE)]


def y_flip(m):
    return [(i, i ^ (2 * m)) for i in range(N_WIDE)]


def z_flip(m):
    return [(i, i ^ (8 * m)) for i in range(N_WIDE)]


X_LO = [(i, i ^ 1) for i in range(N_WIDE)]
CORE = [(i, i ^ 1) for i in range(4)]
X_HI = [(i, i ^ 2) for i in range(4)]


def slots_kernel(panel_ref, owner_ref, row_ref, bag_ref, slots_ref, ids_ref, count_ref, onehots):
    depth, samples = owner_ref.shape
    feats = depth // 2
    bag = bag_ref[pl.ds(pl.multiple_of(panel_ref[0] * feats, feats), feats), :]
    bag = jnp.concatenate([bag[k // 2 : k // 2 + 1, :] for k in range(depth)], axis=0)
    live = (lax.broadcasted_iota(jnp.int32, (depth, samples), 0) & 1) < bag
    owner = jnp.where(live, owner_ref[...], N_WIDE)
    for t in range(N_WIDE):
        onehots[t * depth : (t + 1) * depth, :] = jnp.where(owner == t, 1.0, 0.0).astype(BF16)

    size = N_WIDE * depth
    first = lax.broadcasted_iota(jnp.int32, (samples, samples), 0)
    second = lax.broadcasted_iota(jnp.int32, (samples, samples), 1)
    before = jnp.where(first < second, 1.0, 0.0).astype(BF16)
    within = jnp.dot(onehots[...], before, preferred_element_type=F32)
    in_row = jnp.dot(onehots[...], jnp.ones((samples, E), BF16), preferred_element_type=F32)
    top = jnp.floor(in_row * (1.0 / 16.0))
    low = (in_row - 16.0 * top).astype(BF16)
    top = top.astype(BF16)
    r = lax.broadcasted_iota(jnp.int32, (size, size), 0)
    c = lax.broadcasted_iota(jnp.int32, (size, size), 1)
    shift = depth.bit_length() - 1
    earlier = jnp.where((r >> shift == c >> shift) & (c < r), 1.0, 0.0).astype(BF16)
    rows_before = 16.0 * jnp.dot(earlier, top, preferred_element_type=F32) + jnp.dot(
        earlier, low, preferred_element_type=F32
    )
    t_rows = lax.broadcasted_iota(jnp.int32, (N_WIDE, size), 0)
    t_cols = lax.broadcasted_iota(jnp.int32, (N_WIDE, size), 1)
    members = jnp.where(t_rows == t_cols >> shift, 1.0, 0.0).astype(BF16)
    count_ref[...] = 16.0 * jnp.dot(members, top, preferred_element_type=F32) + jnp.dot(
        members, low, preferred_element_type=F32
    )
    place = jnp.zeros((depth, samples), F32)
    for t in range(N_WIDE):
        at = slice(t * depth, (t + 1) * depth)
        ahead = jnp.concatenate([rows_before[at, :]] * (samples // E), axis=1)
        place = place + jnp.where(owner == t, within[at, :] + ahead, 0.0)
    place = place.astype(jnp.int32)
    slots = jnp.where(live, owner * CAP + place, N_WIDE * CAP)
    for k in range(samples // E):
        slots_ref[k * depth : (k + 1) * depth, :] = slots[:, k * E : (k + 1) * E]

    marked = row_ref[...] + 1
    top = (marked >> 6).astype(F32)
    low = (marked & 63).astype(F32)
    owners = lax.broadcasted_iota(jnp.int32, (N_WIDE, samples), 0)
    places = lax.broadcasted_iota(jnp.int32, (CAP, samples), 0)
    ids = jnp.zeros((2 * N_WIDE, CAP), F32)
    for k in range(depth):
        at = slice(k, k + 1)
        mine = owners == owner[at, :]
        marks = jnp.concatenate([jnp.where(mine, top[at, :], 0.0), jnp.where(mine, low[at, :], 0.0)], axis=0)
        there = jnp.where(places == place[at, :], 1.0, 0.0).astype(BF16)
        ids = ids + lax.dot_general(
            marks.astype(BF16), there, (((1,), (1,)), ((), ())), preferred_element_type=F32
        )
    ids_ref[...] = ids


def entry_slots(panel, owner, row, bag):
    vmem = pl.BlockSpec(memory_space=pltpu.VMEM)
    depth, samples = owner.shape
    return pl.pallas_call(
        slots_kernel,
        out_shape=(
            jax.ShapeDtypeStruct((depth * samples // E, E), jnp.int32),
            jax.ShapeDtypeStruct((2 * N_WIDE, CAP), F32),
            jax.ShapeDtypeStruct((N_WIDE, E), F32),
        ),
        in_specs=[pl.BlockSpec(memory_space=pltpu.SMEM), vmem, vmem, vmem],
        out_specs=(vmem, vmem, vmem),
        scratch_shapes=[pltpu.VMEM((N_WIDE * depth, samples), BF16)],
        compiler_params=pltpu.CompilerParams(vmem_limit_bytes=VMEM_BYTES),
        cost_estimate=LIGHT,
        name="entry_slots",
    )(panel.reshape(1), owner, row, bag)


def place_kernel(
    slots_ref, base_hbm, mate_hbm, far_hbm, ids_ref, count_ref, bias_ref, out_ref, base, mate, far, rows, blocks, sems, sems_in
):
    depth = 16
    dump = N_WIDE * CAP
    loads = [
        pltpu.make_async_copy(src, dst, sems_in.at[k])
        for k, (src, dst) in enumerate(((base_hbm, base), (mate_hbm, mate), (far_hbm, far)))
    ]
    for load in loads:
        load.start()

    def clear(i, _):
        rows[pl.ds(pl.multiple_of(i * 256, 256), 256), :] = jnp.zeros((256, E), F32)
        return 0

    lax.fori_loop(0, dump // 256, clear, 0)
    for load in loads:
        load.wait()

    def place(i, _):
        first = pl.multiple_of(i * 16, 16)
        at = (first // E) * (depth * E) + first % E
        for f in range(8):
            cols = slice(f * E, (f + 1) * E)
            tile = base[pl.ds(first, 16), cols] + (
                mate[pl.ds(first, 16), cols].astype(F32) + far[pl.ds(first, 16), cols].astype(F32)
            )
            for b in range(16):
                row = tile[b : b + 1, :]
                for j in range(2):
                    slot = slots_ref[at + (2 * f + j) * E + b]
                    rows[pl.ds(slot, 1), :] = row
        return 0

    lax.fori_loop(0, base.shape[0] // 16, place, 0)

    bias_top = bias_ref[...].astype(BF16)
    bias_low = (bias_ref[...] - bias_top.astype(F32)).astype(BF16)

    def copy_out(w):
        return pltpu.make_async_copy(blocks.at[w], out_ref.at[w], sems.at[w])

    def narrow_down(w, _):
        blocks[w, :CAP, :] = rows[pl.ds(pl.multiple_of(w * CAP, CAP), CAP), :].astype(BF16)
        top = ids_ref[pl.ds(w, 1), :]
        low = ids_ref[pl.ds(N_WIDE + w, 1), :]
        count = count_ref[pl.ds(w, 1), :]
        count_top = jnp.floor(count * (1.0 / 64.0))
        parts = [top[:, k * E : (k + 1) * E] for k in range(4)] + [low[:, k * E : (k + 1) * E] for k in range(4)]
        ends = [count_top] * 4 + [count - 64.0 * count_top] * 4
        blocks[w, CAP:, :] = jnp.concatenate(
            [
                jnp.concatenate(parts, axis=0).astype(BF16),
                bias_top,
                bias_low,
                jnp.concatenate(ends, axis=0).astype(BF16),
            ],
            axis=0,
        )
        copy_out(w).start()
        return 0

    lax.fori_loop(0, N_WIDE, narrow_down, 0)

    def finish(w, _):
        copy_out(w).wait()
        return 0

    lax.fori_loop(0, N_WIDE, finish, 0)


def place_entries(slots, base, mate, far, ids, counts, bias):
    vmem = pl.BlockSpec(memory_space=pltpu.VMEM)
    hbm = pl.BlockSpec(memory_space=pltpu.HBM)
    return pl.pallas_call(
        place_kernel,
        out_shape=jax.ShapeDtypeStruct((N_WIDE, BLOCK, E), BF16),
        in_specs=[pl.BlockSpec(memory_space=pltpu.SMEM)] + [pl.BlockSpec(memory_space=pl.ANY)] * 3 + [vmem] * 3,
        out_specs=hbm,
        scratch_shapes=[
            pltpu.VMEM(base.shape, F32),
            pltpu.VMEM(base.shape, BF16),
            pltpu.VMEM(base.shape, BF16),
            pltpu.VMEM((N_WIDE * CAP + 8, E), F32),
            pltpu.VMEM((N_WIDE, BLOCK, E), BF16),
            pltpu.SemaphoreType.DMA((N_WIDE,)),
            pltpu.SemaphoreType.DMA((3,)),
        ],
        compiler_params=pltpu.CompilerParams(vmem_limit_bytes=VMEM_BYTES),
        cost_estimate=LIGHT,
        name="place_entries",
    )(slots, base, mate, far, ids, counts, bias)


def sums_kernel(core_ref, recv_ref, keep_ref, send_ref, bias_ref, total, left, right, todo):
    lane_rows = lax.broadcasted_iota(jnp.int32, (LO, E), 0)

    n = 0
    for w in range(N_WIDE):
        ends = recv_ref[w, CAP + 16 :, :].astype(F32)
        count = jnp.max(ends[8:12, :] * 64.0 + ends[12:16, :])
        todo[n] = 2 * w
        n = n + jnp.where(count > 0.0, 1, 0)
        todo[n] = 2 * w + 1
        n = n + jnp.where(count > float(CAP // 2), 1, 0)
    for k in range(12):
        todo[n + k] = -1
    total[...] = jnp.zeros_like(total)
    bias_ref[...] = jnp.sum(
        recv_ref[:, CAP + 8 : CAP + 16, :].astype(F32) + recv_ref[:, CAP + 16 : CAP + 24, :].astype(F32),
        axis=0,
    )

    def build(i, buf):
        for p in range(4):
            item = todo[i * 4 + p]
            w = jnp.maximum(item, 0) // 2
            half = jnp.maximum(item, 0) % 2
            ids = recv_ref[w, CAP : CAP + 16, :].astype(F32)
            row = (ids[0:4, :] * 64.0 + ids[4:8, :]).astype(jnp.int32) - 1
            row = jnp.where(half == 0, row[0:2, :], row[2:4, :])
            row = jnp.where(item < 0, -1, row)
            hi = row >> (LO.bit_length() - 1)
            lo = jnp.where(row < 0, -1, row & (LO - 1))
            hi_col = jnp.transpose(jnp.concatenate([hi] * 4, axis=0).astype(F32), (1, 0))
            for j in range(2):
                at = (2 * p + j) * E
                left[buf, :, at : at + E] = jnp.where(lane_rows == lo[j : j + 1, :], 1.0, 0.0).astype(BF16)
                v = recv_ref[w, pl.ds(pl.multiple_of(half * (CAP // 2), CAP // 2) + j * E, E), :]
                own = jnp.broadcast_to(hi_col[:, j : j + 1], (E, E)).astype(BF16)
                for h in range(HI):
                    right[buf, at : at + E, h * E : (h + 1) * E] = jnp.where(own == BF16(h), v, BF16(0))

    build(0, 0)

    def step(i, _):
        for b in range(2):
            build(2 * i + b + 1, 1 - b)
            total[...] += jnp.dot(left[b], right[b], preferred_element_type=F32)
        return 0

    lax.fori_loop(0, (n + 7) // 8, step, 0)
    for k in range(HI // 2):
        for out_ref, half in ((keep_ref, core_ref[0]), (send_ref, 1 - core_ref[0])):
            at = pl.multiple_of((half * (HI // 2) + k) * E, E)
            out_ref[k * LO : (k + 1) * LO, :] = total[:, pl.ds(at, E)].astype(BF16)


def owned_sums(core, recv):
    vmem = pl.BlockSpec(memory_space=pltpu.VMEM)
    return pl.pallas_call(
        sums_kernel,
        out_shape=[jax.ShapeDtypeStruct((N_ROWS // 2, E), BF16)] * 2 + [jax.ShapeDtypeStruct((8, E), F32)],
        in_specs=[pl.BlockSpec(memory_space=pltpu.SMEM), vmem],
        out_specs=[vmem] * 3,
        scratch_shapes=[
            pltpu.VMEM((LO, HI * E), F32),
            pltpu.VMEM((2, LO, 2 * CAP), BF16),
            pltpu.VMEM((2, 2 * CAP, HI * E), BF16),
            pltpu.SMEM((2 * N_WIDE + 16,), jnp.int32),
        ],
        compiler_params=pltpu.CompilerParams(vmem_limit_bytes=VMEM_BYTES),
        cost_estimate=LIGHT,
        name="owned_sums",
    )(core, recv)


def summed(own, others):
    total = own.astype(F32)
    for other in others:
        total = total + other.astype(F32)
    return total


def own_chunk(a):
    return pl.multiple_of(a * 1024, 1024)


def ring_term(route, turned, embedded, z, y, d):
    part = turned[route * 512 : (route + 1) * 512, :]
    if route == 0:
        rows = embedded[:, pl.ds(own_chunk((z + d) % 4), 1024)]
        return jnp.dot(part, rows, preferred_element_type=F32)
    start = ((y + d) % 4) * 256
    blocks = [embedded[:, pl.ds(pl.multiple_of(k * 1024 + start, 256), 256)] for k in range(4)]
    return jnp.concatenate([jnp.dot(part, rows, preferred_element_type=F32) for rows in blocks], axis=1)


def sent_kernel(n_ref, z_ref, y_ref, cot_hbm, embedded_hbm, weight_hbm, *refs):
    parts_hbm, first_hbm, second_hbm, (scaled_hbm, turned_hbm, bias_ref) = refs[:3], refs[3:7], refs[7:11], refs[11:14]
    cot, embedded, weight, scaled, turned, parts, first, second, sems, sems_out = refs[14:]
    n, z, y = n_ref[0], z_ref[0], y_ref[0]

    def columns(q):
        at = pl.ds(own_chunk(n ^ q), 1024)
        return pltpu.make_async_copy(embedded_hbm.at[:, at], embedded.at[:, at], sems.at[q])

    def rows(q):
        at = pl.ds(own_chunk(n ^ q), 1024)
        return pltpu.make_async_copy(weight_hbm.at[at, :], weight.at[q - 1], sems.at[3 + q])

    outs = [(parts.at[q], parts_hbm[q]) for q in range(3)]
    outs += [(first.at[q], first_hbm[q]) for q in range(4)] + [(second.at[q], second_hbm[q]) for q in range(4)]
    outs += [(scaled, scaled_hbm), (turned, turned_hbm)]
    outs = [pltpu.make_async_copy(src, dst, sems_out.at[k]) for k, (src, dst) in enumerate(outs)]

    get_cot = pltpu.make_async_copy(cot_hbm, cot, sems.at[7])
    get_cot.start()
    columns(0).start()
    rows(3).start()
    get_cot.wait()
    columns(0).wait()
    for q in (1, 2):
        rows(q).start()
    for q in (1, 2, 3):
        columns(q).start()
    grads = (cot[...].astype(F32) * embedded[:, pl.ds(own_chunk(n), 1024)].astype(F32)).astype(BF16)
    scaled[...] = grads
    turned[...] = jnp.transpose(grads, (1, 0))
    sums = jnp.sum(grads.astype(F32), axis=0, keepdims=True)
    bias_ref[...] = jnp.concatenate([sums[:, k * E : (k + 1) * E] for k in range(8)], axis=0)
    outs[11].start()
    outs[12].start()
    for k, q in enumerate((3, 1, 2)):
        rows(q).wait()
        part = lax.dot_general(scaled[...], weight[q - 1], NT, preferred_element_type=F32)
        parts[k] = part.astype(BF16)
        outs[k].start()
    for q in (1, 2, 3):
        columns(q).wait()
    for route in range(2):
        term = ring_term(route, turned, embedded, z, y, 2).astype(BF16)
        for way in range(2):
            first[2 * route + way, :256, :] = term[way * 256 : (way + 1) * 256, :]
        for way in range(2):
            q = 2 * route + way
            term = ring_term(route, turned, embedded, z, y, 3 if way else 1).astype(BF16)
            first[q, 256:, :] = term[(1 - way) * 256 : (2 - way) * 256, :]
            second[q] = term[way * 256 : (way + 1) * 256, :]
            outs[3 + q].start()
            outs[7 + q].start()
    for copy in outs:
        copy.wait()


def sent_terms(n, z, y, cotangent, embedded, weight):
    hbm = pl.BlockSpec(memory_space=pltpu.HBM)
    smem = pl.BlockSpec(memory_space=pltpu.SMEM)
    samples, width = cotangent.shape
    shape = jax.ShapeDtypeStruct
    full, half = shape((samples, width), BF16), shape((256, 1024), BF16)
    results = pl.pallas_call(
        sent_kernel,
        out_shape=[full] * 3 + [shape((512, 1024), BF16)] * 4 + [half] * 4
        + [full, shape((width, samples), BF16), shape((8, E), F32)],
        in_specs=[smem] * 3 + [hbm] * 3,
        out_specs=[hbm] * 13 + [pl.BlockSpec(memory_space=pltpu.VMEM)],
        scratch_shapes=[
            pltpu.VMEM(cotangent.shape, BF16),
            pltpu.VMEM(embedded.shape, BF16),
            pltpu.VMEM((3, 1024, 1024), BF16),
            pltpu.VMEM((samples, width), BF16),
            pltpu.VMEM((width, samples), BF16),
            pltpu.VMEM((3, samples, width), BF16),
            pltpu.VMEM((4, 512, 1024), BF16),
            pltpu.VMEM((4, 256, 1024), BF16),
            pltpu.SemaphoreType.DMA((8,)),
            pltpu.SemaphoreType.DMA((13,)),
        ],
        compiler_params=pltpu.CompilerParams(vmem_limit_bytes=VMEM_BYTES),
        cost_estimate=LIGHT,
        name="sent_terms",
    )(n, z, y, cotangent, embedded, weight)
    return results[:3], results[3:7], results[7:11], *results[11:]


def pass_kernel(*refs):
    passed_hbm, mine_hbm, sent_hbm, (passed, mine, sent, sems, sems_out) = refs[:4], refs[4:8], refs[8:12], refs[12:]
    loads, outs = [], []
    for q in range(4):
        loads.append(pltpu.make_async_copy(passed_hbm[q].at[pl.ds(0, 256), :], passed.at[q], sems.at[2 * q]))
        loads.append(pltpu.make_async_copy(mine_hbm[q], mine.at[q], sems.at[2 * q + 1]))
        outs.append(pltpu.make_async_copy(sent.at[q], sent_hbm[q], sems_out.at[q]))
    for load in loads:
        load.start()
    for q in range(4):
        loads[2 * q].wait()
        loads[2 * q + 1].wait()
        sent[q] = (passed[q].astype(F32) + mine[q].astype(F32)).astype(BF16)
        outs[q].start()
    for copy in outs:
        copy.wait()


def passed_on(first, second):
    hbm = pl.BlockSpec(memory_space=pltpu.HBM)
    return pl.pallas_call(
        pass_kernel,
        out_shape=[jax.ShapeDtypeStruct((256, 1024), BF16)] * 4,
        in_specs=[pl.BlockSpec(memory_space=pl.ANY)] * 8,
        out_specs=[hbm] * 4,
        scratch_shapes=[
            pltpu.VMEM((4, 256, 1024), BF16),
            pltpu.VMEM((4, 256, 1024), BF16),
            pltpu.VMEM((4, 256, 1024), BF16),
            pltpu.SemaphoreType.DMA((8,)),
            pltpu.SemaphoreType.DMA((4,)),
        ],
        compiler_params=pltpu.CompilerParams(vmem_limit_bytes=VMEM_BYTES),
        cost_estimate=LIGHT,
        name="passed_on",
    )(*first, *second)


def kept_kernel(n_ref, cot_hbm, embedded_hbm, weight_hbm, bias_ref, scaled_hbm, base_ref, *scratch):
    cot, embedded, weight, scaled, cross, sems = scratch
    n = n_ref[0]

    def columns(q):
        at = pl.ds(own_chunk(n ^ q), 1024)
        return pltpu.make_async_copy(embedded_hbm.at[:, at], embedded.at[:, at], sems.at[q])

    def rows(q):
        at = pl.ds(own_chunk(n ^ q), 1024)
        return pltpu.make_async_copy(weight_hbm.at[at, :], weight.at[q], sems.at[4 + q])

    get_scaled = pltpu.make_async_copy(scaled_hbm, scaled, sems.at[8])
    get_cot = pltpu.make_async_copy(cot_hbm, cot, sems.at[9])
    rows(0).start()
    columns(0).start()
    get_scaled.start()
    rows(0).wait()
    columns(0).wait()
    for q in (1, 2, 3):
        rows(q).start()
        columns(q).start()
    get_cot.start()
    cross[...] = jnp.dot(embedded[:, pl.ds(own_chunk(n), 1024)], weight[0], preferred_element_type=F32)
    get_scaled.wait()
    base_ref[...] = lax.dot_general(scaled[...], weight[0], NT, preferred_element_type=F32)
    for q in (1, 2):
        rows(q).wait()
        columns(q).wait()
        cross[...] += jnp.dot(embedded[:, pl.ds(own_chunk(n ^ q), 1024)], weight[q], preferred_element_type=F32)
    rows(3).wait()
    columns(3).wait()
    get_cot.wait()
    grad = cot[...].astype(F32)
    last = jnp.dot(embedded[:, pl.ds(own_chunk(n ^ 3), 1024)], weight[3], preferred_element_type=F32)
    base_ref[...] += grad + grad * (cross[...] + last + bias_ref[...])


def kept_terms(n, cotangent, embedded, weight, bias, scaled):
    hbm = pl.BlockSpec(memory_space=pltpu.HBM)
    vmem = pl.BlockSpec(memory_space=pltpu.VMEM)
    samples, width = cotangent.shape
    return pl.pallas_call(
        kept_kernel,
        out_shape=jax.ShapeDtypeStruct((samples, width), F32),
        in_specs=[pl.BlockSpec(memory_space=pltpu.SMEM)] + [hbm] * 3 + [vmem, hbm],
        out_specs=vmem,
        scratch_shapes=[
            pltpu.VMEM(cotangent.shape, BF16),
            pltpu.VMEM(embedded.shape, BF16),
            pltpu.VMEM((4, 1024, 1024), BF16),
            pltpu.VMEM((samples, width), BF16),
            pltpu.VMEM((samples, width), F32),
            pltpu.SemaphoreType.DMA((10,)),
        ],
        compiler_params=pltpu.CompilerParams(vmem_limit_bytes=VMEM_BYTES),
        cost_estimate=LIGHT,
        name="kept_terms",
    )(n, cotangent, embedded, weight, bias.reshape(1, -1), scaled)


def own_kernel(z_ref, y_ref, embedded_hbm, turned_hbm, *refs):
    got_hbm, results, (embedded, turned, got, sems) = refs[:8], refs[8:12], refs[12:]
    z, y = z_ref[0], y_ref[0]
    loads = [(embedded_hbm, embedded), (turned_hbm, turned)]
    loads += [(got_hbm[k].at[pl.ds(256, 256), :], got.at[k]) for k in range(4)]
    loads += [(got_hbm[k], got.at[k]) for k in range(4, 8)]
    loads = [pltpu.make_async_copy(src, dst, sems.at[k]) for k, (src, dst) in enumerate(loads)]
    for load in loads:
        load.start()
    for load in loads:
        load.wait()
    for route, place in ((0, y), (1, z)):
        term = ring_term(route, turned, embedded, z, y, 0)
        up, down = 2 * route, 2 * route + 1
        total = jnp.concatenate(
            [
                term[:256, :] + got[4 + up].astype(F32) + got[down].astype(F32),
                term[256:, :] + got[4 + down].astype(F32) + got[up].astype(F32),
            ],
            axis=0,
        ).astype(BF16)
        high = place >= 2
        results[2 * route][...] = jnp.where(high, total[:, 512:], total[:, :512])
        results[2 * route + 1][...] = jnp.where(high, total[:, :512], total[:, 512:])


def own_terms(z, y, embedded, turned, first, second):
    hbm = pl.BlockSpec(memory_space=pltpu.HBM)
    vmem = pl.BlockSpec(memory_space=pltpu.VMEM)
    return pl.pallas_call(
        own_kernel,
        out_shape=[jax.ShapeDtypeStruct((512, 512), BF16)] * 4,
        in_specs=[pl.BlockSpec(memory_space=pltpu.SMEM)] * 2 + [hbm] + [pl.BlockSpec(memory_space=pl.ANY)] * 9,
        out_specs=[vmem] * 4,
        scratch_shapes=[
            pltpu.VMEM(embedded.shape, BF16),
            pltpu.VMEM(turned.shape, BF16),
            pltpu.VMEM((8, 256, 1024), BF16),
            pltpu.SemaphoreType.DMA((10,)),
        ],
        compiler_params=pltpu.CompilerParams(vmem_limit_bytes=VMEM_BYTES),
        cost_estimate=LIGHT,
        name="own_terms",
    )(z, y, embedded, turned, *first, *second)


def halves_of(array, bit, axis):
    size = array.shape[axis] // 2
    return (
        lax.dynamic_slice_in_dim(array, bit * size, size, axis),
        lax.dynamic_slice_in_dim(array, (1 - bit) * size, size, axis),
    )


def body(
    embedded,
    cotangent,
    cross_weight,
    cross_bias,
    bag_size,
    row_owner,
    row_id,
    emb_table,
    adagrad_state,
):
    panel = lax.axis_index("narrow")
    wide = lax.axis_index("wide")
    z, y, x_lo = wide // 8, (wide // 2) % 4, wide % 2
    core = panel % 2
    batch_rows = cotangent.shape[0]
    norm_factor = 1.0 / math.sqrt(batch_rows * N_WIDE)

    at = (panel.reshape(1), z.reshape(1), y.reshape(1))

    parts, first, second, scaled, turned, bias_part = sent_terms(*at, cotangent, embedded, cross_weight)
    from_mate_far = lax.ppermute(parts[0], "narrow", CORE)
    from_mate = lax.ppermute(parts[1], "narrow", CORE)
    ways = [z_perm(1), z_perm(3), y_perm(1), y_perm(3)]
    first = [lax.ppermute(first[q], "wide", ways[q]) for q in range(4)]
    chip_far = (parts[2].astype(F32) + from_mate_far.astype(F32)).astype(BF16)
    chip_far, scaled, from_mate = lax.optimization_barrier((chip_far, scaled, from_mate))
    far = lax.ppermute(chip_far, "narrow", X_HI)

    base = kept_terms(at[0], cotangent, embedded, cross_weight, cross_bias, scaled)
    row_owner, row_id, bag_size, base = lax.optimization_barrier((row_owner, row_id, bag_size, base))
    slots, ids, counts = entry_slots(
        panel, row_owner.reshape(row_owner.shape[1:3]).T, row_id.reshape(row_id.shape[1:]).T, bag_size.T
    )
    slots, ids, counts, *first = lax.optimization_barrier((slots, ids, counts, *first))
    second = passed_on(first, second)
    slots, far, *second = lax.optimization_barrier((slots, far, *second))
    second = [lax.ppermute(second[q], "wide", ways[q]) for q in range(4)]

    payload = place_entries(slots.reshape(-1), base, from_mate, far, ids, counts, bias_part)
    payload, *second = lax.optimization_barrier((payload, *second))
    recv = lax.all_to_all(payload, "wide", split_axis=0, concat_axis=0, tiled=True)

    keep_y, send_y, keep_z, send_z = own_terms(at[1], at[2], embedded, turned, first, second)
    kept = [
        summed(keep_y, [lax.ppermute(send_y, "wide", y_flip(2))]),
        summed(keep_z, [lax.ppermute(send_z, "wide", z_flip(2))]),
    ]
    quarters = []
    for total, place in zip(kept, (y, z)):
        keep, send = halves_of(total, place % 2, 1)
        quarters.append((keep.astype(BF16), send.astype(BF16)))
    recv, *sends = lax.optimization_barrier((recv, quarters[0][1], quarters[1][1]))
    got = [lax.ppermute(sends[0], "wide", y_flip(1)), lax.ppermute(sends[1], "wide", z_flip(1))]
    keep, send, bias_sums = owned_sums(core.reshape(1), recv)
    keep, send, *got = lax.optimization_barrier((keep, send, *got))
    chip = summed(keep, [lax.ppermute(send, "narrow", CORE)]).astype(BF16)
    pair = jnp.concatenate([summed(quarters[0][0], got[:1]), summed(quarters[1][0], got[1:])], axis=0).astype(BF16)
    x_keep, x_send = halves_of(pair, x_lo, 1)
    other_chip, x_send = lax.optimization_barrier((lax.ppermute(chip, "narrow", X_HI), x_send))
    weight_grad = summed(x_keep, [lax.ppermute(x_send, "wide", X_LO)]).T * norm_factor

    bias_grad = bias_sums.reshape(-1) * norm_factor
    mine = summed(chip, [other_chip])
    mate = lax.ppermute(mine, "narrow", CORE)
    row_grad = jnp.concatenate([jnp.where(core == 0, mine, mate), jnp.where(core == 0, mate, mine)], axis=0)
    new_state = adagrad_state + jnp.mean(row_grad * row_grad, axis=1)
    new_table = emb_table - LEARN_RATE * row_grad / jnp.sqrt(new_state)[:, None]
    return (weight_grad, bias_grad, new_table, new_state)


def solution(mesh):
    in_specs = (
        P("wide", None),
        P("wide", "narrow"),
        P(None, "narrow"),
        P("narrow"),
        P("wide", None),
        P("narrow", "wide", None, None),
        P("narrow", "wide", None),
        P("wide", None),
        P("wide"),
    )
    out_specs = (P("wide", "narrow"), P("narrow"), P("wide", None), P("wide"))
    return jax.shard_map(body, mesh=mesh, in_specs=in_specs, out_specs=out_specs, check_vma=False)
```

```python
import math

import jax
import jax.numpy as jnp
from jax import lax
from jax.experimental import pallas as pl
from jax.experimental.pallas import tpu as pltpu
from jax.sharding import PartitionSpec as P

LEARN_RATE = 0.3
E = 128
N_WIDE = 32
CAP = 512
TAIL = 16
BLOCK = CAP + TAIL
N_ROWS = 2048
HI = 4
LO = N_ROWS // HI
F32 = jnp.float32
BF16 = jnp.bfloat16
LIGHT = pl.CostEstimate(flops=1, bytes_accessed=1, transcendentals=0)
VMEM_BYTES = 56 << 20
NT = (((1,), (1,)), ((), ()))


def z_perm(d):
    return [(i, ((i // 8 + d) % 4) * 8 + i % 8) for i in range(N_WIDE)]


def y_perm(d):
    return [(i, (i // 8) * 8 + (((i // 2) % 4 + d) % 4) * 2 + i % 2) for i in range(N_WIDE)]


def y_flip(m):
    return [(i, i ^ (2 * m)) for i in range(N_WIDE)]


def z_flip(m):
    return [(i, i ^ (8 * m)) for i in range(N_WIDE)]


X_LO = [(i, i ^ 1) for i in range(N_WIDE)]
CORE = [(i, i ^ 1) for i in range(4)]
X_HI = [(i, i ^ 2) for i in range(4)]


def find_slots(panel, owner_ref, row_ref, bag_ref, slots_ref, ids_ref, onehots):
    depth, samples = owner_ref.shape
    feats = depth // 2
    bag = bag_ref[pl.ds(pl.multiple_of(panel * feats, feats), feats), :]
    bag = jnp.concatenate([bag[k // 2 : k // 2 + 1, :] for k in range(depth)], axis=0)
    live = (lax.broadcasted_iota(jnp.int32, (depth, samples), 0) & 1) < bag
    owner = jnp.where(live, owner_ref[...], N_WIDE)
    for t in range(N_WIDE):
        onehots[t * depth : (t + 1) * depth, :] = jnp.where(owner == t, 1.0, 0.0).astype(BF16)

    size = N_WIDE * depth
    first = lax.broadcasted_iota(jnp.int32, (samples, samples), 0)
    second = lax.broadcasted_iota(jnp.int32, (samples, samples), 1)
    before = jnp.where(first < second, 1.0, 0.0).astype(BF16)
    within = jnp.dot(onehots[...], before, preferred_element_type=F32)
    in_row = jnp.dot(onehots[...], jnp.ones((samples, E), BF16), preferred_element_type=F32)
    top = jnp.floor(in_row * (1.0 / 16.0))
    low = (in_row - 16.0 * top).astype(BF16)
    top = top.astype(BF16)
    r = lax.broadcasted_iota(jnp.int32, (size, size), 0)
    c = lax.broadcasted_iota(jnp.int32, (size, size), 1)
    shift = depth.bit_length() - 1
    earlier = jnp.where((r >> shift == c >> shift) & (c < r), 1.0, 0.0).astype(BF16)
    rows_before = 16.0 * jnp.dot(earlier, top, preferred_element_type=F32) + jnp.dot(
        earlier, low, preferred_element_type=F32
    )
    place = jnp.zeros((depth, samples), F32)
    for t in range(N_WIDE):
        at = slice(t * depth, (t + 1) * depth)
        ahead = jnp.concatenate([rows_before[at, :]] * (samples // E), axis=1)
        place = place + jnp.where(owner == t, within[at, :] + ahead, 0.0)
    place = place.astype(jnp.int32)
    slots = jnp.where(live, owner * CAP + place, N_WIDE * CAP)
    for k in range(samples // E):
        slots_ref[k * depth : (k + 1) * depth, :] = slots[:, k * E : (k + 1) * E]

    marked = row_ref[...] + 1
    top = (marked >> 6).astype(F32)
    low = (marked & 63).astype(F32)
    owners = lax.broadcasted_iota(jnp.int32, (N_WIDE, samples), 0)
    places = lax.broadcasted_iota(jnp.int32, (CAP, samples), 0)
    ids = jnp.zeros((2 * N_WIDE, CAP), F32)
    for k in range(depth):
        at = slice(k, k + 1)
        mine = owners == owner[at, :]
        marks = jnp.concatenate([jnp.where(mine, top[at, :], 0.0), jnp.where(mine, low[at, :], 0.0)], axis=0)
        there = jnp.where(places == place[at, :], 1.0, 0.0).astype(BF16)
        ids = ids + lax.dot_general(
            marks.astype(BF16), there, (((1,), (1,)), ((), ())), preferred_element_type=F32
        )
    ids_ref[...] = ids


def place_kernel(
    slots_ref, base_hbm, mate_hbm, far_hbm, ids_ref, bias_ref, out_ref, base, mate, far, rows, blocks, sems, sems_in
):
    depth = 16
    dump = N_WIDE * CAP
    loads = [
        pltpu.make_async_copy(src, dst, sems_in.at[k])
        for k, (src, dst) in enumerate(((base_hbm, base), (mate_hbm, mate), (far_hbm, far)))
    ]
    for load in loads:
        load.start()

    def clear(i, _):
        rows[pl.ds(pl.multiple_of(i * 256, 256), 256), :] = jnp.zeros((256, E), F32)
        return 0

    lax.fori_loop(0, dump // 256, clear, 0)
    for load in loads:
        load.wait()

    def place(i, _):
        first = pl.multiple_of(i * 16, 16)
        at = (first // E) * (depth * E) + first % E
        for f in range(8):
            cols = slice(f * E, (f + 1) * E)
            tile = base[pl.ds(first, 16), cols] + (
                mate[pl.ds(first, 16), cols].astype(F32) + far[pl.ds(first, 16), cols].astype(F32)
            )
            for b in range(16):
                row = tile[b : b + 1, :]
                for j in range(2):
                    slot = slots_ref[at + (2 * f + j) * E + b]
                    rows[pl.ds(slot, 1), :] = row
        return 0

    lax.fori_loop(0, base.shape[0] // 16, place, 0)

    bias = bias_ref[...]

    def copy_out(w):
        return pltpu.make_async_copy(blocks.at[w], out_ref.at[w], sems.at[w])

    def narrow_down(w, _):
        blocks[w, :CAP, :] = rows[pl.ds(pl.multiple_of(w * CAP, CAP), CAP), :].astype(BF16)
        top = ids_ref[pl.ds(w, 1), :]
        low = ids_ref[pl.ds(N_WIDE + w, 1), :]
        parts = [top[:, k * E : (k + 1) * E] for k in range(4)] + [low[:, k * E : (k + 1) * E] for k in range(4)]
        blocks[w, CAP:, :] = jnp.concatenate(parts + [bias], axis=0).astype(BF16)
        copy_out(w).start()
        return 0

    lax.fori_loop(0, N_WIDE, narrow_down, 0)

    def finish(w, _):
        copy_out(w).wait()
        return 0

    lax.fori_loop(0, N_WIDE, finish, 0)


def place_entries(slots, base, mate, far, ids, bias):
    vmem = pl.BlockSpec(memory_space=pltpu.VMEM)
    hbm = pl.BlockSpec(memory_space=pltpu.HBM)
    return pl.pallas_call(
        place_kernel,
        out_shape=jax.ShapeDtypeStruct((N_WIDE, BLOCK, E), BF16),
        in_specs=[pl.BlockSpec(memory_space=pltpu.SMEM)] + [pl.BlockSpec(memory_space=pl.ANY)] * 3 + [vmem] * 2,
        out_specs=hbm,
        scratch_shapes=[
            pltpu.VMEM(base.shape, F32),
            pltpu.VMEM(base.shape, BF16),
            pltpu.VMEM(base.shape, BF16),
            pltpu.VMEM((N_WIDE * CAP + 8, E), F32),
            pltpu.VMEM((N_WIDE, BLOCK, E), BF16),
            pltpu.SemaphoreType.DMA((N_WIDE,)),
            pltpu.SemaphoreType.DMA((3,)),
        ],
        compiler_params=pltpu.CompilerParams(vmem_limit_bytes=VMEM_BYTES),
        cost_estimate=LIGHT,
        name="place_entries",
    )(slots, base, mate, far, ids, bias)


def sums_kernel(core_ref, recv_ref, keep_ref, send_ref, bias_ref, total, left, right, todo):
    lane_rows = lax.broadcasted_iota(jnp.int32, (LO, E), 0)

    n = 0
    for w in range(N_WIDE):
        ids = recv_ref[w, CAP:, :].astype(F32)
        ids = ids[0:4, :] + ids[4:8, :]
        halves = jnp.max(jnp.where(ids[2:3, :] > 0.0, 2.0, jnp.where(ids[0:1, :] > 0.0, 1.0, 0.0)))
        todo[n] = 2 * w
        n = n + jnp.where(halves > 0.5, 1, 0)
        todo[n] = 2 * w + 1
        n = n + jnp.where(halves > 1.5, 1, 0)
    for k in range(12):
        todo[n + k] = -1
    total[...] = jnp.zeros_like(total)
    bias_ref[...] = jnp.sum(recv_ref[:, CAP + 8 : CAP + 16, :].astype(F32), axis=0)

    def build(i, buf):
        for p in range(4):
            item = todo[i * 4 + p]
            w = jnp.maximum(item, 0) // 2
            half = jnp.maximum(item, 0) % 2
            ids = recv_ref[w, CAP : CAP + 16, :].astype(F32)
            row = (ids[0:4, :] * 64.0 + ids[4:8, :]).astype(jnp.int32) - 1
            row = jnp.where(half == 0, row[0:2, :], row[2:4, :])
            row = jnp.where(item < 0, -1, row)
            hi = row >> (LO.bit_length() - 1)
            lo = jnp.where(row < 0, -1, row & (LO - 1))
            hi_col = jnp.transpose(jnp.concatenate([hi] * 4, axis=0).astype(F32), (1, 0))
            for j in range(2):
                at = (2 * p + j) * E
                left[buf, :, at : at + E] = jnp.where(lane_rows == lo[j : j + 1, :], 1.0, 0.0).astype(BF16)
                v = recv_ref[w, pl.ds(pl.multiple_of(half * (CAP // 2), CAP // 2) + j * E, E), :]
                own = jnp.broadcast_to(hi_col[:, j : j + 1], (E, E)).astype(BF16)
                for h in range(HI):
                    right[buf, at : at + E, h * E : (h + 1) * E] = jnp.where(own == BF16(h), v, BF16(0))

    build(0, 0)

    def step(i, _):
        for b in range(2):
            build(2 * i + b + 1, 1 - b)
            total[...] += jnp.dot(left[b], right[b], preferred_element_type=F32)
        return 0

    lax.fori_loop(0, (n + 7) // 8, step, 0)
    for k in range(HI // 2):
        for out_ref, half in ((keep_ref, core_ref[0]), (send_ref, 1 - core_ref[0])):
            at = pl.multiple_of((half * (HI // 2) + k) * E, E)
            out_ref[k * LO : (k + 1) * LO, :] = total[:, pl.ds(at, E)].astype(BF16)


def owned_sums(core, recv):
    vmem = pl.BlockSpec(memory_space=pltpu.VMEM)
    return pl.pallas_call(
        sums_kernel,
        out_shape=[jax.ShapeDtypeStruct((N_ROWS // 2, E), BF16)] * 2 + [jax.ShapeDtypeStruct((8, E), F32)],
        in_specs=[pl.BlockSpec(memory_space=pltpu.SMEM), vmem],
        out_specs=[vmem] * 3,
        scratch_shapes=[
            pltpu.VMEM((LO, HI * E), F32),
            pltpu.VMEM((2, LO, 2 * CAP), BF16),
            pltpu.VMEM((2, 2 * CAP, HI * E), BF16),
            pltpu.SMEM((2 * N_WIDE + 16,), jnp.int32),
        ],
        compiler_params=pltpu.CompilerParams(vmem_limit_bytes=VMEM_BYTES),
        cost_estimate=LIGHT,
        name="owned_sums",
    )(core, recv)


def summed(own, others):
    total = own.astype(F32)
    for other in others:
        total = total + other.astype(F32)
    return total


def own_chunk(a):
    return pl.multiple_of(a * 1024, 1024)


def ring_term(route, turned, embedded, z, y, d):
    part = turned[route * 512 : (route + 1) * 512, :]
    if route == 0:
        rows = embedded[:, pl.ds(own_chunk((z + d) % 4), 1024)]
        return jnp.dot(part, rows, preferred_element_type=F32)
    start = ((y + d) % 4) * 256
    blocks = [embedded[:, pl.ds(pl.multiple_of(k * 1024 + start, 256), 256)] for k in range(4)]
    return jnp.concatenate([jnp.dot(part, rows, preferred_element_type=F32) for rows in blocks], axis=1)


def sent_kernel(n_ref, z_ref, y_ref, cot_hbm, embedded_hbm, weight_hbm, *refs):
    parts_hbm, first_hbm, second_hbm, (scaled_hbm, turned_hbm, bias_ref) = refs[:3], refs[3:7], refs[7:11], refs[11:14]
    cot, embedded, weight, scaled, turned, parts, first, second, sems, sems_out = refs[14:]
    n, z, y = n_ref[0], z_ref[0], y_ref[0]

    def columns(q):
        at = pl.ds(own_chunk(n ^ q), 1024)
        return pltpu.make_async_copy(embedded_hbm.at[:, at], embedded.at[:, at], sems.at[q])

    def rows(q):
        at = pl.ds(own_chunk(n ^ q), 1024)
        return pltpu.make_async_copy(weight_hbm.at[at, :], weight.at[q - 1], sems.at[3 + q])

    outs = [(parts.at[q], parts_hbm[q]) for q in range(3)]
    outs += [(first.at[q], first_hbm[q]) for q in range(4)] + [(second.at[q], second_hbm[q]) for q in range(4)]
    outs += [(scaled, scaled_hbm), (turned, turned_hbm)]
    outs = [pltpu.make_async_copy(src, dst, sems_out.at[k]) for k, (src, dst) in enumerate(outs)]

    get_cot = pltpu.make_async_copy(cot_hbm, cot, sems.at[7])
    get_cot.start()
    columns(0).start()
    rows(3).start()
    get_cot.wait()
    columns(0).wait()
    for q in (1, 2):
        rows(q).start()
    for q in (1, 2, 3):
        columns(q).start()
    grads = (cot[...].astype(F32) * embedded[:, pl.ds(own_chunk(n), 1024)].astype(F32)).astype(BF16)
    scaled[...] = grads
    turned[...] = jnp.transpose(grads, (1, 0))
    sums = jnp.sum(grads.astype(F32), axis=0, keepdims=True)
    bias_ref[...] = jnp.concatenate([sums[:, k * E : (k + 1) * E] for k in range(8)], axis=0)
    outs[11].start()
    outs[12].start()
    for k, q in enumerate((3, 1, 2)):
        rows(q).wait()
        part = lax.dot_general(scaled[...], weight[q - 1], NT, preferred_element_type=F32)
        parts[k] = part.astype(BF16)
        outs[k].start()
    for q in (1, 2, 3):
        columns(q).wait()
    for route in range(2):
        term = ring_term(route, turned, embedded, z, y, 2).astype(BF16)
        for way in range(2):
            first[2 * route + way, :256, :] = term[way * 256 : (way + 1) * 256, :]
        for way in range(2):
            q = 2 * route + way
            term = ring_term(route, turned, embedded, z, y, 3 if way else 1).astype(BF16)
            first[q, 256:, :] = term[(1 - way) * 256 : (2 - way) * 256, :]
            second[q] = term[way * 256 : (way + 1) * 256, :]
            outs[3 + q].start()
            outs[7 + q].start()
    for copy in outs:
        copy.wait()


def sent_terms(n, z, y, cotangent, embedded, weight):
    hbm = pl.BlockSpec(memory_space=pltpu.HBM)
    smem = pl.BlockSpec(memory_space=pltpu.SMEM)
    samples, width = cotangent.shape
    shape = jax.ShapeDtypeStruct
    full, half = shape((samples, width), BF16), shape((256, 1024), BF16)
    results = pl.pallas_call(
        sent_kernel,
        out_shape=[full] * 3 + [shape((512, 1024), BF16)] * 4 + [half] * 4
        + [full, shape((width, samples), BF16), shape((8, E), F32)],
        in_specs=[smem] * 3 + [hbm] * 3,
        out_specs=[hbm] * 13 + [pl.BlockSpec(memory_space=pltpu.VMEM)],
        scratch_shapes=[
            pltpu.VMEM(cotangent.shape, BF16),
            pltpu.VMEM(embedded.shape, BF16),
            pltpu.VMEM((3, 1024, 1024), BF16),
            pltpu.VMEM((samples, width), BF16),
            pltpu.VMEM((width, samples), BF16),
            pltpu.VMEM((3, samples, width), BF16),
            pltpu.VMEM((4, 512, 1024), BF16),
            pltpu.VMEM((4, 256, 1024), BF16),
            pltpu.SemaphoreType.DMA((8,)),
            pltpu.SemaphoreType.DMA((13,)),
        ],
        compiler_params=pltpu.CompilerParams(vmem_limit_bytes=VMEM_BYTES),
        cost_estimate=LIGHT,
        name="sent_terms",
    )(n, z, y, cotangent, embedded, weight)
    return results[:3], results[3:7], results[7:11], *results[11:]


def pass_kernel(*refs):
    passed_hbm, mine_hbm, sent_hbm, (passed, mine, sent, sems, sems_out) = refs[:4], refs[4:8], refs[8:12], refs[12:]
    loads, outs = [], []
    for q in range(4):
        loads.append(pltpu.make_async_copy(passed_hbm[q].at[pl.ds(0, 256), :], passed.at[q], sems.at[2 * q]))
        loads.append(pltpu.make_async_copy(mine_hbm[q], mine.at[q], sems.at[2 * q + 1]))
        outs.append(pltpu.make_async_copy(sent.at[q], sent_hbm[q], sems_out.at[q]))
    for load in loads:
        load.start()
    for q in range(4):
        loads[2 * q].wait()
        loads[2 * q + 1].wait()
        sent[q] = (passed[q].astype(F32) + mine[q].astype(F32)).astype(BF16)
        outs[q].start()
    for copy in outs:
        copy.wait()


def passed_on(first, second):
    hbm = pl.BlockSpec(memory_space=pltpu.HBM)
    return pl.pallas_call(
        pass_kernel,
        out_shape=[jax.ShapeDtypeStruct((256, 1024), BF16)] * 4,
        in_specs=[pl.BlockSpec(memory_space=pl.ANY)] * 8,
        out_specs=[hbm] * 4,
        scratch_shapes=[
            pltpu.VMEM((4, 256, 1024), BF16),
            pltpu.VMEM((4, 256, 1024), BF16),
            pltpu.VMEM((4, 256, 1024), BF16),
            pltpu.SemaphoreType.DMA((8,)),
            pltpu.SemaphoreType.DMA((4,)),
        ],
        compiler_params=pltpu.CompilerParams(vmem_limit_bytes=VMEM_BYTES),
        cost_estimate=LIGHT,
        name="passed_on",
    )(*first, *second)


def kept_kernel(
    n_ref, cot_hbm, embedded_hbm, weight_hbm, bias_ref, scaled_hbm, owner_ref, row_ref, bag_ref, base_ref, slots_ref, ids_ref, *scratch
):
    cot, embedded, weight, scaled, cross, onehots, sems = scratch
    n = n_ref[0]

    def columns(q):
        at = pl.ds(own_chunk(n ^ q), 1024)
        return pltpu.make_async_copy(embedded_hbm.at[:, at], embedded.at[:, at], sems.at[q])

    def rows(q):
        at = pl.ds(own_chunk(n ^ q), 1024)
        return pltpu.make_async_copy(weight_hbm.at[at, :], weight.at[q], sems.at[4 + q])

    get_scaled = pltpu.make_async_copy(scaled_hbm, scaled, sems.at[8])
    get_cot = pltpu.make_async_copy(cot_hbm, cot, sems.at[9])
    rows(0).start()
    columns(0).start()
    get_scaled.start()
    for q in (1, 2, 3):
        rows(q).start()
        columns(q).start()
    get_cot.start()
    find_slots(n, owner_ref, row_ref, bag_ref, slots_ref, ids_ref, onehots)
    rows(0).wait()
    columns(0).wait()
    cross[...] = jnp.dot(embedded[:, pl.ds(own_chunk(n), 1024)], weight[0], preferred_element_type=F32)
    get_scaled.wait()
    base_ref[...] = lax.dot_general(scaled[...], weight[0], NT, preferred_element_type=F32)
    for q in (1, 2):
        rows(q).wait()
        columns(q).wait()
        cross[...] += jnp.dot(embedded[:, pl.ds(own_chunk(n ^ q), 1024)], weight[q], preferred_element_type=F32)
    rows(3).wait()
    columns(3).wait()
    get_cot.wait()
    grad = cot[...].astype(F32)
    last = jnp.dot(embedded[:, pl.ds(own_chunk(n ^ 3), 1024)], weight[3], preferred_element_type=F32)
    base_ref[...] += grad + grad * (cross[...] + last + bias_ref[...])


def kept_terms(n, cotangent, embedded, weight, bias, scaled, owner, row, bag):
    hbm = pl.BlockSpec(memory_space=pltpu.HBM)
    vmem = pl.BlockSpec(memory_space=pltpu.VMEM)
    samples, width = cotangent.shape
    depth = owner.shape[0]
    return pl.pallas_call(
        kept_kernel,
        out_shape=[
            jax.ShapeDtypeStruct((samples, width), F32),
            jax.ShapeDtypeStruct((depth * samples // E, E), jnp.int32),
            jax.ShapeDtypeStruct((2 * N_WIDE, CAP), F32),
        ],
        in_specs=[pl.BlockSpec(memory_space=pltpu.SMEM)] + [hbm] * 3 + [vmem, hbm] + [vmem] * 3,
        out_specs=[vmem] * 3,
        scratch_shapes=[
            pltpu.VMEM(cotangent.shape, BF16),
            pltpu.VMEM(embedded.shape, BF16),
            pltpu.VMEM((4, 1024, 1024), BF16),
            pltpu.VMEM((samples, width), BF16),
            pltpu.VMEM((samples, width), F32),
            pltpu.VMEM((N_WIDE * depth, samples), BF16),
            pltpu.SemaphoreType.DMA((10,)),
        ],
        compiler_params=pltpu.CompilerParams(vmem_limit_bytes=VMEM_BYTES),
        cost_estimate=LIGHT,
        name="kept_terms",
    )(n, cotangent, embedded, weight, bias.reshape(1, -1), scaled, owner, row, bag)


def own_kernel(z_ref, y_ref, embedded_hbm, turned_hbm, *refs):
    got_hbm, results, (embedded, turned, got, sems) = refs[:8], refs[8:12], refs[12:]
    z, y = z_ref[0], y_ref[0]
    loads = [(embedded_hbm, embedded), (turned_hbm, turned)]
    loads += [(got_hbm[k].at[pl.ds(256, 256), :], got.at[k]) for k in range(4)]
    loads += [(got_hbm[k], got.at[k]) for k in range(4, 8)]
    loads = [pltpu.make_async_copy(src, dst, sems.at[k]) for k, (src, dst) in enumerate(loads)]
    for load in loads:
        load.start()
    for load in loads:
        load.wait()
    for route, place in ((0, y), (1, z)):
        term = ring_term(route, turned, embedded, z, y, 0)
        up, down = 2 * route, 2 * route + 1
        total = jnp.concatenate(
            [
                term[:256, :] + got[4 + up].astype(F32) + got[down].astype(F32),
                term[256:, :] + got[4 + down].astype(F32) + got[up].astype(F32),
            ],
            axis=0,
        ).astype(BF16)
        high = place >= 2
        results[2 * route][...] = jnp.where(high, total[:, 512:], total[:, :512])
        results[2 * route + 1][...] = jnp.where(high, total[:, :512], total[:, 512:])


def own_terms(z, y, embedded, turned, first, second):
    hbm = pl.BlockSpec(memory_space=pltpu.HBM)
    vmem = pl.BlockSpec(memory_space=pltpu.VMEM)
    return pl.pallas_call(
        own_kernel,
        out_shape=[jax.ShapeDtypeStruct((512, 512), BF16)] * 4,
        in_specs=[pl.BlockSpec(memory_space=pltpu.SMEM)] * 2 + [hbm] + [pl.BlockSpec(memory_space=pl.ANY)] * 9,
        out_specs=[vmem] * 4,
        scratch_shapes=[
            pltpu.VMEM(embedded.shape, BF16),
            pltpu.VMEM(turned.shape, BF16),
            pltpu.VMEM((8, 256, 1024), BF16),
            pltpu.SemaphoreType.DMA((10,)),
        ],
        compiler_params=pltpu.CompilerParams(vmem_limit_bytes=VMEM_BYTES),
        cost_estimate=LIGHT,
        name="own_terms",
    )(z, y, embedded, turned, *first, *second)


def halves_of(array, bit, axis):
    size = array.shape[axis] // 2
    return (
        lax.dynamic_slice_in_dim(array, bit * size, size, axis),
        lax.dynamic_slice_in_dim(array, (1 - bit) * size, size, axis),
    )


def body(
    embedded,
    cotangent,
    cross_weight,
    cross_bias,
    bag_size,
    row_owner,
    row_id,
    emb_table,
    adagrad_state,
):
    panel = lax.axis_index("narrow")
    wide = lax.axis_index("wide")
    z, y, x_lo = wide // 8, (wide // 2) % 4, wide % 2
    core = panel % 2
    batch_rows = cotangent.shape[0]
    norm_factor = 1.0 / math.sqrt(batch_rows * N_WIDE)

    at = (panel.reshape(1), z.reshape(1), y.reshape(1))

    parts, first, second, scaled, turned, bias_part = sent_terms(*at, cotangent, embedded, cross_weight)
    from_mate_far = lax.ppermute(parts[0], "narrow", CORE)
    from_mate = lax.ppermute(parts[1], "narrow", CORE)
    ways = [z_perm(1), z_perm(3), y_perm(1), y_perm(3)]
    first = [lax.ppermute(first[q], "wide", ways[q]) for q in range(4)]
    chip_far = (parts[2].astype(F32) + from_mate_far.astype(F32)).astype(BF16)
    chip_far, scaled, from_mate = lax.optimization_barrier((chip_far, scaled, from_mate))
    far = lax.ppermute(chip_far, "narrow", X_HI)

    entries = (row_owner.reshape(row_owner.shape[1:3]).T, row_id.reshape(row_id.shape[1:]).T, bag_size.T)
    base, slots, ids = kept_terms(at[0], cotangent, embedded, cross_weight, cross_bias, scaled, *entries)
    slots, ids, *first = lax.optimization_barrier((slots, ids, *first))
    second = passed_on(first, second)
    slots, far, *second = lax.optimization_barrier((slots, far, *second))
    second = [lax.ppermute(second[q], "wide", ways[q]) for q in range(4)]

    payload = place_entries(slots.reshape(-1), base, from_mate, far, ids, bias_part)
    payload, *second = lax.optimization_barrier((payload, *second))
    recv = lax.all_to_all(payload, "wide", split_axis=0, concat_axis=0, tiled=True)

    keep_y, send_y, keep_z, send_z = own_terms(at[1], at[2], embedded, turned, first, second)
    recv, send_y, send_z = lax.optimization_barrier((recv, send_y, send_z))
    got = [lax.ppermute(send_y, "wide", y_flip(2)), lax.ppermute(send_z, "wide", z_flip(2))]
    keep, send, bias_sums = owned_sums(core.reshape(1), recv)
    from_core = lax.ppermute(send, "narrow", CORE)
    keep, *got = lax.optimization_barrier((keep, *got))
    quarters = []
    for half, other, place in ((keep_y, got[0], y), (keep_z, got[1], z)):
        quarters.append([part.astype(BF16) for part in halves_of(summed(half, [other]), place % 2, 1)])
    got = [lax.ppermute(quarters[0][1], "wide", y_flip(1)), lax.ppermute(quarters[1][1], "wide", z_flip(1))]
    keep, from_core, *_ = lax.optimization_barrier((keep, from_core, quarters[0][1], quarters[1][1]))
    chip = summed(keep, [from_core]).astype(BF16)
    pair = jnp.concatenate([summed(quarters[0][0], got[:1]), summed(quarters[1][0], got[1:])], axis=0).astype(BF16)
    x_keep, x_send = halves_of(pair, x_lo, 1)
    other_chip, x_send = lax.optimization_barrier((lax.ppermute(chip, "narrow", X_HI), x_send))
    x_got = lax.ppermute(x_send, "wide", X_LO)

    bias_grad = bias_sums.reshape(-1) * norm_factor
    mine = summed(chip, [other_chip])
    mate, x_got = lax.optimization_barrier((lax.ppermute(mine, "narrow", CORE), x_got))
    weight_grad = summed(x_keep, [x_got]).T * norm_factor
    row_grad = jnp.concatenate([jnp.where(core == 0, mine, mate), jnp.where(core == 0, mate, mine)], axis=0)
    new_state = adagrad_state + jnp.mean(row_grad * row_grad, axis=1)
    new_table = emb_table - LEARN_RATE * row_grad / jnp.sqrt(new_state)[:, None]
    return (weight_grad, bias_grad, new_table, new_state)


def solution(mesh):
    in_specs = (
        P("wide", None),
        P("wide", "narrow"),
        P(None, "narrow"),
        P("narrow"),
        P("wide", None),
        P("narrow", "wide", None, None),
        P("narrow", "wide", None),
        P("wide", None),
        P("wide"),
    )
    out_specs = (P("wide", "narrow"), P("narrow"), P("wide", None), P("wide"))
    return jax.shard_map(body, mesh=mesh, in_specs=in_specs, out_specs=out_specs, check_vma=False)
```

```python
import math

import jax
import jax.numpy as jnp
from jax import lax
from jax.experimental import pallas as pl
from jax.experimental.pallas import tpu as pltpu
from jax.sharding import PartitionSpec as P

LEARN_RATE = 0.3
E = 128
N_WIDE = 32
CAP = 512
TAIL = 16
BLOCK = CAP + TAIL
N_ROWS = 2048
HI = 4
LO = N_ROWS // HI
F32 = jnp.float32
BF16 = jnp.bfloat16
LIGHT = pl.CostEstimate(flops=1, bytes_accessed=1, transcendentals=0)
VMEM_BYTES = 56 << 20
NT = (((1,), (1,)), ((), ()))


def z_perm(d):
    return [(i, ((i // 8 + d) % 4) * 8 + i % 8) for i in range(N_WIDE)]


def y_perm(d):
    return [(i, (i // 8) * 8 + (((i // 2) % 4 + d) % 4) * 2 + i % 2) for i in range(N_WIDE)]


def y_flip(m):
    return [(i, i ^ (2 * m)) for i in range(N_WIDE)]


def z_flip(m):
    return [(i, i ^ (8 * m)) for i in range(N_WIDE)]


X_LO = [(i, i ^ 1) for i in range(N_WIDE)]
CORE = [(i, i ^ 1) for i in range(4)]
X_HI = [(i, i ^ 2) for i in range(4)]


def find_slots(panel, owner_ref, row_ref, bag_ref, slots_ref, ids_ref, onehots):
    depth, samples = owner_ref.shape
    feats = depth // 2
    bag = bag_ref[pl.ds(pl.multiple_of(panel * feats, feats), feats), :]
    bag = jnp.concatenate([bag[k // 2 : k // 2 + 1, :] for k in range(depth)], axis=0)
    live = (lax.broadcasted_iota(jnp.int32, (depth, samples), 0) & 1) < bag
    owner = jnp.where(live, owner_ref[...], N_WIDE)
    for t in range(N_WIDE):
        onehots[t * depth : (t + 1) * depth, :] = jnp.where(owner == t, 1.0, 0.0).astype(BF16)

    size = N_WIDE * depth
    first = lax.broadcasted_iota(jnp.int32, (samples, samples), 0)
    second = lax.broadcasted_iota(jnp.int32, (samples, samples), 1)
    before = jnp.where(first < second, 1.0, 0.0).astype(BF16)
    within = jnp.dot(onehots[...], before, preferred_element_type=F32)
    in_row = jnp.dot(onehots[...], jnp.ones((samples, E), BF16), preferred_element_type=F32)
    top = jnp.floor(in_row * (1.0 / 16.0))
    low = (in_row - 16.0 * top).astype(BF16)
    top = top.astype(BF16)
    r = lax.broadcasted_iota(jnp.int32, (size, size), 0)
    c = lax.broadcasted_iota(jnp.int32, (size, size), 1)
    shift = depth.bit_length() - 1
    earlier = jnp.where((r >> shift == c >> shift) & (c < r), 1.0, 0.0).astype(BF16)
    rows_before = 16.0 * jnp.dot(earlier, top, preferred_element_type=F32) + jnp.dot(
        earlier, low, preferred_element_type=F32
    )
    place = jnp.zeros((depth, samples), F32)
    for t in range(N_WIDE):
        at = slice(t * depth, (t + 1) * depth)
        ahead = jnp.concatenate([rows_before[at, :]] * (samples // E), axis=1)
        place = place + jnp.where(owner == t, within[at, :] + ahead, 0.0)
    place = place.astype(jnp.int32)
    slots = jnp.where(live, owner * CAP + place, N_WIDE * CAP)
    for k in range(samples // E):
        slots_ref[k * depth : (k + 1) * depth, :] = slots[:, k * E : (k + 1) * E]

    marked = row_ref[...] + 1
    top = (marked >> 6).astype(F32)
    low = (marked & 63).astype(F32)
    owners = lax.broadcasted_iota(jnp.int32, (N_WIDE, samples), 0)
    places = lax.broadcasted_iota(jnp.int32, (CAP, samples), 0)
    ids = jnp.zeros((2 * N_WIDE, CAP), F32)
    for k in range(depth):
        at = slice(k, k + 1)
        mine = owners == owner[at, :]
        marks = jnp.concatenate([jnp.where(mine, top[at, :], 0.0), jnp.where(mine, low[at, :], 0.0)], axis=0)
        there = jnp.where(places == place[at, :], 1.0, 0.0).astype(BF16)
        ids = ids + lax.dot_general(
            marks.astype(BF16), there, (((1,), (1,)), ((), ())), preferred_element_type=F32
        )
    ids_ref[...] = ids


def place_kernel(
    slots_ref, base_hbm, mate_hbm, far_hbm, ids_ref, bias_ref, out_ref, base, mate, far, rows, blocks, sems, sems_in
):
    depth = 16
    dump = N_WIDE * CAP
    loads = [
        pltpu.make_async_copy(src, dst, sems_in.at[k])
        for k, (src, dst) in enumerate(((base_hbm, base), (mate_hbm, mate), (far_hbm, far)))
    ]
    for load in loads:
        load.start()

    def clear(i, _):
        rows[pl.ds(pl.multiple_of(i * 256, 256), 256), :] = jnp.zeros((256, E), F32)
        return 0

    lax.fori_loop(0, dump // 256, clear, 0)
    for load in loads:
        load.wait()

    def place(i, _):
        first = pl.multiple_of(i * 16, 16)
        at = (first // E) * (depth * E) + first % E
        for f in range(8):
            cols = slice(f * E, (f + 1) * E)
            tile = base[pl.ds(first, 16), cols] + (
                mate[pl.ds(first, 16), cols].astype(F32) + far[pl.ds(first, 16), cols].astype(F32)
            )
            for b in range(16):
                row = tile[b : b + 1, :]
                for j in range(2):
                    slot = slots_ref[at + (2 * f + j) * E + b]
                    rows[pl.ds(slot, 1), :] = row
        return 0

    lax.fori_loop(0, base.shape[0] // 16, place, 0)

    bias = bias_ref[...]

    def copy_out(w):
        return pltpu.make_async_copy(blocks.at[w], out_ref.at[w], sems.at[w])

    def narrow_down(w, _):
        blocks[w, :CAP, :] = rows[pl.ds(pl.multiple_of(w * CAP, CAP), CAP), :].astype(BF16)
        top = ids_ref[pl.ds(w, 1), :]
        low = ids_ref[pl.ds(N_WIDE + w, 1), :]
        parts = [top[:, k * E : (k + 1) * E] for k in range(4)] + [low[:, k * E : (k + 1) * E] for k in range(4)]
        blocks[w, CAP:, :] = jnp.concatenate(parts + [bias], axis=0).astype(BF16)
        copy_out(w).start()
        return 0

    lax.fori_loop(0, N_WIDE, narrow_down, 0)

    def finish(w, _):
        copy_out(w).wait()
        return 0

    lax.fori_loop(0, N_WIDE, finish, 0)


def place_entries(slots, base, mate, far, ids, bias):
    vmem = pl.BlockSpec(memory_space=pltpu.VMEM)
    hbm = pl.BlockSpec(memory_space=pltpu.HBM)
    return pl.pallas_call(
        place_kernel,
        out_shape=jax.ShapeDtypeStruct((N_WIDE, BLOCK, E), BF16),
        in_specs=[pl.BlockSpec(memory_space=pltpu.SMEM)] + [pl.BlockSpec(memory_space=pl.ANY)] * 3 + [vmem] * 2,
        out_specs=hbm,
        scratch_shapes=[
            pltpu.VMEM(base.shape, F32),
            pltpu.VMEM(base.shape, BF16),
            pltpu.VMEM(base.shape, BF16),
            pltpu.VMEM((N_WIDE * CAP + 8, E), F32),
            pltpu.VMEM((N_WIDE, BLOCK, E), BF16),
            pltpu.SemaphoreType.DMA((N_WIDE,)),
            pltpu.SemaphoreType.DMA((3,)),
        ],
        compiler_params=pltpu.CompilerParams(vmem_limit_bytes=VMEM_BYTES),
        cost_estimate=LIGHT,
        name="place_entries",
    )(slots, base, mate, far, ids, bias)


def sums_kernel(core_ref, recv_hbm, keep_ref, send_ref, bias_ref, recv_ref, total, left, right, sems):
    lane_rows = lax.broadcasted_iota(jnp.int32, (LO, E), 0)
    steps = N_WIDE // 2

    def load(i):
        at = pl.ds(2 * i, 2)
        return pltpu.make_async_copy(recv_hbm.at[at], recv_ref.at[at], sems.at[i])

    def build(i, buf):
        for p in range(2):
            w = 2 * i + p
            ids = recv_ref[w, CAP : CAP + 16, :].astype(F32)
            row = (ids[0:4, :] * 64.0 + ids[4:8, :]).astype(jnp.int32) - 1
            hi = row >> (LO.bit_length() - 1)
            lo = jnp.where(row < 0, -1, row & (LO - 1))
            hi_col = jnp.transpose(jnp.concatenate([hi, hi], axis=0).astype(F32), (1, 0))
            for j in range(CAP // E):
                at = p * CAP + j * E
                left[buf, :, at : at + E] = jnp.where(lane_rows == lo[j : j + 1, :], 1.0, 0.0).astype(BF16)
                v = recv_ref[w, j * E : (j + 1) * E, :]
                own = jnp.broadcast_to(hi_col[:, j : j + 1], (E, E)).astype(BF16)
                for h in range(HI):
                    right[buf, at : at + E, h * E : (h + 1) * E] = jnp.where(own == BF16(h), v, BF16(0))

    for i in range(steps):
        load(i).start()
    total[...] = jnp.zeros_like(total)
    load(0).wait()
    build(0, 0)
    for i in range(1, steps):
        load(i).wait()

    def step(i, _):
        for b in range(2):
            build(jnp.minimum(2 * i + b + 1, steps - 1), 1 - b)
            total[...] += jnp.dot(left[b], right[b], preferred_element_type=F32)
        return 0

    lax.fori_loop(0, steps // 2, step, 0)
    bias_ref[...] = jnp.sum(recv_ref[:, CAP + 8 : CAP + 16, :].astype(F32), axis=0)
    for k in range(HI // 2):
        for out_ref, half in ((keep_ref, core_ref[0]), (send_ref, 1 - core_ref[0])):
            at = pl.multiple_of((half * (HI // 2) + k) * E, E)
            out_ref[k * LO : (k + 1) * LO, :] = total[:, pl.ds(at, E)].astype(BF16)


def owned_sums(core, recv):
    vmem = pl.BlockSpec(memory_space=pltpu.VMEM)
    return pl.pallas_call(
        sums_kernel,
        out_shape=[jax.ShapeDtypeStruct((N_ROWS // 2, E), BF16)] * 2 + [jax.ShapeDtypeStruct((8, E), F32)],
        in_specs=[pl.BlockSpec(memory_space=pltpu.SMEM), pl.BlockSpec(memory_space=pltpu.HBM)],
        out_specs=[vmem] * 3,
        scratch_shapes=[
            pltpu.VMEM((N_WIDE, BLOCK, E), BF16),
            pltpu.VMEM((LO, HI * E), F32),
            pltpu.VMEM((2, LO, 2 * CAP), BF16),
            pltpu.VMEM((2, 2 * CAP, HI * E), BF16),
            pltpu.SemaphoreType.DMA((N_WIDE // 2,)),
        ],
        compiler_params=pltpu.CompilerParams(vmem_limit_bytes=VMEM_BYTES),
        cost_estimate=LIGHT,
        name="owned_sums",
    )(core, recv)


def summed(own, others):
    total = own.astype(F32)
    for other in others:
        total = total + other.astype(F32)
    return total


def own_chunk(a):
    return pl.multiple_of(a * 1024, 1024)


def ring_term(route, turned, embedded, z, y, d):
    part = turned[route * 512 : (route + 1) * 512, :]
    if route == 0:
        rows = embedded[:, pl.ds(own_chunk((z + d) % 4), 1024)]
        return jnp.dot(part, rows, preferred_element_type=F32)
    start = ((y + d) % 4) * 256
    blocks = [embedded[:, pl.ds(pl.multiple_of(k * 1024 + start, 256), 256)] for k in range(4)]
    return jnp.concatenate([jnp.dot(part, rows, preferred_element_type=F32) for rows in blocks], axis=1)


def sent_kernel(n_ref, z_ref, y_ref, cot_hbm, embedded_hbm, weight_hbm, *refs):
    parts_hbm, first_hbm, second_hbm, (scaled_hbm, turned_hbm, bias_ref) = refs[:3], refs[3:7], refs[7:11], refs[11:14]
    cot, embedded, weight, scaled, turned, parts, first, second, sems, sems_out = refs[14:]
    n, z, y = n_ref[0], z_ref[0], y_ref[0]

    def columns(q):
        at = pl.ds(own_chunk(n ^ q), 1024)
        return pltpu.make_async_copy(embedded_hbm.at[:, at], embedded.at[:, at], sems.at[q])

    def rows(q):
        at = pl.ds(own_chunk(n ^ q), 1024)
        return pltpu.make_async_copy(weight_hbm.at[at, :], weight.at[q - 1], sems.at[3 + q])

    outs = [(parts.at[q], parts_hbm[q]) for q in range(3)]
    outs += [(first.at[q], first_hbm[q]) for q in range(4)] + [(second.at[q], second_hbm[q]) for q in range(4)]
    outs += [(scaled, scaled_hbm), (turned, turned_hbm)]
    outs = [pltpu.make_async_copy(src, dst, sems_out.at[k]) for k, (src, dst) in enumerate(outs)]

    get_cot = pltpu.make_async_copy(cot_hbm, cot, sems.at[7])
    get_cot.start()
    columns(0).start()
    rows(3).start()
    rows(1).start()
    get_cot.wait()
    columns(0).wait()
    rows(2).start()
    for q in (1, 2, 3):
        columns(q).start()
    grads = (cot[...].astype(F32) * embedded[:, pl.ds(own_chunk(n), 1024)].astype(F32)).astype(BF16)
    scaled[...] = grads
    outs[11].start()
    rows(3).wait()
    parts[0] = lax.dot_general(scaled[...], weight[2], NT, preferred_element_type=F32).astype(BF16)
    turned[...] = jnp.transpose(grads, (1, 0))
    sums = jnp.sum(grads.astype(F32), axis=0, keepdims=True)
    bias_ref[...] = jnp.concatenate([sums[:, k * E : (k + 1) * E] for k in range(8)], axis=0)
    outs[0].start()
    outs[12].start()
    for k, q in ((1, 1), (2, 2)):
        rows(q).wait()
        part = lax.dot_general(scaled[...], weight[q - 1], NT, preferred_element_type=F32)
        parts[k] = part.astype(BF16)
        outs[k].start()
    for q in (1, 2, 3):
        columns(q).wait()
    for route in range(2):
        term = ring_term(route, turned, embedded, z, y, 2).astype(BF16)
        for way in range(2):
            first[2 * route + way, :256, :] = term[way * 256 : (way + 1) * 256, :]
        for way in range(2):
            q = 2 * route + way
            term = ring_term(route, turned, embedded, z, y, 3 if way else 1).astype(BF16)
            other = term[(1 - way) * 256 : (2 - way) * 256, :]
            first[q, 256:, :] = other[:128, :]
            second[q, :256, :] = term[way * 256 : (way + 1) * 256, :]
            second[q, 256:, :] = other[128:, :]
            outs[3 + q].start()
            outs[7 + q].start()
    for copy in outs:
        copy.wait()


def sent_terms(n, z, y, cotangent, embedded, weight):
    hbm = pl.BlockSpec(memory_space=pltpu.HBM)
    smem = pl.BlockSpec(memory_space=pltpu.SMEM)
    samples, width = cotangent.shape
    shape = jax.ShapeDtypeStruct
    full, ring = shape((samples, width), BF16), shape((384, 1024), BF16)
    results = pl.pallas_call(
        sent_kernel,
        out_shape=[full] * 3 + [ring] * 8
        + [full, shape((width, samples), BF16), shape((8, E), F32)],
        in_specs=[smem] * 3 + [hbm] * 3,
        out_specs=[hbm] * 13 + [pl.BlockSpec(memory_space=pltpu.VMEM)],
        scratch_shapes=[
            pltpu.VMEM(cotangent.shape, BF16),
            pltpu.VMEM(embedded.shape, BF16),
            pltpu.VMEM((3, 1024, 1024), BF16),
            pltpu.VMEM((samples, width), BF16),
            pltpu.VMEM((width, samples), BF16),
            pltpu.VMEM((3, samples, width), BF16),
            pltpu.VMEM((4, 384, 1024), BF16),
            pltpu.VMEM((4, 384, 1024), BF16),
            pltpu.SemaphoreType.DMA((8,)),
            pltpu.SemaphoreType.DMA((13,)),
        ],
        compiler_params=pltpu.CompilerParams(vmem_limit_bytes=VMEM_BYTES),
        cost_estimate=LIGHT,
        name="sent_terms",
    )(n, z, y, cotangent, embedded, weight)
    return results[:3], results[3:7], results[7:11], *results[11:]


def pass_kernel(*refs):
    passed_hbm, mine_hbm, sent_hbm, (passed, mine, sems, sems_out) = refs[:4], refs[4:8], refs[8:12], refs[12:]
    loads, outs = [], []
    for q in range(4):
        loads.append(pltpu.make_async_copy(passed_hbm[q].at[pl.ds(0, 256), :], passed.at[q], sems.at[2 * q]))
        loads.append(pltpu.make_async_copy(mine_hbm[q], mine.at[q], sems.at[2 * q + 1]))
        outs.append(pltpu.make_async_copy(mine.at[q], sent_hbm[q], sems_out.at[q]))
    for load in loads:
        load.start()
    for q in range(4):
        loads[2 * q].wait()
        loads[2 * q + 1].wait()
        mine[q, :256, :] = (passed[q].astype(F32) + mine[q, :256, :].astype(F32)).astype(BF16)
        outs[q].start()
    for copy in outs:
        copy.wait()


def passed_on(first, second):
    hbm = pl.BlockSpec(memory_space=pltpu.HBM)
    return pl.pallas_call(
        pass_kernel,
        out_shape=[jax.ShapeDtypeStruct((384, 1024), BF16)] * 4,
        in_specs=[pl.BlockSpec(memory_space=pl.ANY)] * 8,
        out_specs=[hbm] * 4,
        scratch_shapes=[
            pltpu.VMEM((4, 256, 1024), BF16),
            pltpu.VMEM((4, 384, 1024), BF16),
            pltpu.SemaphoreType.DMA((8,)),
            pltpu.SemaphoreType.DMA((4,)),
        ],
        compiler_params=pltpu.CompilerParams(vmem_limit_bytes=VMEM_BYTES),
        cost_estimate=LIGHT,
        name="passed_on",
    )(*first, *second)


def kept_kernel(
    n_ref, cot_hbm, embedded_hbm, weight_hbm, bias_ref, scaled_hbm, owner_ref, row_ref, bag_ref, base_ref, slots_ref, ids_ref, *scratch
):
    cot, embedded, weight, scaled, cross, onehots, sems = scratch
    n = n_ref[0]

    def columns(q):
        at = pl.ds(own_chunk(n ^ q), 1024)
        return pltpu.make_async_copy(embedded_hbm.at[:, at], embedded.at[:, at], sems.at[q])

    def rows(q):
        at = pl.ds(own_chunk(n ^ q), 1024)
        return pltpu.make_async_copy(weight_hbm.at[at, :], weight.at[q], sems.at[4 + q])

    get_scaled = pltpu.make_async_copy(scaled_hbm, scaled, sems.at[8])
    get_cot = pltpu.make_async_copy(cot_hbm, cot, sems.at[9])
    rows(0).start()
    columns(0).start()
    get_scaled.start()
    for q in (1, 2, 3):
        rows(q).start()
        columns(q).start()
    get_cot.start()
    find_slots(n, owner_ref, row_ref, bag_ref, slots_ref, ids_ref, onehots)
    rows(0).wait()
    columns(0).wait()
    cross[...] = jnp.dot(embedded[:, pl.ds(own_chunk(n), 1024)], weight[0], preferred_element_type=F32)
    get_scaled.wait()
    base_ref[...] = lax.dot_general(scaled[...], weight[0], NT, preferred_element_type=F32)
    for q in (1, 2):
        rows(q).wait()
        columns(q).wait()
        cross[...] += jnp.dot(embedded[:, pl.ds(own_chunk(n ^ q), 1024)], weight[q], preferred_element_type=F32)
    rows(3).wait()
    columns(3).wait()
    get_cot.wait()
    grad = cot[...].astype(F32)
    last = jnp.dot(embedded[:, pl.ds(own_chunk(n ^ 3), 1024)], weight[3], preferred_element_type=F32)
    base_ref[...] += grad + grad * (cross[...] + last + bias_ref[...])


def kept_terms(n, cotangent, embedded, weight, bias, scaled, owner, row, bag):
    hbm = pl.BlockSpec(memory_space=pltpu.HBM)
    vmem = pl.BlockSpec(memory_space=pltpu.VMEM)
    samples, width = cotangent.shape
    depth = owner.shape[0]
    return pl.pallas_call(
        kept_kernel,
        out_shape=[
            jax.ShapeDtypeStruct((samples, width), F32),
            jax.ShapeDtypeStruct((depth * samples // E, E), jnp.int32),
            jax.ShapeDtypeStruct((2 * N_WIDE, CAP), F32),
        ],
        in_specs=[pl.BlockSpec(memory_space=pltpu.SMEM)] + [hbm] * 3 + [vmem, hbm] + [vmem] * 3,
        out_specs=[vmem] * 3,
        scratch_shapes=[
            pltpu.VMEM(cotangent.shape, BF16),
            pltpu.VMEM(embedded.shape, BF16),
            pltpu.VMEM((4, 1024, 1024), BF16),
            pltpu.VMEM((samples, width), BF16),
            pltpu.VMEM((samples, width), F32),
            pltpu.VMEM((N_WIDE * depth, samples), BF16),
            pltpu.SemaphoreType.DMA((10,)),
        ],
        compiler_params=pltpu.CompilerParams(vmem_limit_bytes=VMEM_BYTES),
        cost_estimate=LIGHT,
        name="kept_terms",
    )(n, cotangent, embedded, weight, bias.reshape(1, -1), scaled, owner, row, bag)


def own_kernel(z_ref, y_ref, embedded_hbm, turned_hbm, *refs):
    got_hbm, results, (embedded, turned, first, second, sems) = refs[:8], refs[8:12], refs[12:]
    z, y = z_ref[0], y_ref[0]
    loads = [(embedded_hbm, embedded), (turned_hbm, turned)]
    loads += [(got_hbm[k].at[pl.ds(256, 128), :], first.at[k]) for k in range(4)]
    loads += [(got_hbm[4 + k], second.at[k]) for k in range(4)]
    loads = [pltpu.make_async_copy(src, dst, sems.at[k]) for k, (src, dst) in enumerate(loads)]
    for load in loads:
        load.start()
    for load in loads:
        load.wait()
    for route, place in ((0, y), (1, z)):
        term = ring_term(route, turned, embedded, z, y, 0)
        up, down = 2 * route, 2 * route + 1
        total = []
        for at, mine, other in ((0, up, down), (256, down, up)):
            top = second[mine, :128, :].astype(F32) + first[other].astype(F32)
            low = second[mine, 128:256, :].astype(F32) + second[other, 256:, :].astype(F32)
            total += [term[at : at + 128, :] + top, term[at + 128 : at + 256, :] + low]
        total = jnp.concatenate(total, axis=0).astype(BF16)
        high = place >= 2
        results[2 * route][...] = jnp.where(high, total[:, 512:], total[:, :512])
        results[2 * route + 1][...] = jnp.where(high, total[:, :512], total[:, 512:])


def own_terms(z, y, embedded, turned, first, second):
    hbm = pl.BlockSpec(memory_space=pltpu.HBM)
    vmem = pl.BlockSpec(memory_space=pltpu.VMEM)
    return pl.pallas_call(
        own_kernel,
        out_shape=[jax.ShapeDtypeStruct((512, 512), BF16)] * 4,
        in_specs=[pl.BlockSpec(memory_space=pltpu.SMEM)] * 2 + [hbm] + [pl.BlockSpec(memory_space=pl.ANY)] * 9,
        out_specs=[vmem] * 4,
        scratch_shapes=[
            pltpu.VMEM(embedded.shape, BF16),
            pltpu.VMEM(turned.shape, BF16),
            pltpu.VMEM((4, 128, 1024), BF16),
            pltpu.VMEM((4, 384, 1024), BF16),
            pltpu.SemaphoreType.DMA((10,)),
        ],
        compiler_params=pltpu.CompilerParams(vmem_limit_bytes=VMEM_BYTES),
        cost_estimate=LIGHT,
        name="own_terms",
    )(z, y, embedded, turned, *first, *second)


def halves_of(array, bit, axis):
    size = array.shape[axis] // 2
    return (
        lax.dynamic_slice_in_dim(array, bit * size, size, axis),
        lax.dynamic_slice_in_dim(array, (1 - bit) * size, size, axis),
    )


def body(
    embedded,
    cotangent,
    cross_weight,
    cross_bias,
    bag_size,
    row_owner,
    row_id,
    emb_table,
    adagrad_state,
):
    panel = lax.axis_index("narrow")
    wide = lax.axis_index("wide")
    z, y, x_lo = wide // 8, (wide // 2) % 4, wide % 2
    core = panel % 2
    batch_rows = cotangent.shape[0]
    norm_factor = 1.0 / math.sqrt(batch_rows * N_WIDE)

    at = (panel.reshape(1), z.reshape(1), y.reshape(1))

    parts, first, second, scaled, turned, bias_part = sent_terms(*at, cotangent, embedded, cross_weight)
    from_mate_far = lax.ppermute(parts[0], "narrow", CORE)
    from_mate = lax.ppermute(parts[1], "narrow", CORE)
    ways = [z_perm(1), z_perm(3), y_perm(1), y_perm(3)]
    first = [lax.ppermute(first[q], "wide", ways[q]) for q in range(4)]
    chip_far = (parts[2].astype(F32) + from_mate_far.astype(F32)).astype(BF16)
    chip_far, scaled, from_mate = lax.optimization_barrier((chip_far, scaled, from_mate))
    far = lax.ppermute(chip_far, "narrow", X_HI)

    entries = (row_owner.reshape(row_owner.shape[1:3]).T, row_id.reshape(row_id.shape[1:]).T, bag_size.T)
    base, slots, ids = kept_terms(at[0], cotangent, embedded, cross_weight, cross_bias, scaled, *entries)
    slots, ids, *first = lax.optimization_barrier((slots, ids, *first))
    second = passed_on(first, second)
    slots, far, *second = lax.optimization_barrier((slots, far, *second))
    second = [lax.ppermute(second[q], "wide", ways[q]) for q in range(4)]

    payload = place_entries(slots.reshape(-1), base, from_mate, far, ids, bias_part)
    recv = lax.all_to_all(payload, "wide", split_axis=0, concat_axis=0, tiled=True)

    turned, payload = lax.optimization_barrier((turned, payload))
    keep_y, send_y, keep_z, send_z = own_terms(at[1], at[2], embedded, turned, first, second)
    recv, send_y, send_z = lax.optimization_barrier((recv, send_y, send_z))
    got = [lax.ppermute(send_y, "wide", y_flip(2)), lax.ppermute(send_z, "wide", z_flip(2))]
    keep, send, bias_sums = owned_sums(core.reshape(1), recv)
    from_core = lax.ppermute(send, "narrow", CORE)
    keep, *got = lax.optimization_barrier((keep, *got))
    quarters = []
    for half, other, place in ((keep_y, got[0], y), (keep_z, got[1], z)):
        quarters.append([part.astype(BF16) for part in halves_of(summed(half, [other]), place % 2, 1)])
    got = [lax.ppermute(quarters[0][1], "wide", y_flip(1)), lax.ppermute(quarters[1][1], "wide", z_flip(1))]
    keep, from_core, *_ = lax.optimization_barrier((keep, from_core, quarters[0][1], quarters[1][1]))
    chip = summed(keep, [from_core]).astype(BF16)
    pair = jnp.concatenate([summed(quarters[0][0], got[:1]), summed(quarters[1][0], got[1:])], axis=0).astype(BF16)
    x_keep, x_send = halves_of(pair, x_lo, 1)
    other_chip, x_send = lax.optimization_barrier((lax.ppermute(chip, "narrow", X_HI), x_send))
    x_got = lax.ppermute(x_send, "wide", X_LO)

    bias_grad = bias_sums.reshape(-1) * norm_factor
    mine = summed(chip, [other_chip])
    mate, x_got = lax.optimization_barrier((lax.ppermute(mine, "narrow", CORE), x_got))
    weight_grad = summed(x_keep, [x_got]).T * norm_factor
    row_grad = jnp.concatenate([jnp.where(core == 0, mine, mate), jnp.where(core == 0, mate, mine)], axis=0)
    new_state = adagrad_state + jnp.mean(row_grad * row_grad, axis=1)
    new_table = emb_table - LEARN_RATE * row_grad / jnp.sqrt(new_state)[:, None]
    return (weight_grad, bias_grad, new_table, new_state)


def solution(mesh):
    in_specs = (
        P("wide", None),
        P("wide", "narrow"),
        P(None, "narrow"),
        P("narrow"),
        P("wide", None),
        P("narrow", "wide", None, None),
        P("narrow", "wide", None),
        P("wide", None),
        P("wide"),
    )
    out_specs = (P("wide", "narrow"), P("narrow"), P("wide", None), P("wide"))
    return jax.shard_map(body, mesh=mesh, in_specs=in_specs, out_specs=out_specs, check_vma=False)
```

```python
import functools
import math

import jax
import jax.numpy as jnp
from jax import lax
from jax.experimental import pallas as pl
from jax.experimental.pallas import tpu as pltpu
from jax.sharding import PartitionSpec as P

LEARN_RATE = 0.3
E = 128
N_WIDE = 32
CAP = 512
TAIL = 16
BLOCK = CAP + TAIL
N_ROWS = 2048
HI = 4
LO = N_ROWS // HI
F32 = jnp.float32
BF16 = jnp.bfloat16
LIGHT = pl.CostEstimate(flops=1, bytes_accessed=1, transcendentals=0)
VMEM_BYTES = 56 << 20
NT = (((1,), (1,)), ((), ()))


def z_perm(d):
    return [(i, ((i // 8 + d) % 4) * 8 + i % 8) for i in range(N_WIDE)]


def y_perm(d):
    return [(i, (i // 8) * 8 + (((i // 2) % 4 + d) % 4) * 2 + i % 2) for i in range(N_WIDE)]


def y_flip(m):
    return [(i, i ^ (2 * m)) for i in range(N_WIDE)]


def z_flip(m):
    return [(i, i ^ (8 * m)) for i in range(N_WIDE)]


X_LO = [(i, i ^ 1) for i in range(N_WIDE)]
CORE = [(i, i ^ 1) for i in range(4)]
X_HI = [(i, i ^ 2) for i in range(4)]


def find_slots(panel, owner_ref, row_ref, bag_ref, slots_ref, ids_ref, onehots):
    depth, samples = owner_ref.shape
    feats = depth // 2
    bag = bag_ref[pl.ds(pl.multiple_of(panel * feats, feats), feats), :]
    bag = jnp.concatenate([bag[k // 2 : k // 2 + 1, :] for k in range(depth)], axis=0)
    live = (lax.broadcasted_iota(jnp.int32, (depth, samples), 0) & 1) < bag
    owner = jnp.where(live, owner_ref[...], N_WIDE)
    for t in range(N_WIDE):
        onehots[t * depth : (t + 1) * depth, :] = jnp.where(owner == t, 1.0, 0.0).astype(BF16)

    size = N_WIDE * depth
    first = lax.broadcasted_iota(jnp.int32, (samples, samples), 0)
    second = lax.broadcasted_iota(jnp.int32, (samples, samples), 1)
    before = jnp.where(first < second, 1.0, 0.0).astype(BF16)
    within = jnp.dot(onehots[...], before, preferred_element_type=F32)
    in_row = jnp.dot(onehots[...], jnp.ones((samples, E), BF16), preferred_element_type=F32)
    top = jnp.floor(in_row * (1.0 / 16.0))
    low = (in_row - 16.0 * top).astype(BF16)
    top = top.astype(BF16)
    r = lax.broadcasted_iota(jnp.int32, (size, size), 0)
    c = lax.broadcasted_iota(jnp.int32, (size, size), 1)
    shift = depth.bit_length() - 1
    earlier = jnp.where((r >> shift == c >> shift) & (c < r), 1.0, 0.0).astype(BF16)
    rows_before = 16.0 * jnp.dot(earlier, top, preferred_element_type=F32) + jnp.dot(
        earlier, low, preferred_element_type=F32
    )
    place = jnp.zeros((depth, samples), F32)
    for t in range(N_WIDE):
        at = slice(t * depth, (t + 1) * depth)
        ahead = jnp.concatenate([rows_before[at, :]] * (samples // E), axis=1)
        place = place + jnp.where(owner == t, within[at, :] + ahead, 0.0)
    place = place.astype(jnp.int32)
    slots = jnp.where(live, owner * CAP + place, N_WIDE * CAP)
    for k in range(samples // E):
        slots_ref[k * depth : (k + 1) * depth, :] = slots[:, k * E : (k + 1) * E]

    marked = row_ref[...] + 1
    top = (marked >> 6).astype(F32)
    low = (marked & 63).astype(F32)
    owners = lax.broadcasted_iota(jnp.int32, (N_WIDE, samples), 0)
    places = lax.broadcasted_iota(jnp.int32, (CAP, samples), 0)
    ids = jnp.zeros((2 * N_WIDE, CAP), F32)
    for k in range(depth):
        at = slice(k, k + 1)
        mine = owners == owner[at, :]
        marks = jnp.concatenate([jnp.where(mine, top[at, :], 0.0), jnp.where(mine, low[at, :], 0.0)], axis=0)
        there = jnp.where(places == place[at, :], 1.0, 0.0).astype(BF16)
        ids = ids + lax.dot_general(
            marks.astype(BF16), there, (((1,), (1,)), ((), ())), preferred_element_type=F32
        )
    ids_ref[...] = ids


def place_kernel(
    slots_ref, base_hbm, mate_hbm, far_hbm, ids_ref, bias_ref, out_ref, base, mate, far, rows, blocks, sems, sems_in
):
    depth = 16
    dump = N_WIDE * CAP
    loads = [
        pltpu.make_async_copy(src, dst, sems_in.at[k])
        for k, (src, dst) in enumerate(((base_hbm, base), (mate_hbm, mate), (far_hbm, far)))
    ]
    for load in loads:
        load.start()

    def clear(i, _):
        rows[pl.ds(pl.multiple_of(i * 256, 256), 256), :] = jnp.zeros((256, E), F32)
        return 0

    lax.fori_loop(0, dump // 256, clear, 0)
    for load in loads:
        load.wait()

    def place(i, _):
        first = pl.multiple_of(i * 16, 16)
        at = (first // E) * (depth * E) + first % E
        for f in range(8):
            cols = slice(f * E, (f + 1) * E)
            tile = base[pl.ds(first, 16), cols] + (
                mate[pl.ds(first, 16), cols].astype(F32) + far[pl.ds(first, 16), cols].astype(F32)
            )
            for b in range(16):
                row = tile[b : b + 1, :]
                for j in range(2):
                    slot = slots_ref[at + (2 * f + j) * E + b]
                    rows[pl.ds(slot, 1), :] = row
        return 0

    lax.fori_loop(0, base.shape[0] // 16, place, 0)

    bias = bias_ref[...]

    def copy_out(w):
        return pltpu.make_async_copy(blocks.at[w], out_ref.at[w], sems.at[w])

    def narrow_down(w, _):
        blocks[w, :CAP, :] = rows[pl.ds(pl.multiple_of(w * CAP, CAP), CAP), :].astype(BF16)
        top = ids_ref[pl.ds(w, 1), :]
        low = ids_ref[pl.ds(N_WIDE + w, 1), :]
        parts = [top[:, k * E : (k + 1) * E] for k in range(4)] + [low[:, k * E : (k + 1) * E] for k in range(4)]
        blocks[w, CAP:, :] = jnp.concatenate(parts + [bias], axis=0).astype(BF16)
        copy_out(w).start()
        return 0

    lax.fori_loop(0, N_WIDE, narrow_down, 0)

    def finish(w, _):
        copy_out(w).wait()
        return 0

    lax.fori_loop(0, N_WIDE, finish, 0)


def place_entries(slots, base, mate, far, ids, bias):
    vmem = pl.BlockSpec(memory_space=pltpu.VMEM)
    hbm = pl.BlockSpec(memory_space=pltpu.HBM)
    return pl.pallas_call(
        place_kernel,
        out_shape=jax.ShapeDtypeStruct((N_WIDE, BLOCK, E), BF16),
        in_specs=[pl.BlockSpec(memory_space=pltpu.SMEM)] + [pl.BlockSpec(memory_space=pl.ANY)] * 3 + [vmem] * 2,
        out_specs=hbm,
        scratch_shapes=[
            pltpu.VMEM(base.shape, F32),
            pltpu.VMEM(base.shape, BF16),
            pltpu.VMEM(base.shape, BF16),
            pltpu.VMEM((N_WIDE * CAP + 8, E), F32),
            pltpu.VMEM((N_WIDE, BLOCK, E), BF16),
            pltpu.SemaphoreType.DMA((N_WIDE,)),
            pltpu.SemaphoreType.DMA((3,)),
        ],
        compiler_params=pltpu.CompilerParams(vmem_limit_bytes=VMEM_BYTES),
        cost_estimate=LIGHT,
        name="place_entries",
    )(slots, base, mate, far, ids, bias)


def sums_kernel(norm_factor, core_ref, recv_ref, keep_ref, send_ref, bias_ref, total, left, right, todo):
    lane_rows = lax.broadcasted_iota(jnp.int32, (LO, E), 0)

    n = 0
    for w in range(N_WIDE):
        ids = recv_ref[w, CAP:, :].astype(F32)
        ids = ids[0:4, :] + ids[4:8, :]
        halves = jnp.max(jnp.where(ids[2:3, :] > 0.0, 2.0, jnp.where(ids[0:1, :] > 0.0, 1.0, 0.0)))
        todo[n] = 2 * w
        n = n + jnp.where(halves > 0.5, 1, 0)
        todo[n] = 2 * w + 1
        n = n + jnp.where(halves > 1.5, 1, 0)
    for k in range(12):
        todo[n + k] = -1
    total[...] = jnp.zeros_like(total)
    bias_ref[...] = jnp.sum(recv_ref[:, CAP + 8 : CAP + 16, :].astype(F32), axis=0) * norm_factor

    def build(i, buf):
        for p in range(4):
            item = todo[i * 4 + p]
            w = jnp.maximum(item, 0) // 2
            half = jnp.maximum(item, 0) % 2
            ids = recv_ref[w, CAP : CAP + 16, :].astype(F32)
            row = (ids[0:4, :] * 64.0 + ids[4:8, :]).astype(jnp.int32) - 1
            row = jnp.where(half == 0, row[0:2, :], row[2:4, :])
            row = jnp.where(item < 0, -1, row)
            hi = row >> (LO.bit_length() - 1)
            lo = jnp.where(row < 0, -1, row & (LO - 1))
            hi_col = jnp.transpose(jnp.concatenate([hi] * 4, axis=0).astype(F32), (1, 0))
            for j in range(2):
                at = (2 * p + j) * E
                left[buf, :, at : at + E] = jnp.where(lane_rows == lo[j : j + 1, :], 1.0, 0.0).astype(BF16)
                v = recv_ref[w, pl.ds(pl.multiple_of(half * (CAP // 2), CAP // 2) + j * E, E), :]
                own = jnp.broadcast_to(hi_col[:, j : j + 1], (E, E)).astype(BF16)
                for h in range(HI):
                    right[buf, at : at + E, h * E : (h + 1) * E] = jnp.where(own == BF16(h), v, BF16(0))

    build(0, 0)

    def step(i, _):
        for b in range(2):
            build(2 * i + b + 1, 1 - b)
            total[...] += jnp.dot(left[b], right[b], preferred_element_type=F32)
        return 0

    lax.fori_loop(0, (n + 7) // 8, step, 0)
    for k in range(HI // 2):
        for out_ref, half in ((keep_ref, core_ref[0]), (send_ref, 1 - core_ref[0])):
            at = pl.multiple_of((half * (HI // 2) + k) * E, E)
            out_ref[k * LO : (k + 1) * LO, :] = total[:, pl.ds(at, E)].astype(BF16)


def owned_sums(norm_factor, core, recv):
    vmem = pl.BlockSpec(memory_space=pltpu.VMEM)
    return pl.pallas_call(
        functools.partial(sums_kernel, norm_factor),
        out_shape=[jax.ShapeDtypeStruct((N_ROWS // 2, E), BF16)] * 2 + [jax.ShapeDtypeStruct((8, E), F32)],
        in_specs=[pl.BlockSpec(memory_space=pltpu.SMEM), vmem],
        out_specs=[vmem] * 3,
        scratch_shapes=[
            pltpu.VMEM((LO, HI * E), F32),
            pltpu.VMEM((2, LO, 2 * CAP), BF16),
            pltpu.VMEM((2, 2 * CAP, HI * E), BF16),
            pltpu.SMEM((2 * N_WIDE + 16,), jnp.int32),
        ],
        compiler_params=pltpu.CompilerParams(vmem_limit_bytes=VMEM_BYTES),
        cost_estimate=LIGHT,
        name="owned_sums",
    )(core, recv)


def summed(own, others):
    total = own.astype(F32)
    for other in others:
        total = total + other.astype(F32)
    return total


def own_chunk(a):
    return pl.multiple_of(a * 1024, 1024)


def ring_terms(route, turned, embedded, z, y, d):
    part = turned[route * 512 : (route + 1) * 512, :]
    if route == 0:
        rows = embedded[:, pl.ds(own_chunk((z + d) % 4), 1024)]
        yield slice(0, 1024), jnp.dot(part, rows, preferred_element_type=F32)
        return
    start = ((y + d) % 4) * 256
    for k in range(4):
        rows = embedded[:, pl.ds(pl.multiple_of(k * 1024 + start, 256), 256)]
        yield slice(k * 256, (k + 1) * 256), jnp.dot(part, rows, preferred_element_type=F32)


def sent_kernel(n_ref, z_ref, y_ref, cot_hbm, embedded_hbm, weight_hbm, *refs):
    parts_hbm, first_hbm, second_hbm, (scaled_hbm, turned_hbm, bias_ref) = refs[:3], refs[3:7], refs[7:11], refs[11:14]
    cot, embedded, weight, scaled, turned, parts, first, second, sems, sems_out = refs[14:]
    n, z, y = n_ref[0], z_ref[0], y_ref[0]

    def columns(q):
        at = pl.ds(own_chunk(n ^ q), 1024)
        return pltpu.make_async_copy(embedded_hbm.at[:, at], embedded.at[:, at], sems.at[q])

    def rows(q):
        at = pl.ds(own_chunk(n ^ q), 1024)
        return pltpu.make_async_copy(weight_hbm.at[at, :], weight.at[q - 1], sems.at[3 + q])

    outs = [(parts.at[q], parts_hbm[q]) for q in range(3)]
    outs += [(first.at[q], first_hbm[q]) for q in range(4)] + [(second.at[q], second_hbm[q]) for q in range(4)]
    outs += [(scaled, scaled_hbm), (turned, turned_hbm)]
    outs = [pltpu.make_async_copy(src, dst, sems_out.at[k]) for k, (src, dst) in enumerate(outs)]

    get_cot = pltpu.make_async_copy(cot_hbm, cot, sems.at[7])
    get_cot.start()
    columns(0).start()
    rows(3).start()
    get_cot.wait()
    columns(0).wait()
    for q in (1, 2):
        rows(q).start()
    for q in (1, 2, 3):
        columns(q).start()
    grads = (cot[...].astype(F32) * embedded[:, pl.ds(own_chunk(n), 1024)].astype(F32)).astype(BF16)
    scaled[...] = grads
    outs[11].start()
    rows(3).wait()
    parts[0] = lax.dot_general(scaled[...], weight[2], NT, preferred_element_type=F32).astype(BF16)
    turned[...] = jnp.transpose(grads, (1, 0))
    sums = jnp.sum(grads.astype(F32), axis=0, keepdims=True)
    bias_ref[...] = jnp.concatenate([sums[:, k * E : (k + 1) * E] for k in range(8)], axis=0)
    outs[0].start()
    outs[12].start()
    for k, q in ((1, 1), (2, 2)):
        rows(q).wait()
        part = lax.dot_general(scaled[...], weight[q - 1], NT, preferred_element_type=F32)
        parts[k] = part.astype(BF16)
        outs[k].start()
    for q in (1, 2, 3):
        columns(q).wait()
    for route in range(2):
        for at, term in ring_terms(route, turned, embedded, z, y, 2):
            term = term.astype(BF16)
            for way in range(2):
                first[2 * route + way, :256, at] = term[way * 256 : (way + 1) * 256, :]
        for way in range(2):
            q = 2 * route + way
            for at, term in ring_terms(route, turned, embedded, z, y, 3 if way else 1):
                term = term.astype(BF16)
                first[q, 256:, at] = term[(1 - way) * 256 : (2 - way) * 256, :]
                second[q, :, at] = term[way * 256 : (way + 1) * 256, :]
            outs[3 + q].start()
            outs[7 + q].start()
    for copy in outs:
        copy.wait()


def sent_terms(n, z, y, cotangent, embedded, weight):
    hbm = pl.BlockSpec(memory_space=pltpu.HBM)
    smem = pl.BlockSpec(memory_space=pltpu.SMEM)
    samples, width = cotangent.shape
    shape = jax.ShapeDtypeStruct
    full, half = shape((samples, width), BF16), shape((256, 1024), BF16)
    results = pl.pallas_call(
        sent_kernel,
        out_shape=[full] * 3 + [shape((512, 1024), BF16)] * 4 + [half] * 4
        + [full, shape((width, samples), BF16), shape((8, E), F32)],
        in_specs=[smem] * 3 + [hbm] * 3,
        out_specs=[hbm] * 13 + [pl.BlockSpec(memory_space=pltpu.VMEM)],
        scratch_shapes=[
            pltpu.VMEM(cotangent.shape, BF16),
            pltpu.VMEM(embedded.shape, BF16),
            pltpu.VMEM((3, 1024, 1024), BF16),
            pltpu.VMEM((samples, width), BF16),
            pltpu.VMEM((width, samples), BF16),
            pltpu.VMEM((3, samples, width), BF16),
            pltpu.VMEM((4, 512, 1024), BF16),
            pltpu.VMEM((4, 256, 1024), BF16),
            pltpu.SemaphoreType.DMA((8,)),
            pltpu.SemaphoreType.DMA((13,)),
        ],
        compiler_params=pltpu.CompilerParams(vmem_limit_bytes=VMEM_BYTES),
        cost_estimate=LIGHT,
        name="sent_terms",
    )(n, z, y, cotangent, embedded, weight)
    return results[:3], results[3:7], results[7:11], *results[11:]


def pass_kernel(*refs):
    passed_hbm, mine_hbm, sent_hbm, (passed, mine, sent, sems, sems_out) = refs[:4], refs[4:8], refs[8:12], refs[12:]
    loads, outs = [], []
    for q in range(4):
        loads.append(pltpu.make_async_copy(passed_hbm[q].at[pl.ds(0, 256), :], passed.at[q], sems.at[2 * q]))
        loads.append(pltpu.make_async_copy(mine_hbm[q], mine.at[q], sems.at[2 * q + 1]))
        outs.append(pltpu.make_async_copy(sent.at[q], sent_hbm[q], sems_out.at[q]))
    for load in loads:
        load.start()
    for q in range(4):
        loads[2 * q].wait()
        loads[2 * q + 1].wait()
        sent[q] = (passed[q].astype(F32) + mine[q].astype(F32)).astype(BF16)
        outs[q].start()
    for copy in outs:
        copy.wait()


def passed_on(first, second):
    hbm = pl.BlockSpec(memory_space=pltpu.HBM)
    return pl.pallas_call(
        pass_kernel,
        out_shape=[jax.ShapeDtypeStruct((256, 1024), BF16)] * 4,
        in_specs=[pl.BlockSpec(memory_space=pl.ANY)] * 8,
        out_specs=[hbm] * 4,
        scratch_shapes=[
            pltpu.VMEM((4, 256, 1024), BF16),
            pltpu.VMEM((4, 256, 1024), BF16),
            pltpu.VMEM((4, 256, 1024), BF16),
            pltpu.SemaphoreType.DMA((8,)),
            pltpu.SemaphoreType.DMA((4,)),
        ],
        compiler_params=pltpu.CompilerParams(vmem_limit_bytes=VMEM_BYTES),
        cost_estimate=LIGHT,
        name="passed_on",
    )(*first, *second)


def kept_kernel(
    n_ref, cot_hbm, embedded_hbm, weight_hbm, bias_ref, scaled_hbm, owner_ref, row_ref, bag_ref, base_ref, slots_ref, ids_ref, *scratch
):
    cot, embedded, weight, scaled, cross, onehots, sems = scratch
    n = n_ref[0]

    def columns(q):
        at = pl.ds(own_chunk(n ^ q), 1024)
        return pltpu.make_async_copy(embedded_hbm.at[:, at], embedded.at[:, at], sems.at[q])

    def rows(q):
        at = pl.ds(own_chunk(n ^ q), 1024)
        return pltpu.make_async_copy(weight_hbm.at[at, :], weight.at[q], sems.at[4 + q])

    get_scaled = pltpu.make_async_copy(scaled_hbm, scaled, sems.at[8])
    get_cot = pltpu.make_async_copy(cot_hbm, cot, sems.at[9])
    rows(0).start()
    columns(0).start()
    get_scaled.start()
    for q in (1, 2, 3):
        rows(q).start()
        columns(q).start()
    get_cot.start()
    find_slots(n, owner_ref, row_ref, bag_ref, slots_ref, ids_ref, onehots)
    rows(0).wait()
    columns(0).wait()
    cross[...] = jnp.dot(embedded[:, pl.ds(own_chunk(n), 1024)], weight[0], preferred_element_type=F32)
    get_scaled.wait()
    base_ref[...] = lax.dot_general(scaled[...], weight[0], NT, preferred_element_type=F32)
    for q in (1, 2):
        rows(q).wait()
        columns(q).wait()
        cross[...] += jnp.dot(embedded[:, pl.ds(own_chunk(n ^ q), 1024)], weight[q], preferred_element_type=F32)
    rows(3).wait()
    columns(3).wait()
    get_cot.wait()
    grad = cot[...].astype(F32)
    last = jnp.dot(embedded[:, pl.ds(own_chunk(n ^ 3), 1024)], weight[3], preferred_element_type=F32)
    base_ref[...] += grad + grad * (cross[...] + last + bias_ref[...])


def kept_terms(n, cotangent, embedded, weight, bias, scaled, owner, row, bag):
    hbm = pl.BlockSpec(memory_space=pltpu.HBM)
    vmem = pl.BlockSpec(memory_space=pltpu.VMEM)
    samples, width = cotangent.shape
    depth = owner.shape[0]
    return pl.pallas_call(
        kept_kernel,
        out_shape=[
            jax.ShapeDtypeStruct((samples, width), F32),
            jax.ShapeDtypeStruct((depth * samples // E, E), jnp.int32),
            jax.ShapeDtypeStruct((2 * N_WIDE, CAP), F32),
        ],
        in_specs=[pl.BlockSpec(memory_space=pltpu.SMEM)] + [hbm] * 3 + [vmem, hbm] + [vmem] * 3,
        out_specs=[vmem] * 3,
        scratch_shapes=[
            pltpu.VMEM(cotangent.shape, BF16),
            pltpu.VMEM(embedded.shape, BF16),
            pltpu.VMEM((4, 1024, 1024), BF16),
            pltpu.VMEM((samples, width), BF16),
            pltpu.VMEM((samples, width), F32),
            pltpu.VMEM((N_WIDE * depth, samples), BF16),
            pltpu.SemaphoreType.DMA((10,)),
        ],
        compiler_params=pltpu.CompilerParams(vmem_limit_bytes=VMEM_BYTES),
        cost_estimate=LIGHT,
        name="kept_terms",
    )(n, cotangent, embedded, weight, bias.reshape(1, -1), scaled, owner, row, bag)


def own_kernel(z_ref, y_ref, embedded_hbm, turned_hbm, *refs):
    got_hbm, results, (embedded, turned, got, sems) = refs[:8], refs[8:12], refs[12:]
    z, y = z_ref[0], y_ref[0]
    loads = [(embedded_hbm, embedded), (turned_hbm, turned)]
    loads += [(got_hbm[k].at[pl.ds(256, 256), :], got.at[k]) for k in range(4)]
    loads += [(got_hbm[k], got.at[k]) for k in range(4, 8)]
    loads = [pltpu.make_async_copy(src, dst, sems.at[k]) for k, (src, dst) in enumerate(loads)]
    for load in loads:
        load.start()
    for load in loads:
        load.wait()
    for route, place in ((0, y), (1, z)):
        term = jnp.concatenate([term for _, term in ring_terms(route, turned, embedded, z, y, 0)], axis=1)
        up, down = 2 * route, 2 * route + 1
        total = jnp.concatenate(
            [
                term[:256, :] + got[4 + up].astype(F32) + got[down].astype(F32),
                term[256:, :] + got[4 + down].astype(F32) + got[up].astype(F32),
            ],
            axis=0,
        ).astype(BF16)
        high = place >= 2
        results[2 * route][...] = jnp.where(high, total[:, 512:], total[:, :512])
        results[2 * route + 1][...] = jnp.where(high, total[:, :512], total[:, 512:])


def own_terms(z, y, embedded, turned, first, second):
    hbm = pl.BlockSpec(memory_space=pltpu.HBM)
    vmem = pl.BlockSpec(memory_space=pltpu.VMEM)
    return pl.pallas_call(
        own_kernel,
        out_shape=[jax.ShapeDtypeStruct((512, 512), BF16)] * 4,
        in_specs=[pl.BlockSpec(memory_space=pltpu.SMEM)] * 2 + [hbm] + [pl.BlockSpec(memory_space=pl.ANY)] * 9,
        out_specs=[vmem] * 4,
        scratch_shapes=[
            pltpu.VMEM(embedded.shape, BF16),
            pltpu.VMEM(turned.shape, BF16),
            pltpu.VMEM((8, 256, 1024), BF16),
            pltpu.SemaphoreType.DMA((10,)),
        ],
        compiler_params=pltpu.CompilerParams(vmem_limit_bytes=VMEM_BYTES),
        cost_estimate=LIGHT,
        name="own_terms",
    )(z, y, embedded, turned, *first, *second)


def halves_of(array, bit, axis):
    size = array.shape[axis] // 2
    return (
        lax.dynamic_slice_in_dim(array, bit * size, size, axis),
        lax.dynamic_slice_in_dim(array, (1 - bit) * size, size, axis),
    )


def body(
    embedded,
    cotangent,
    cross_weight,
    cross_bias,
    bag_size,
    row_owner,
    row_id,
    emb_table,
    adagrad_state,
):
    panel = lax.axis_index("narrow")
    wide = lax.axis_index("wide")
    z, y, x_lo = wide // 8, (wide // 2) % 4, wide % 2
    core = panel % 2
    batch_rows = cotangent.shape[0]
    norm_factor = 1.0 / math.sqrt(batch_rows * N_WIDE)

    at = (panel.reshape(1), z.reshape(1), y.reshape(1))

    parts, first, second, scaled, turned, bias_part = sent_terms(*at, cotangent, embedded, cross_weight)
    from_mate_far = lax.ppermute(parts[0], "narrow", CORE)
    from_mate = lax.ppermute(parts[1], "narrow", CORE)
    ways = [z_perm(1), z_perm(3), y_perm(1), y_perm(3)]
    first = [lax.ppermute(first[q], "wide", ways[q]) for q in range(4)]
    chip_far = (parts[2].astype(F32) + from_mate_far.astype(F32)).astype(BF16)
    chip_far, scaled, from_mate = lax.optimization_barrier((chip_far, scaled, from_mate))
    far = lax.ppermute(chip_far, "narrow", X_HI)

    entries = (row_owner.reshape(row_owner.shape[1:3]).T, row_id.reshape(row_id.shape[1:]).T, bag_size.T)
    base, slots, ids = kept_terms(at[0], cotangent, embedded, cross_weight, cross_bias, scaled, *entries)
    slots, ids, *first = lax.optimization_barrier((slots, ids, *first))
    second = passed_on(first, second)
    slots, far, *second = lax.optimization_barrier((slots, far, *second))
    second = [lax.ppermute(second[q], "wide", ways[q]) for q in range(4)]

    payload = place_entries(slots.reshape(-1), base, from_mate, far, ids, bias_part)
    payload, *second = lax.optimization_barrier((payload, *second))
    recv = lax.all_to_all(payload, "wide", split_axis=0, concat_axis=0, tiled=True)

    keep_y, send_y, keep_z, send_z = own_terms(at[1], at[2], embedded, turned, first, second)
    recv, send_y, send_z = lax.optimization_barrier((recv, send_y, send_z))
    got = [lax.ppermute(send_y, "wide", y_flip(2)), lax.ppermute(send_z, "wide", z_flip(2))]
    keep, send, bias_sums = owned_sums(norm_factor, core.reshape(1), recv)
    from_core = lax.ppermute(send, "narrow", CORE)
    keep, *got = lax.optimization_barrier((keep, *got))
    quarters = []
    for half, other, place in ((keep_y, got[0], y), (keep_z, got[1], z)):
        quarters.append([part.astype(BF16) for part in halves_of(summed(half, [other]), place % 2, 1)])
    got = [lax.ppermute(quarters[0][1], "wide", y_flip(1)), lax.ppermute(quarters[1][1], "wide", z_flip(1))]
    keep, from_core, *_ = lax.optimization_barrier((keep, from_core, quarters[0][1], quarters[1][1]))
    chip = summed(keep, [from_core]).astype(BF16)
    pair = jnp.concatenate([summed(quarters[0][0], got[:1]), summed(quarters[1][0], got[1:])], axis=0).astype(BF16)
    x_keep, x_send = halves_of(pair, x_lo, 1)
    other_chip, _ = lax.optimization_barrier((lax.ppermute(chip, "narrow", X_HI), x_send))
    x_got = lax.ppermute(jnp.pad(x_send, ((0, 16), (0, 0))), "wide", X_LO)[:1024]

    bias_grad = bias_sums.reshape(-1)
    mine = summed(chip, [other_chip]).astype(BF16)
    mate, x_got = lax.optimization_barrier((lax.ppermute(mine, "narrow", CORE), x_got))
    weight_grad = summed(x_keep, [x_got]).T * norm_factor
    row_grad = jnp.concatenate([jnp.where(core == 0, mine, mate), jnp.where(core == 0, mate, mine)], axis=0).astype(F32)
    new_state = adagrad_state + jnp.mean(row_grad * row_grad, axis=1)
    new_table = emb_table - LEARN_RATE * row_grad / jnp.sqrt(new_state)[:, None]
    return (weight_grad, bias_grad, new_table, new_state)


def solution(mesh):
    in_specs = (
        P("wide", None),
        P("wide", "narrow"),
        P(None, "narrow"),
        P("narrow"),
        P("wide", None),
        P("narrow", "wide", None, None),
        P("narrow", "wide", None),
        P("wide", None),
        P("wide"),
    )
    out_specs = (P("wide", "narrow"), P("narrow"), P("wide", None), P("wide"))
    return jax.shard_map(body, mesh=mesh, in_specs=in_specs, out_specs=out_specs, check_vma=False)
```

```python
import functools
import math

import jax
import jax.numpy as jnp
from jax import lax
from jax.experimental import pallas as pl
from jax.experimental.pallas import tpu as pltpu
from jax.sharding import PartitionSpec as P

LEARN_RATE = 0.3
E = 128
N_WIDE = 32
CAP = 512
TAIL = 16
BLOCK = CAP + TAIL
N_ROWS = 2048
HI = 4
LO = N_ROWS // HI
F32 = jnp.float32
BF16 = jnp.bfloat16
LIGHT = pl.CostEstimate(flops=1, bytes_accessed=1, transcendentals=0)
VMEM_BYTES = 56 << 20
NT = (((1,), (1,)), ((), ()))


def z_perm(d):
    return [(i, ((i // 8 + d) % 4) * 8 + i % 8) for i in range(N_WIDE)]


def y_perm(d):
    return [(i, (i // 8) * 8 + (((i // 2) % 4 + d) % 4) * 2 + i % 2) for i in range(N_WIDE)]


def y_flip(m):
    return [(i, i ^ (2 * m)) for i in range(N_WIDE)]


def z_flip(m):
    return [(i, i ^ (8 * m)) for i in range(N_WIDE)]


X_LO = [(i, i ^ 1) for i in range(N_WIDE)]
CORE = [(i, i ^ 1) for i in range(4)]
X_HI = [(i, i ^ 2) for i in range(4)]


def find_slots(panel, owner_ref, row_ref, bag_ref, slots_ref, ids_ref, onehots):
    depth, samples = owner_ref.shape
    feats = depth // 2
    bag = bag_ref[pl.ds(pl.multiple_of(panel * feats, feats), feats), :]
    bag = jnp.concatenate([bag[k // 2 : k // 2 + 1, :] for k in range(depth)], axis=0)
    live = (lax.broadcasted_iota(jnp.int32, (depth, samples), 0) & 1) < bag
    owner = jnp.where(live, owner_ref[...], N_WIDE)
    for t in range(N_WIDE):
        onehots[t * depth : (t + 1) * depth, :] = jnp.where(owner == t, 1.0, 0.0).astype(BF16)

    size = N_WIDE * depth
    first = lax.broadcasted_iota(jnp.int32, (samples, samples), 0)
    second = lax.broadcasted_iota(jnp.int32, (samples, samples), 1)
    before = jnp.where(first < second, 1.0, 0.0).astype(BF16)
    within = jnp.dot(onehots[...], before, preferred_element_type=F32)
    in_row = jnp.dot(onehots[...], jnp.ones((samples, E), BF16), preferred_element_type=F32)
    top = jnp.floor(in_row * (1.0 / 16.0))
    low = (in_row - 16.0 * top).astype(BF16)
    top = top.astype(BF16)
    r = lax.broadcasted_iota(jnp.int32, (size, size), 0)
    c = lax.broadcasted_iota(jnp.int32, (size, size), 1)
    shift = depth.bit_length() - 1
    earlier = jnp.where((r >> shift == c >> shift) & (c < r), 1.0, 0.0).astype(BF16)
    rows_before = 16.0 * jnp.dot(earlier, top, preferred_element_type=F32) + jnp.dot(
        earlier, low, preferred_element_type=F32
    )
    place = jnp.zeros((depth, samples), F32)
    for t in range(N_WIDE):
        at = slice(t * depth, (t + 1) * depth)
        ahead = jnp.concatenate([rows_before[at, :]] * (samples // E), axis=1)
        place = place + jnp.where(owner == t, within[at, :] + ahead, 0.0)
    place = place.astype(jnp.int32)
    slots = jnp.where(live, owner * CAP + place, N_WIDE * CAP)
    for k in range(samples // E):
        slots_ref[k * depth : (k + 1) * depth, :] = slots[:, k * E : (k + 1) * E]

    marked = row_ref[...] + 1
    top = (marked >> 6).astype(F32)
    low = (marked & 63).astype(F32)
    owners = lax.broadcasted_iota(jnp.int32, (N_WIDE, samples), 0)
    places = lax.broadcasted_iota(jnp.int32, (CAP, samples), 0)
    ids = jnp.zeros((2 * N_WIDE, CAP), F32)
    for k in range(depth):
        at = slice(k, k + 1)
        mine = owners == owner[at, :]
        marks = jnp.concatenate([jnp.where(mine, top[at, :], 0.0), jnp.where(mine, low[at, :], 0.0)], axis=0)
        there = jnp.where(places == place[at, :], 1.0, 0.0).astype(BF16)
        ids = ids + lax.dot_general(
            marks.astype(BF16), there, (((1,), (1,)), ((), ())), preferred_element_type=F32
        )
    ids_ref[...] = ids


def place_kernel(
    slots_ref, base_hbm, mate_hbm, far_hbm, ids_ref, bias_ref, out_ref, base, mate, far, rows, blocks, sems, sems_in
):
    depth = 16
    dump = N_WIDE * CAP
    loads = [
        pltpu.make_async_copy(src, dst, sems_in.at[k])
        for k, (src, dst) in enumerate(((base_hbm, base), (mate_hbm, mate), (far_hbm, far)))
    ]
    for load in loads:
        load.start()

    def clear(i, _):
        rows[pl.ds(pl.multiple_of(i * 256, 256), 256), :] = jnp.zeros((256, E), F32)
        return 0

    lax.fori_loop(0, dump // 256, clear, 0)
    for load in loads:
        load.wait()

    def place(i, _):
        first = pl.multiple_of(i * 16, 16)
        at = (first // E) * (depth * E) + first % E
        for f in range(8):
            cols = slice(f * E, (f + 1) * E)
            tile = base[pl.ds(first, 16), cols] + (
                mate[pl.ds(first, 16), cols].astype(F32) + far[pl.ds(first, 16), cols].astype(F32)
            )
            for b in range(16):
                row = tile[b : b + 1, :]
                for j in range(2):
                    slot = slots_ref[at + (2 * f + j) * E + b]
                    rows[pl.ds(slot, 1), :] = row
        return 0

    lax.fori_loop(0, base.shape[0] // 16, place, 0)

    bias = bias_ref[...]

    def copy_out(w):
        return pltpu.make_async_copy(blocks.at[w], out_ref.at[w], sems.at[w])

    def narrow_down(w, _):
        blocks[w, :CAP, :] = rows[pl.ds(pl.multiple_of(w * CAP, CAP), CAP), :].astype(BF16)
        top = ids_ref[pl.ds(w, 1), :]
        low = ids_ref[pl.ds(N_WIDE + w, 1), :]
        parts = [top[:, k * E : (k + 1) * E] for k in range(4)] + [low[:, k * E : (k + 1) * E] for k in range(4)]
        blocks[w, CAP:, :] = jnp.concatenate(parts + [bias], axis=0).astype(BF16)
        copy_out(w).start()
        return 0

    lax.fori_loop(0, N_WIDE, narrow_down, 0)

    def finish(w, _):
        copy_out(w).wait()
        return 0

    lax.fori_loop(0, N_WIDE, finish, 0)


def place_entries(slots, base, mate, far, ids, bias):
    vmem = pl.BlockSpec(memory_space=pltpu.VMEM)
    hbm = pl.BlockSpec(memory_space=pltpu.HBM)
    return pl.pallas_call(
        place_kernel,
        out_shape=jax.ShapeDtypeStruct((N_WIDE, BLOCK, E), BF16),
        in_specs=[pl.BlockSpec(memory_space=pltpu.SMEM)] + [pl.BlockSpec(memory_space=pl.ANY)] * 3 + [vmem] * 2,
        out_specs=hbm,
        scratch_shapes=[
            pltpu.VMEM(base.shape, F32),
            pltpu.VMEM(base.shape, BF16),
            pltpu.VMEM(base.shape, BF16),
            pltpu.VMEM((N_WIDE * CAP + 8, E), F32),
            pltpu.VMEM((N_WIDE, BLOCK, E), BF16),
            pltpu.SemaphoreType.DMA((N_WIDE,)),
            pltpu.SemaphoreType.DMA((3,)),
        ],
        compiler_params=pltpu.CompilerParams(vmem_limit_bytes=VMEM_BYTES),
        cost_estimate=LIGHT,
        name="place_entries",
    )(slots, base, mate, far, ids, bias)


def sums_kernel(
    norm_factor, core_ref, recv_hbm, keep_ref, send_ref, bias_ref, recv_ref, tails, total, left, right, todo, sems
):
    get_tails = pltpu.make_async_copy(recv_hbm.at[:, pl.ds(CAP, TAIL), :], tails, sems.at[0])
    get_values = pltpu.make_async_copy(recv_hbm.at[:, pl.ds(0, CAP), :], recv_ref, sems.at[1])
    get_tails.start()
    get_values.start()
    get_tails.wait()
    lane_rows = lax.broadcasted_iota(jnp.int32, (LO, E), 0)

    n = 0
    for w in range(N_WIDE):
        ids = tails[w].astype(F32)
        ids = ids[0:4, :] + ids[4:8, :]
        halves = jnp.max(jnp.where(ids[2:3, :] > 0.0, 2.0, jnp.where(ids[0:1, :] > 0.0, 1.0, 0.0)))
        todo[n] = 2 * w
        n = n + jnp.where(halves > 0.5, 1, 0)
        todo[n] = 2 * w + 1
        n = n + jnp.where(halves > 1.5, 1, 0)
    for k in range(12):
        todo[n + k] = -1
    total[...] = jnp.zeros_like(total)
    bias_ref[...] = jnp.sum(tails[:, 8:, :].astype(F32), axis=0) * norm_factor
    get_values.wait()

    def build(i, buf):
        for p in range(4):
            item = todo[i * 4 + p]
            w = jnp.maximum(item, 0) // 2
            half = jnp.maximum(item, 0) % 2
            ids = tails[w].astype(F32)
            row = (ids[0:4, :] * 64.0 + ids[4:8, :]).astype(jnp.int32) - 1
            row = jnp.where(half == 0, row[0:2, :], row[2:4, :])
            row = jnp.where(item < 0, -1, row)
            hi = row >> (LO.bit_length() - 1)
            lo = jnp.where(row < 0, -1, row & (LO - 1))
            hi_col = jnp.transpose(jnp.concatenate([hi] * 4, axis=0).astype(F32), (1, 0))
            for j in range(2):
                at = (2 * p + j) * E
                left[buf, :, at : at + E] = jnp.where(lane_rows == lo[j : j + 1, :], 1.0, 0.0).astype(BF16)
                v = recv_ref[w, pl.ds(pl.multiple_of(half * (CAP // 2), CAP // 2) + j * E, E), :]
                own = jnp.broadcast_to(hi_col[:, j : j + 1], (E, E)).astype(BF16)
                for h in range(HI):
                    right[buf, at : at + E, h * E : (h + 1) * E] = jnp.where(own == BF16(h), v, BF16(0))

    build(0, 0)

    def step(i, _):
        for b in range(2):
            build(2 * i + b + 1, 1 - b)
            total[...] += jnp.dot(left[b], right[b], preferred_element_type=F32)
        return 0

    lax.fori_loop(0, (n + 7) // 8, step, 0)
    for k in range(HI // 2):
        for out_ref, half in ((keep_ref, core_ref[0]), (send_ref, 1 - core_ref[0])):
            at = pl.multiple_of((half * (HI // 2) + k) * E, E)
            out_ref[k * LO : (k + 1) * LO, :] = total[:, pl.ds(at, E)].astype(BF16)


def owned_sums(norm_factor, core, recv):
    vmem = pl.BlockSpec(memory_space=pltpu.VMEM)
    return pl.pallas_call(
        functools.partial(sums_kernel, norm_factor),
        out_shape=[jax.ShapeDtypeStruct((N_ROWS // 2, E), BF16)] * 2 + [jax.ShapeDtypeStruct((8, E), F32)],
        in_specs=[pl.BlockSpec(memory_space=pltpu.SMEM), pl.BlockSpec(memory_space=pltpu.HBM)],
        out_specs=[vmem] * 3,
        scratch_shapes=[
            pltpu.VMEM((N_WIDE, CAP, E), BF16),
            pltpu.VMEM((N_WIDE, TAIL, E), BF16),
            pltpu.VMEM((LO, HI * E), F32),
            pltpu.VMEM((2, LO, 2 * CAP), BF16),
            pltpu.VMEM((2, 2 * CAP, HI * E), BF16),
            pltpu.SMEM((2 * N_WIDE + 16,), jnp.int32),
            pltpu.SemaphoreType.DMA((2,)),
        ],
        compiler_params=pltpu.CompilerParams(vmem_limit_bytes=VMEM_BYTES),
        cost_estimate=LIGHT,
        name="owned_sums",
    )(core, recv)


def summed(own, others):
    total = own.astype(F32)
    for other in others:
        total = total + other.astype(F32)
    return total


def own_chunk(a):
    return pl.multiple_of(a * 1024, 1024)


def ring_terms(route, part, embedded, z, y, d):
    if route == 0:
        rows = embedded[:, pl.ds(own_chunk((z + d) % 4), 1024)]
        yield slice(0, 1024), jnp.dot(part, rows, preferred_element_type=F32)
        return
    start = ((y + d) % 4) * 256
    for k in range(4):
        rows = embedded[:, pl.ds(pl.multiple_of(k * 1024 + start, 256), 256)]
        yield slice(k * 256, (k + 1) * 256), jnp.dot(part, rows, preferred_element_type=F32)


def sent_kernel(n_ref, z_ref, y_ref, cot_hbm, embedded_hbm, weight_hbm, *refs):
    parts_hbm, first_hbm, (scaled_hbm, turned_hbm) = refs[:2], refs[2:6], refs[6:8]
    cot, embedded, weight, scaled, turned, parts, first, sems, sems_out = refs[8:]
    n, z, y = n_ref[0], z_ref[0], y_ref[0]

    def columns(q):
        at = pl.ds(own_chunk(n ^ q), 1024)
        return pltpu.make_async_copy(embedded_hbm.at[:, at], embedded.at[:, at], sems.at[q])

    def rows(q):
        at = pl.ds(own_chunk(n ^ q), 1024)
        return pltpu.make_async_copy(weight_hbm.at[at, :], weight.at[q - 2], sems.at[2 + q])

    outs = [(parts.at[q], parts_hbm[q]) for q in range(2)]
    outs += [(first.at[q], first_hbm[q]) for q in range(4)]
    outs += [(scaled, scaled_hbm), (turned, turned_hbm)]
    outs = [pltpu.make_async_copy(src, dst, sems_out.at[k]) for k, (src, dst) in enumerate(outs)]

    get_cot = pltpu.make_async_copy(cot_hbm, cot, sems.at[6])
    get_cot.start()
    columns(0).start()
    rows(3).start()
    get_cot.wait()
    columns(0).wait()
    rows(2).start()
    for q in (1, 2, 3):
        columns(q).start()
    grads = (cot[...].astype(F32) * embedded[:, pl.ds(own_chunk(n), 1024)].astype(F32)).astype(BF16)
    scaled[...] = grads
    outs[6].start()
    rows(3).wait()
    parts[0] = lax.dot_general(scaled[...], weight[1], NT, preferred_element_type=F32).astype(BF16)
    turned[...] = jnp.transpose(grads, (1, 0))
    outs[0].start()
    outs[7].start()
    rows(2).wait()
    parts[1] = lax.dot_general(scaled[...], weight[0], NT, preferred_element_type=F32).astype(BF16)
    outs[1].start()
    for q in (1, 2, 3):
        columns(q).wait()
    for route in range(2):
        low = route * 512
        for at, term in ring_terms(route, turned[low : low + 512, :], embedded, z, y, 2):
            term = term.astype(BF16)
            for way in range(2):
                first[2 * route + way, :256, at] = term[way * 256 : (way + 1) * 256, :]
        for way in range(2):
            q = 2 * route + way
            other = turned[low + (1 - way) * 256 : low + (2 - way) * 256, :]
            for at, term in ring_terms(route, other, embedded, z, y, 3 if way else 1):
                first[q, 256:, at] = term.astype(BF16)
            outs[2 + q].start()
    for copy in outs:
        copy.wait()


def sent_terms(n, z, y, cotangent, embedded, weight):
    hbm = pl.BlockSpec(memory_space=pltpu.HBM)
    smem = pl.BlockSpec(memory_space=pltpu.SMEM)
    samples, width = cotangent.shape
    shape = jax.ShapeDtypeStruct
    full = shape((samples, width), BF16)
    results = pl.pallas_call(
        sent_kernel,
        out_shape=[full] * 2 + [shape((512, 1024), BF16)] * 4 + [full, shape((width, samples), BF16)],
        in_specs=[smem] * 3 + [hbm] * 3,
        out_specs=[hbm] * 8,
        scratch_shapes=[
            pltpu.VMEM(cotangent.shape, BF16),
            pltpu.VMEM(embedded.shape, BF16),
            pltpu.VMEM((2, 1024, 1024), BF16),
            pltpu.VMEM((samples, width), BF16),
            pltpu.VMEM((width, samples), BF16),
            pltpu.VMEM((2, samples, width), BF16),
            pltpu.VMEM((4, 512, 1024), BF16),
            pltpu.SemaphoreType.DMA((7,)),
            pltpu.SemaphoreType.DMA((8,)),
        ],
        compiler_params=pltpu.CompilerParams(vmem_limit_bytes=VMEM_BYTES),
        cost_estimate=LIGHT,
        name="sent_terms",
    )(n, z, y, cotangent, embedded, weight)
    return results[:2], results[2:6], *results[6:]


def pass_kernel(*refs):
    passed_hbm, mine_hbm, sent_hbm, (passed, mine, sent, sems, sems_out) = refs[:4], refs[4:8], refs[8:12], refs[12:]
    loads, outs = [], []
    for q in range(4):
        loads.append(pltpu.make_async_copy(passed_hbm[q].at[pl.ds(0, 256), :], passed.at[q], sems.at[2 * q]))
        loads.append(pltpu.make_async_copy(mine_hbm[q], mine.at[q], sems.at[2 * q + 1]))
        outs.append(pltpu.make_async_copy(sent.at[q], sent_hbm[q], sems_out.at[q]))
    for load in loads:
        load.start()
    for q in range(4):
        loads[2 * q].wait()
        loads[2 * q + 1].wait()
        sent[q] = (passed[q].astype(F32) + mine[q].astype(F32)).astype(BF16)
        outs[q].start()
    for copy in outs:
        copy.wait()


def passed_on(first, second):
    hbm = pl.BlockSpec(memory_space=pltpu.HBM)
    return pl.pallas_call(
        pass_kernel,
        out_shape=[jax.ShapeDtypeStruct((256, 1024), BF16)] * 4,
        in_specs=[pl.BlockSpec(memory_space=pl.ANY)] * 8,
        out_specs=[hbm] * 4,
        scratch_shapes=[
            pltpu.VMEM((4, 256, 1024), BF16),
            pltpu.VMEM((4, 256, 1024), BF16),
            pltpu.VMEM((4, 256, 1024), BF16),
            pltpu.SemaphoreType.DMA((8,)),
            pltpu.SemaphoreType.DMA((4,)),
        ],
        compiler_params=pltpu.CompilerParams(vmem_limit_bytes=VMEM_BYTES),
        cost_estimate=LIGHT,
        name="passed_on",
    )(*first, *second)


def kept_kernel(
    n_ref, z_ref, y_ref, cot_hbm, embedded_hbm, weight_hbm, bias_ref, scaled_hbm, turned_hbm, owner_ref, row_ref, bag_ref, *refs
):
    base_ref, slots_ref, ids_ref, bias_sum_ref, mate_hbm, second_hbm = *refs[:5], refs[5:9]
    cot, embedded, weight, scaled, turned, cross, onehots, mate, second, sems, sems_out = refs[9:]
    n, z, y = n_ref[0], z_ref[0], y_ref[0]

    def columns(q):
        at = pl.ds(own_chunk(n ^ q), 1024)
        return pltpu.make_async_copy(embedded_hbm.at[:, at], embedded.at[:, at], sems.at[q])

    def rows(q):
        at = pl.ds(own_chunk(n ^ q), 1024)
        return pltpu.make_async_copy(weight_hbm.at[at, :], weight.at[q], sems.at[4 + q])

    get_scaled = pltpu.make_async_copy(scaled_hbm, scaled, sems.at[8])
    get_cot = pltpu.make_async_copy(cot_hbm, cot, sems.at[9])
    get_turned = pltpu.make_async_copy(turned_hbm, turned, sems.at[10])
    outs = [(mate, mate_hbm)] + [(second.at[q], second_hbm[q]) for q in range(4)]
    outs = [pltpu.make_async_copy(src, dst, sems_out.at[k]) for k, (src, dst) in enumerate(outs)]
    rows(0).start()
    columns(0).start()
    get_scaled.start()
    for q in (1, 2, 3):
        rows(q).start()
        columns(q).start()
    get_cot.start()
    get_turned.start()
    find_slots(n, owner_ref, row_ref, bag_ref, slots_ref, ids_ref, onehots)
    get_scaled.wait()
    rows(1).wait()
    mate[...] = lax.dot_general(scaled[...], weight[1], NT, preferred_element_type=F32).astype(BF16)
    outs[0].start()
    for q in range(4):
        columns(q).wait()
    get_turned.wait()
    for route in range(2):
        for way in range(2):
            q = 2 * route + way
            low = route * 512 + way * 256
            for at, term in ring_terms(route, turned[low : low + 256, :], embedded, z, y, 3 if way else 1):
                second[q, :, at] = term.astype(BF16)
            outs[1 + q].start()
    sums = jnp.sum(scaled[...].astype(F32), axis=0, keepdims=True)
    bias_sum_ref[...] = jnp.concatenate([sums[:, k * E : (k + 1) * E] for k in range(8)], axis=0)
    rows(0).wait()
    cross[...] = jnp.dot(embedded[:, pl.ds(own_chunk(n), 1024)], weight[0], preferred_element_type=F32)
    base_ref[...] = lax.dot_general(scaled[...], weight[0], NT, preferred_element_type=F32)
    for q in (1, 2):
        if q > 1:
            rows(q).wait()
        cross[...] += jnp.dot(embedded[:, pl.ds(own_chunk(n ^ q), 1024)], weight[q], preferred_element_type=F32)
    rows(3).wait()
    get_cot.wait()
    grad = cot[...].astype(F32)
    last = jnp.dot(embedded[:, pl.ds(own_chunk(n ^ 3), 1024)], weight[3], preferred_element_type=F32)
    base_ref[...] += grad + grad * (cross[...] + last + bias_ref[...])
    for copy in outs:
        copy.wait()


def kept_terms(n, z, y, cotangent, embedded, weight, bias, scaled, turned, owner, row, bag):
    hbm = pl.BlockSpec(memory_space=pltpu.HBM)
    vmem = pl.BlockSpec(memory_space=pltpu.VMEM)
    samples, width = cotangent.shape
    depth = owner.shape[0]
    shape = jax.ShapeDtypeStruct
    results = pl.pallas_call(
        kept_kernel,
        out_shape=[
            shape((samples, width), F32),
            shape((depth * samples // E, E), jnp.int32),
            shape((2 * N_WIDE, CAP), F32),
            shape((8, E), F32),
            shape((samples, width), BF16),
        ]
        + [shape((256, 1024), BF16)] * 4,
        in_specs=[pl.BlockSpec(memory_space=pltpu.SMEM)] * 3 + [hbm] * 3 + [vmem, hbm, hbm] + [vmem] * 3,
        out_specs=[vmem] * 4 + [hbm] * 5,
        scratch_shapes=[
            pltpu.VMEM(cotangent.shape, BF16),
            pltpu.VMEM(embedded.shape, BF16),
            pltpu.VMEM((4, 1024, 1024), BF16),
            pltpu.VMEM((samples, width), BF16),
            pltpu.VMEM((width, samples), BF16),
            pltpu.VMEM((samples, width), F32),
            pltpu.VMEM((N_WIDE * depth, samples), BF16),
            pltpu.VMEM((samples, width), BF16),
            pltpu.VMEM((4, 256, 1024), BF16),
            pltpu.SemaphoreType.DMA((11,)),
            pltpu.SemaphoreType.DMA((5,)),
        ],
        compiler_params=pltpu.CompilerParams(vmem_limit_bytes=VMEM_BYTES),
        cost_estimate=LIGHT,
        name="kept_terms",
    )(n, z, y, cotangent, embedded, weight, bias.reshape(1, -1), scaled, turned, owner, row, bag)
    return *results[:5], results[5:]


def own_kernel(z_ref, y_ref, embedded_hbm, turned_hbm, *refs):
    got_hbm, results, (embedded, turned, got, sems) = refs[:8], refs[8:12], refs[12:]
    z, y = z_ref[0], y_ref[0]
    loads = [(embedded_hbm, embedded), (turned_hbm, turned)]
    loads += [(got_hbm[k].at[pl.ds(256, 256), :], got.at[k]) for k in range(4)]
    loads += [(got_hbm[k], got.at[k]) for k in range(4, 8)]
    loads = [pltpu.make_async_copy(src, dst, sems.at[k]) for k, (src, dst) in enumerate(loads)]
    for load in loads:
        load.start()
    for load in loads:
        load.wait()
    for route, place in ((0, y), (1, z)):
        term = jnp.concatenate([term for _, term in ring_terms(route, turned[route * 512 : (route + 1) * 512, :], embedded, z, y, 0)], axis=1)
        up, down = 2 * route, 2 * route + 1
        total = jnp.concatenate(
            [
                term[:256, :] + got[4 + up].astype(F32) + got[down].astype(F32),
                term[256:, :] + got[4 + down].astype(F32) + got[up].astype(F32),
            ],
            axis=0,
        ).astype(BF16)
        high = place >= 2
        results[2 * route][...] = jnp.where(high, total[:, 512:], total[:, :512])
        results[2 * route + 1][...] = jnp.where(high, total[:, :512], total[:, 512:])


def own_terms(z, y, embedded, turned, first, second):
    hbm = pl.BlockSpec(memory_space=pltpu.HBM)
    vmem = pl.BlockSpec(memory_space=pltpu.VMEM)
    return pl.pallas_call(
        own_kernel,
        out_shape=[jax.ShapeDtypeStruct((512, 512), BF16)] * 4,
        in_specs=[pl.BlockSpec(memory_space=pltpu.SMEM)] * 2 + [hbm] + [pl.BlockSpec(memory_space=pl.ANY)] * 9,
        out_specs=[vmem] * 4,
        scratch_shapes=[
            pltpu.VMEM(embedded.shape, BF16),
            pltpu.VMEM(turned.shape, BF16),
            pltpu.VMEM((8, 256, 1024), BF16),
            pltpu.SemaphoreType.DMA((10,)),
        ],
        compiler_params=pltpu.CompilerParams(vmem_limit_bytes=VMEM_BYTES),
        cost_estimate=LIGHT,
        name="own_terms",
    )(z, y, embedded, turned, *first, *second)


def halves_of(array, bit, axis):
    size = array.shape[axis] // 2
    return (
        lax.dynamic_slice_in_dim(array, bit * size, size, axis),
        lax.dynamic_slice_in_dim(array, (1 - bit) * size, size, axis),
    )


def body(
    embedded,
    cotangent,
    cross_weight,
    cross_bias,
    bag_size,
    row_owner,
    row_id,
    emb_table,
    adagrad_state,
):
    panel = lax.axis_index("narrow")
    wide = lax.axis_index("wide")
    z, y, x_lo = wide // 8, (wide // 2) % 4, wide % 2
    core = panel % 2
    batch_rows = cotangent.shape[0]
    norm_factor = 1.0 / math.sqrt(batch_rows * N_WIDE)

    at = (panel.reshape(1), z.reshape(1), y.reshape(1))

    parts, first, scaled, turned = sent_terms(*at, cotangent, embedded, cross_weight)
    from_mate_far = lax.ppermute(parts[0], "narrow", CORE)
    ways = [z_perm(1), z_perm(3), y_perm(1), y_perm(3)]
    first = [lax.ppermute(first[q], "wide", ways[q]) for q in range(4)]
    chip_far = (parts[1].astype(F32) + from_mate_far.astype(F32)).astype(BF16)
    chip_far, scaled, turned = lax.optimization_barrier((chip_far, scaled, turned))
    far = lax.ppermute(chip_far, "narrow", X_HI)

    entries = (row_owner.reshape(row_owner.shape[1:3]).T, row_id.reshape(row_id.shape[1:]).T, bag_size.T)
    base, slots, ids, bias_part, part, second = kept_terms(
        *at, cotangent, embedded, cross_weight, cross_bias, scaled, turned, *entries
    )
    slots, ids, part, *first = lax.optimization_barrier((slots, ids, part, *first))
    from_mate = lax.ppermute(part, "narrow", CORE)
    second = passed_on(first, second)
    slots, far, *second = lax.optimization_barrier((slots, far, *second))
    second = [lax.ppermute(second[q], "wide", ways[q]) for q in range(4)]

    payload = place_entries(slots.reshape(-1), base, from_mate, far, ids, bias_part)
    payload, *second = lax.optimization_barrier((payload, *second))
    recv = lax.all_to_all(payload, "wide", split_axis=0, concat_axis=0, tiled=True)

    keep_y, send_y, keep_z, send_z = own_terms(at[1], at[2], embedded, turned, first, second)
    recv, send_y, send_z = lax.optimization_barrier((recv, send_y, send_z))
    got = [lax.ppermute(send_y, "wide", y_flip(2)), lax.ppermute(send_z, "wide", z_flip(2))]
    keep, send, bias_sums = owned_sums(norm_factor, core.reshape(1), recv)
    from_core = lax.ppermute(send, "narrow", CORE)
    keep, *got = lax.optimization_barrier((keep, *got))
    quarters = []
    for half, other, place in ((keep_y, got[0], y), (keep_z, got[1], z)):
        quarters.append([part.astype(BF16) for part in halves_of(summed(half, [other]), place % 2, 1)])
    got = [lax.ppermute(quarters[0][1], "wide", y_flip(1)), lax.ppermute(quarters[1][1], "wide", z_flip(1))]
    keep, from_core, *_ = lax.optimization_barrier((keep, from_core, quarters[0][1], quarters[1][1]))
    chip = summed(keep, [from_core]).astype(BF16)
    pair = jnp.concatenate([summed(quarters[0][0], got[:1]), summed(quarters[1][0], got[1:])], axis=0).astype(BF16)
    x_keep, x_send = halves_of(pair, x_lo, 1)
    other_chip, _ = lax.optimization_barrier((lax.ppermute(chip, "narrow", X_HI), x_send))
    x_got = lax.ppermute(jnp.pad(x_send, ((0, 16), (0, 0))), "wide", X_LO)[:1024]

    bias_grad = bias_sums.reshape(-1)
    mine = summed(chip, [other_chip]).astype(BF16)
    mate, x_got = lax.optimization_barrier((lax.ppermute(mine, "narrow", CORE), x_got))
    weight_grad = summed(x_keep, [x_got]).T * norm_factor
    row_grad = jnp.concatenate([jnp.where(core == 0, mine, mate), jnp.where(core == 0, mate, mine)], axis=0).astype(F32)
    new_state = adagrad_state + jnp.mean(row_grad * row_grad, axis=1)
    new_table = emb_table - LEARN_RATE * row_grad / jnp.sqrt(new_state)[:, None]
    return (weight_grad, bias_grad, new_table, new_state)


def solution(mesh):
    in_specs = (
        P("wide", None),
        P("wide", "narrow"),
        P(None, "narrow"),
        P("narrow"),
        P("wide", None),
        P("narrow", "wide", None, None),
        P("narrow", "wide", None),
        P("wide", None),
        P("wide"),
    )
    out_specs = (P("wide", "narrow"), P("narrow"), P("wide", None), P("wide"))
    return jax.shard_map(body, mesh=mesh, in_specs=in_specs, out_specs=out_specs, check_vma=False)
```

```python
import functools
import math

import jax
import jax.numpy as jnp
from jax import lax
from jax.experimental import pallas as pl
from jax.experimental.pallas import tpu as pltpu
from jax.sharding import PartitionSpec as P

LEARN_RATE = 0.3
E = 128
N_WIDE = 32
CAP = 512
TAIL = 16
BLOCK = CAP + TAIL
N_ROWS = 2048
HI = 4
LO = N_ROWS // HI
F32 = jnp.float32
BF16 = jnp.bfloat16
LIGHT = pl.CostEstimate(flops=1, bytes_accessed=1, transcendentals=0)
NT = (((1,), (1,)), ((), ()))


def z_perm(d):
    return [(i, ((i // 8 + d) % 4) * 8 + i % 8) for i in range(N_WIDE)]


def y_perm(d):
    return [(i, (i // 8) * 8 + (((i // 2) % 4 + d) % 4) * 2 + i % 2) for i in range(N_WIDE)]


def y_flip(m):
    return [(i, i ^ (2 * m)) for i in range(N_WIDE)]


def z_flip(m):
    return [(i, i ^ (8 * m)) for i in range(N_WIDE)]


X_LO = [(i, i ^ 1) for i in range(N_WIDE)]
CORE = [(i, i ^ 1) for i in range(4)]
X_HI = [(i, i ^ 2) for i in range(4)]


def find_slots(panel, owner_ref, row_ref, bag_ref, slots_ref, ids_ref, onehots):
    depth, samples = owner_ref.shape
    feats = depth // 2
    bag = bag_ref[pl.ds(pl.multiple_of(panel * feats, feats), feats), :]
    bag = jnp.concatenate([bag[k // 2 : k // 2 + 1, :] for k in range(depth)], axis=0)
    live = (lax.broadcasted_iota(jnp.int32, (depth, samples), 0) & 1) < bag
    owner = jnp.where(live, owner_ref[...], N_WIDE)
    for t in range(N_WIDE):
        onehots[t * depth : (t + 1) * depth, :] = jnp.where(owner == t, 1.0, 0.0).astype(BF16)

    size = N_WIDE * depth
    first = lax.broadcasted_iota(jnp.int32, (samples, samples), 0)
    second = lax.broadcasted_iota(jnp.int32, (samples, samples), 1)
    before = jnp.where(first < second, 1.0, 0.0).astype(BF16)
    within = jnp.dot(onehots[...], before, preferred_element_type=F32)
    in_row = jnp.dot(onehots[...], jnp.ones((samples, E), BF16), preferred_element_type=F32)
    top = jnp.floor(in_row * (1.0 / 16.0))
    low = (in_row - 16.0 * top).astype(BF16)
    top = top.astype(BF16)
    r = lax.broadcasted_iota(jnp.int32, (size, size), 0)
    c = lax.broadcasted_iota(jnp.int32, (size, size), 1)
    shift = depth.bit_length() - 1
    earlier = jnp.where((r >> shift == c >> shift) & (c < r), 1.0, 0.0).astype(BF16)
    rows_before = 16.0 * jnp.dot(earlier, top, preferred_element_type=F32) + jnp.dot(
        earlier, low, preferred_element_type=F32
    )
    place = jnp.zeros((depth, samples), F32)
    for t in range(N_WIDE):
        at = slice(t * depth, (t + 1) * depth)
        ahead = jnp.concatenate([rows_before[at, :]] * (samples // E), axis=1)
        place = place + jnp.where(owner == t, within[at, :] + ahead, 0.0)
    place = place.astype(jnp.int32)
    slots = jnp.where(live, owner * CAP + place, N_WIDE * CAP)
    for k in range(samples // E):
        slots_ref[k * depth : (k + 1) * depth, :] = slots[:, k * E : (k + 1) * E]

    marked = row_ref[...] + 1
    top = (marked >> 6).astype(F32)
    low = (marked & 63).astype(F32)
    owners = lax.broadcasted_iota(jnp.int32, (N_WIDE, samples), 0)
    places = lax.broadcasted_iota(jnp.int32, (CAP, samples), 0)
    ids = jnp.zeros((2 * N_WIDE, CAP), F32)
    for k in range(depth):
        at = slice(k, k + 1)
        mine = owners == owner[at, :]
        marks = jnp.concatenate([jnp.where(mine, top[at, :], 0.0), jnp.where(mine, low[at, :], 0.0)], axis=0)
        there = jnp.where(places == place[at, :], 1.0, 0.0).astype(BF16)
        ids = ids + lax.dot_general(
            marks.astype(BF16), there, (((1,), (1,)), ((), ())), preferred_element_type=F32
        )
    ids_ref[...] = ids


def place_kernel(
    slots_ref, base_hbm, mate_hbm, far_hbm, ids_ref, bias_ref, out_ref, base, mate, far, rows, blocks, sems, sems_in
):
    depth = 16
    dump = N_WIDE * CAP
    loads = [
        pltpu.make_async_copy(src, dst, sems_in.at[k])
        for k, (src, dst) in enumerate(((base_hbm, base), (mate_hbm, mate), (far_hbm, far)))
    ]
    for load in loads:
        load.start()

    def clear(i, _):
        rows[pl.ds(pl.multiple_of(i * 256, 256), 256), :] = jnp.zeros((256, E), F32)
        return 0

    lax.fori_loop(0, dump // 256, clear, 0)
    for load in loads:
        load.wait()

    def place(i, _):
        first = pl.multiple_of(i * 16, 16)
        at = (first // E) * (depth * E) + first % E
        for f in range(8):
            cols = slice(f * E, (f + 1) * E)
            tile = base[pl.ds(first, 16), cols] + (
                mate[pl.ds(first, 16), cols].astype(F32) + far[pl.ds(first, 16), cols].astype(F32)
            )
            for b in range(16):
                row = tile[b : b + 1, :]
                for j in range(2):
                    slot = slots_ref[at + (2 * f + j) * E + b]
                    rows[pl.ds(slot, 1), :] = row
        return 0

    lax.fori_loop(0, base.shape[0] // 16, place, 0)

    bias = bias_ref[...]

    def copy_out(w):
        return pltpu.make_async_copy(blocks.at[w], out_ref.at[w], sems.at[w])

    def narrow_down(w, _):
        blocks[w, :CAP, :] = rows[pl.ds(pl.multiple_of(w * CAP, CAP), CAP), :].astype(BF16)
        top = ids_ref[pl.ds(w, 1), :]
        low = ids_ref[pl.ds(N_WIDE + w, 1), :]
        parts = [top[:, k * E : (k + 1) * E] for k in range(4)] + [low[:, k * E : (k + 1) * E] for k in range(4)]
        blocks[w, CAP:, :] = jnp.concatenate(parts + [bias], axis=0).astype(BF16)
        copy_out(w).start()
        return 0

    lax.fori_loop(0, N_WIDE, narrow_down, 0)

    def finish(w, _):
        copy_out(w).wait()
        return 0

    lax.fori_loop(0, N_WIDE, finish, 0)


def place_entries(slots, base, mate, far, ids, bias):
    vmem = pl.BlockSpec(memory_space=pltpu.VMEM)
    hbm = pl.BlockSpec(memory_space=pltpu.HBM)
    return pl.pallas_call(
        place_kernel,
        out_shape=jax.ShapeDtypeStruct((N_WIDE, BLOCK, E), BF16),
        in_specs=[pl.BlockSpec(memory_space=pltpu.SMEM)] + [pl.BlockSpec(memory_space=pl.ANY)] * 3 + [vmem] * 2,
        out_specs=hbm,
        scratch_shapes=[
            pltpu.VMEM(base.shape, F32),
            pltpu.VMEM(base.shape, BF16),
            pltpu.VMEM(base.shape, BF16),
            pltpu.VMEM((N_WIDE * CAP + 8, E), F32),
            pltpu.VMEM((N_WIDE, BLOCK, E), BF16),
            pltpu.SemaphoreType.DMA((N_WIDE,)),
            pltpu.SemaphoreType.DMA((3,)),
        ],
        compiler_params=pltpu.CompilerParams(vmem_limit_bytes=28 << 20),
        cost_estimate=LIGHT,
        name="place_entries",
    )(slots, base, mate, far, ids, bias)


def sums_kernel(
    norm_factor, core_ref, recv_hbm, keep_ref, send_ref, bias_ref, recv_ref, tails, total, left, right, todo, sems
):
    get_tails = pltpu.make_async_copy(recv_hbm.at[:, pl.ds(CAP, TAIL), :], tails, sems.at[0])
    get_values = pltpu.make_async_copy(recv_hbm.at[:, pl.ds(0, CAP), :], recv_ref, sems.at[1])
    get_tails.start()
    get_values.start()
    get_tails.wait()
    lane_rows = lax.broadcasted_iota(jnp.int32, (LO, E), 0)

    n = 0
    for w in range(N_WIDE):
        ids = tails[w].astype(F32)
        ids = ids[0:4, :] + ids[4:8, :]
        halves = jnp.max(jnp.where(ids[2:3, :] > 0.0, 2.0, jnp.where(ids[0:1, :] > 0.0, 1.0, 0.0)))
        todo[n] = 2 * w
        n = n + jnp.where(halves > 0.5, 1, 0)
        todo[n] = 2 * w + 1
        n = n + jnp.where(halves > 1.5, 1, 0)
    for k in range(12):
        todo[n + k] = -1
    total[...] = jnp.zeros_like(total)
    bias_ref[...] = jnp.sum(tails[:, 8:, :].astype(F32), axis=0) * norm_factor
    get_values.wait()

    def build(i, buf):
        for p in range(4):
            item = todo[i * 4 + p]
            w = jnp.maximum(item, 0) // 2
            half = jnp.maximum(item, 0) % 2
            ids = tails[w].astype(F32)
            row = (ids[0:4, :] * 64.0 + ids[4:8, :]).astype(jnp.int32) - 1
            row = jnp.where(half == 0, row[0:2, :], row[2:4, :])
            row = jnp.where(item < 0, -1, row)
            hi = row >> (LO.bit_length() - 1)
            lo = jnp.where(row < 0, -1, row & (LO - 1))
            hi_col = jnp.transpose(jnp.concatenate([hi] * 4, axis=0).astype(F32), (1, 0))
            for j in range(2):
                at = (2 * p + j) * E
                left[buf, :, at : at + E] = jnp.where(lane_rows == lo[j : j + 1, :], 1.0, 0.0).astype(BF16)
                v = recv_ref[w, pl.ds(pl.multiple_of(half * (CAP // 2), CAP // 2) + j * E, E), :]
                own = jnp.broadcast_to(hi_col[:, j : j + 1], (E, E)).astype(BF16)
                for h in range(HI):
                    right[buf, at : at + E, h * E : (h + 1) * E] = jnp.where(own == BF16(h), v, BF16(0))

    build(0, 0)

    def step(i, _):
        for b in range(2):
            build(2 * i + b + 1, 1 - b)
            total[...] += jnp.dot(left[b], right[b], preferred_element_type=F32)
        return 0

    lax.fori_loop(0, (n + 7) // 8, step, 0)
    for k in range(HI // 2):
        for out_ref, half in ((keep_ref, core_ref[0]), (send_ref, 1 - core_ref[0])):
            at = pl.multiple_of((half * (HI // 2) + k) * E, E)
            out_ref[k * LO : (k + 1) * LO, :] = total[:, pl.ds(at, E)].astype(BF16)


def owned_sums(norm_factor, core, recv):
    vmem = pl.BlockSpec(memory_space=pltpu.VMEM)
    return pl.pallas_call(
        functools.partial(sums_kernel, norm_factor),
        out_shape=[jax.ShapeDtypeStruct((N_ROWS // 2, E), BF16)] * 2 + [jax.ShapeDtypeStruct((8, E), F32)],
        in_specs=[pl.BlockSpec(memory_space=pltpu.SMEM), pl.BlockSpec(memory_space=pltpu.HBM)],
        out_specs=[vmem] * 3,
        scratch_shapes=[
            pltpu.VMEM((N_WIDE, CAP, E), BF16),
            pltpu.VMEM((N_WIDE, TAIL, E), BF16),
            pltpu.VMEM((LO, HI * E), F32),
            pltpu.VMEM((2, LO, 2 * CAP), BF16),
            pltpu.VMEM((2, 2 * CAP, HI * E), BF16),
            pltpu.SMEM((2 * N_WIDE + 16,), jnp.int32),
            pltpu.SemaphoreType.DMA((2,)),
        ],
        compiler_params=pltpu.CompilerParams(vmem_limit_bytes=24 << 20),
        cost_estimate=LIGHT,
        name="owned_sums",
    )(core, recv)


def summed(own, others):
    total = own.astype(F32)
    for other in others:
        total = total + other.astype(F32)
    return total


def own_chunk(a):
    return pl.multiple_of(a * 1024, 1024)


def ring_terms(route, part, embedded, z, y, d):
    if route == 0:
        rows = embedded[:, pl.ds(own_chunk((z + d) % 4), 1024)]
        yield slice(0, 1024), jnp.dot(part, rows, preferred_element_type=F32)
        return
    start = ((y + d) % 4) * 256
    for k in range(4):
        rows = embedded[:, pl.ds(pl.multiple_of(k * 1024 + start, 256), 256)]
        yield slice(k * 256, (k + 1) * 256), jnp.dot(part, rows, preferred_element_type=F32)


def sent_kernel(n_ref, z_ref, y_ref, cot_hbm, embedded_hbm, weight_hbm, *refs):
    parts_hbm, first_hbm, (scaled_hbm, turned_hbm) = refs[:2], refs[2:6], refs[6:8]
    cot, embedded, weight, scaled, turned, parts, first, sems, sems_out = refs[8:]
    n, z, y = n_ref[0], z_ref[0], y_ref[0]

    def columns(q):
        at = pl.ds(own_chunk(n ^ q), 1024)
        return pltpu.make_async_copy(embedded_hbm.at[:, at], embedded.at[:, at], sems.at[q])

    def rows(q):
        at = pl.ds(own_chunk(n ^ q), 1024)
        return pltpu.make_async_copy(weight_hbm.at[at, :], weight.at[q - 2], sems.at[2 + q])

    outs = [(parts.at[q], parts_hbm[q]) for q in range(2)]
    outs += [(first.at[q], first_hbm[q]) for q in range(4)]
    outs += [(scaled, scaled_hbm), (turned, turned_hbm)]
    outs = [pltpu.make_async_copy(src, dst, sems_out.at[k]) for k, (src, dst) in enumerate(outs)]

    get_cot = pltpu.make_async_copy(cot_hbm, cot, sems.at[6])
    get_cot.start()
    columns(0).start()
    rows(3).start()
    get_cot.wait()
    columns(0).wait()
    rows(2).start()
    for q in (1, 2, 3):
        columns(q).start()
    grads = (cot[...].astype(F32) * embedded[:, pl.ds(own_chunk(n), 1024)].astype(F32)).astype(BF16)
    scaled[...] = grads
    outs[6].start()
    rows(3).wait()
    parts[0] = lax.dot_general(scaled[...], weight[1], NT, preferred_element_type=F32).astype(BF16)
    turned[...] = jnp.transpose(grads, (1, 0))
    outs[0].start()
    outs[7].start()
    rows(2).wait()
    parts[1] = lax.dot_general(scaled[...], weight[0], NT, preferred_element_type=F32).astype(BF16)
    outs[1].start()
    for q in (1, 2, 3):
        columns(q).wait()
    for route in range(2):
        low = route * 512
        for at, term in ring_terms(route, turned[low : low + 512, :], embedded, z, y, 2):
            term = term.astype(BF16)
            for way in range(2):
                first[2 * route + way, :256, at] = term[way * 256 : (way + 1) * 256, :]
        for way in range(2):
            q = 2 * route + way
            other = turned[low + (1 - way) * 256 : low + (2 - way) * 256, :]
            for at, term in ring_terms(route, other, embedded, z, y, 3 if way else 1):
                first[q, 256:, at] = term.astype(BF16)
            outs[2 + q].start()
    for copy in outs:
        copy.wait()


def sent_terms(n, z, y, cotangent, embedded, weight):
    hbm = pl.BlockSpec(memory_space=pltpu.HBM)
    smem = pl.BlockSpec(memory_space=pltpu.SMEM)
    samples, width = cotangent.shape
    shape = jax.ShapeDtypeStruct
    full = shape((samples, width), BF16)
    results = pl.pallas_call(
        sent_kernel,
        out_shape=[full] * 2 + [shape((512, 1024), BF16)] * 4 + [full, shape((width, samples), BF16)],
        in_specs=[smem] * 3 + [hbm] * 3,
        out_specs=[hbm] * 8,
        scratch_shapes=[
            pltpu.VMEM(cotangent.shape, BF16),
            pltpu.VMEM(embedded.shape, BF16),
            pltpu.VMEM((2, 1024, 1024), BF16),
            pltpu.VMEM((samples, width), BF16),
            pltpu.VMEM((width, samples), BF16),
            pltpu.VMEM((2, samples, width), BF16),
            pltpu.VMEM((4, 512, 1024), BF16),
            pltpu.SemaphoreType.DMA((7,)),
            pltpu.SemaphoreType.DMA((8,)),
        ],
        compiler_params=pltpu.CompilerParams(vmem_limit_bytes=60 << 20),
        cost_estimate=LIGHT,
        name="sent_terms",
    )(n, z, y, cotangent, embedded, weight)
    return results[:2], results[2:6], *results[6:]


def pass_kernel(*refs):
    passed_hbm, mine_hbm, sent_hbm, (passed, mine, sent, sems, sems_out) = refs[:4], refs[4:8], refs[8:12], refs[12:]
    loads, outs = [], []
    for q in range(4):
        loads.append(pltpu.make_async_copy(passed_hbm[q].at[pl.ds(0, 256), :], passed.at[q], sems.at[2 * q]))
        loads.append(pltpu.make_async_copy(mine_hbm[q], mine.at[q], sems.at[2 * q + 1]))
        outs.append(pltpu.make_async_copy(sent.at[q], sent_hbm[q], sems_out.at[q]))
    for load in loads:
        load.start()
    for q in range(4):
        loads[2 * q].wait()
        loads[2 * q + 1].wait()
        sent[q] = (passed[q].astype(F32) + mine[q].astype(F32)).astype(BF16)
        outs[q].start()
    for copy in outs:
        copy.wait()


def passed_on(first, second):
    hbm = pl.BlockSpec(memory_space=pltpu.HBM)
    return pl.pallas_call(
        pass_kernel,
        out_shape=[jax.ShapeDtypeStruct((256, 1024), BF16)] * 4,
        in_specs=[pl.BlockSpec(memory_space=pl.ANY)] * 8,
        out_specs=[hbm] * 4,
        scratch_shapes=[
            pltpu.VMEM((4, 256, 1024), BF16),
            pltpu.VMEM((4, 256, 1024), BF16),
            pltpu.VMEM((4, 256, 1024), BF16),
            pltpu.SemaphoreType.DMA((8,)),
            pltpu.SemaphoreType.DMA((4,)),
        ],
        compiler_params=pltpu.CompilerParams(vmem_limit_bytes=14 << 20),
        cost_estimate=LIGHT,
        name="passed_on",
    )(*first, *second)


def kept_kernel(
    n_ref, z_ref, y_ref, cot_hbm, embedded_hbm, weight_hbm, bias_ref, scaled_hbm, turned_hbm, owner_ref, row_ref, bag_ref, *refs
):
    base_ref, slots_ref, ids_ref, bias_sum_ref, mate_hbm, second_hbm = *refs[:5], refs[5:9]
    cot, embedded, weight, scaled, turned, cross, onehots, mate, second, sems, sems_out = refs[9:]
    n, z, y = n_ref[0], z_ref[0], y_ref[0]

    def columns(q):
        at = pl.ds(own_chunk(n ^ q), 1024)
        return pltpu.make_async_copy(embedded_hbm.at[:, at], embedded.at[:, at], sems.at[q])

    def rows(q):
        at = pl.ds(own_chunk(n ^ q), 1024)
        return pltpu.make_async_copy(weight_hbm.at[at, :], weight.at[q], sems.at[4 + q])

    get_scaled = pltpu.make_async_copy(scaled_hbm, scaled, sems.at[8])
    get_cot = pltpu.make_async_copy(cot_hbm, cot, sems.at[9])
    get_turned = pltpu.make_async_copy(turned_hbm, turned, sems.at[10])
    outs = [(mate, mate_hbm)] + [(second.at[q], second_hbm[q]) for q in range(4)]
    outs = [pltpu.make_async_copy(src, dst, sems_out.at[k]) for k, (src, dst) in enumerate(outs)]
    rows(0).start()
    columns(0).start()
    get_scaled.start()
    for q in (1, 2, 3):
        rows(q).start()
        columns(q).start()
    get_cot.start()
    get_turned.start()
    find_slots(n, owner_ref, row_ref, bag_ref, slots_ref, ids_ref, onehots)
    get_scaled.wait()
    rows(1).wait()
    mate[...] = lax.dot_general(scaled[...], weight[1], NT, preferred_element_type=F32).astype(BF16)
    outs[0].start()
    for q in range(4):
        columns(q).wait()
    get_turned.wait()
    for route in range(2):
        for way in range(2):
            q = 2 * route + way
            low = route * 512 + way * 256
            for at, term in ring_terms(route, turned[low : low + 256, :], embedded, z, y, 3 if way else 1):
                second[q, :, at] = term.astype(BF16)
            outs[1 + q].start()
    sums = jnp.sum(scaled[...].astype(F32), axis=0, keepdims=True)
    bias_sum_ref[...] = jnp.concatenate([sums[:, k * E : (k + 1) * E] for k in range(8)], axis=0)
    rows(0).wait()
    cross[...] = jnp.dot(embedded[:, pl.ds(own_chunk(n), 1024)], weight[0], preferred_element_type=F32)
    base_ref[...] = lax.dot_general(scaled[...], weight[0], NT, preferred_element_type=F32)
    for q in (1, 2):
        if q > 1:
            rows(q).wait()
        cross[...] += jnp.dot(embedded[:, pl.ds(own_chunk(n ^ q), 1024)], weight[q], preferred_element_type=F32)
    rows(3).wait()
    get_cot.wait()
    grad = cot[...].astype(F32)
    last = jnp.dot(embedded[:, pl.ds(own_chunk(n ^ 3), 1024)], weight[3], preferred_element_type=F32)
    base_ref[...] += grad + grad * (cross[...] + last + bias_ref[...])
    for copy in outs:
        copy.wait()


def kept_terms(n, z, y, cotangent, embedded, weight, bias, scaled, turned, owner, row, bag):
    hbm = pl.BlockSpec(memory_space=pltpu.HBM)
    vmem = pl.BlockSpec(memory_space=pltpu.VMEM)
    samples, width = cotangent.shape
    depth = owner.shape[0]
    shape = jax.ShapeDtypeStruct
    results = pl.pallas_call(
        kept_kernel,
        out_shape=[
            shape((samples, width), F32),
            shape((depth * samples // E, E), jnp.int32),
            shape((2 * N_WIDE, CAP), F32),
            shape((8, E), F32),
            shape((samples, width), BF16),
        ]
        + [shape((256, 1024), BF16)] * 4,
        in_specs=[pl.BlockSpec(memory_space=pltpu.SMEM)] * 3 + [hbm] * 3 + [vmem, hbm, hbm] + [vmem] * 3,
        out_specs=[vmem] * 4 + [hbm] * 5,
        scratch_shapes=[
            pltpu.VMEM(cotangent.shape, BF16),
            pltpu.VMEM(embedded.shape, BF16),
            pltpu.VMEM((4, 1024, 1024), BF16),
            pltpu.VMEM((samples, width), BF16),
            pltpu.VMEM((width, samples), BF16),
            pltpu.VMEM((samples, width), F32),
            pltpu.VMEM((N_WIDE * depth, samples), BF16),
            pltpu.VMEM((samples, width), BF16),
            pltpu.VMEM((4, 256, 1024), BF16),
            pltpu.SemaphoreType.DMA((11,)),
            pltpu.SemaphoreType.DMA((5,)),
        ],
        compiler_params=pltpu.CompilerParams(vmem_limit_bytes=58 << 20),
        cost_estimate=LIGHT,
        name="kept_terms",
    )(n, z, y, cotangent, embedded, weight, bias.reshape(1, -1), scaled, turned, owner, row, bag)
    return *results[:5], results[5:]


def own_kernel(z_ref, y_ref, embedded_hbm, turned_hbm, *refs):
    got_hbm, results, (embedded, turned, got, sems) = refs[:8], refs[8:12], refs[12:]
    z, y = z_ref[0], y_ref[0]
    loads = [(embedded_hbm, embedded), (turned_hbm, turned)]
    loads += [(got_hbm[k].at[pl.ds(256, 256), :], got.at[k]) for k in range(4)]
    loads += [(got_hbm[k], got.at[k]) for k in range(4, 8)]
    loads = [pltpu.make_async_copy(src, dst, sems.at[k]) for k, (src, dst) in enumerate(loads)]
    for load in loads:
        load.start()
    for load in loads:
        load.wait()
    for route, place in ((0, y), (1, z)):
        term = jnp.concatenate([term for _, term in ring_terms(route, turned[route * 512 : (route + 1) * 512, :], embedded, z, y, 0)], axis=1)
        up, down = 2 * route, 2 * route + 1
        total = jnp.concatenate(
            [
                term[:256, :] + got[4 + up].astype(F32) + got[down].astype(F32),
                term[256:, :] + got[4 + down].astype(F32) + got[up].astype(F32),
            ],
            axis=0,
        ).astype(BF16)
        high = place >= 2
        results[2 * route][...] = jnp.where(high, total[:, 512:], total[:, :512])
        results[2 * route + 1][...] = jnp.where(high, total[:, :512], total[:, 512:])


def own_terms(z, y, embedded, turned, first, second):
    hbm = pl.BlockSpec(memory_space=pltpu.HBM)
    vmem = pl.BlockSpec(memory_space=pltpu.VMEM)
    return pl.pallas_call(
        own_kernel,
        out_shape=[jax.ShapeDtypeStruct((512, 512), BF16)] * 4,
        in_specs=[pl.BlockSpec(memory_space=pltpu.SMEM)] * 2 + [hbm] + [pl.BlockSpec(memory_space=pl.ANY)] * 9,
        out_specs=[vmem] * 4,
        scratch_shapes=[
            pltpu.VMEM(embedded.shape, BF16),
            pltpu.VMEM(turned.shape, BF16),
            pltpu.VMEM((8, 256, 1024), BF16),
            pltpu.SemaphoreType.DMA((10,)),
        ],
        compiler_params=pltpu.CompilerParams(vmem_limit_bytes=30 << 20),
        cost_estimate=LIGHT,
        name="own_terms",
    )(z, y, embedded, turned, *first, *second)


def halves_of(array, bit, axis):
    size = array.shape[axis] // 2
    return (
        lax.dynamic_slice_in_dim(array, bit * size, size, axis),
        lax.dynamic_slice_in_dim(array, (1 - bit) * size, size, axis),
    )


def body(
    embedded,
    cotangent,
    cross_weight,
    cross_bias,
    bag_size,
    row_owner,
    row_id,
    emb_table,
    adagrad_state,
):
    panel = lax.axis_index("narrow")
    wide = lax.axis_index("wide")
    z, y, x_lo = wide // 8, (wide // 2) % 4, wide % 2
    core = panel % 2
    batch_rows = cotangent.shape[0]
    norm_factor = 1.0 / math.sqrt(batch_rows * N_WIDE)

    at = (panel.reshape(1), z.reshape(1), y.reshape(1))

    parts, first, scaled, turned = sent_terms(*at, cotangent, embedded, cross_weight)
    from_mate_far = lax.ppermute(parts[0], "narrow", CORE)
    ways = [z_perm(1), z_perm(3), y_perm(1), y_perm(3)]
    first = [lax.ppermute(first[q], "wide", ways[q]) for q in range(4)]
    chip_far = (parts[1].astype(F32) + from_mate_far.astype(F32)).astype(BF16)
    chip_far, scaled, turned = lax.optimization_barrier((chip_far, scaled, turned))
    far = lax.ppermute(chip_far, "narrow", X_HI)

    entries = (row_owner.reshape(row_owner.shape[1:3]).T, row_id.reshape(row_id.shape[1:]).T, bag_size.T)
    base, slots, ids, bias_part, part, second = kept_terms(
        *at, cotangent, embedded, cross_weight, cross_bias, scaled, turned, *entries
    )
    slots, ids, part, *first = lax.optimization_barrier((slots, ids, part, *first))
    from_mate = lax.ppermute(part, "narrow", CORE)
    second = passed_on(first, second)
    slots, far, *second = lax.optimization_barrier((slots, far, *second))
    second = [lax.ppermute(second[q], "wide", ways[q]) for q in range(4)]

    payload = place_entries(slots.reshape(-1), base, from_mate, far, ids, bias_part)
    payload, *second = lax.optimization_barrier((payload, *second))
    recv = lax.all_to_all(payload, "wide", split_axis=0, concat_axis=0, tiled=True)

    keep_y, send_y, keep_z, send_z = own_terms(at[1], at[2], embedded, turned, first, second)
    recv, send_y, send_z = lax.optimization_barrier((recv, send_y, send_z))
    got = [lax.ppermute(send_y, "wide", y_flip(2)), lax.ppermute(send_z, "wide", z_flip(2))]
    keep, send, bias_sums = owned_sums(norm_factor, core.reshape(1), recv)
    from_core = lax.ppermute(send, "narrow", CORE)
    keep, *got = lax.optimization_barrier((keep, *got))
    quarters = []
    for half, other, place in ((keep_y, got[0], y), (keep_z, got[1], z)):
        quarters.append([part.astype(BF16) for part in halves_of(summed(half, [other]), place % 2, 1)])
    got = [lax.ppermute(quarters[0][1], "wide", y_flip(1)), lax.ppermute(quarters[1][1], "wide", z_flip(1))]
    keep, from_core, *_ = lax.optimization_barrier((keep, from_core, quarters[0][1], quarters[1][1]))
    chip = summed(keep, [from_core]).astype(BF16)
    pair = jnp.concatenate([summed(quarters[0][0], got[:1]), summed(quarters[1][0], got[1:])], axis=0).astype(BF16)
    x_keep, x_send = halves_of(pair, x_lo, 1)
    other_chip, _ = lax.optimization_barrier((lax.ppermute(chip, "narrow", X_HI), x_send))
    x_got = lax.ppermute(jnp.pad(x_send, ((0, 16), (0, 0))), "wide", X_LO)[:1024]

    bias_grad = bias_sums.reshape(-1)
    mine = summed(chip, [other_chip]).astype(BF16)
    mate, x_got = lax.optimization_barrier((lax.ppermute(mine, "narrow", CORE), x_got))
    weight_grad = summed(x_keep, [x_got]).T * norm_factor
    row_grad = jnp.concatenate([jnp.where(core == 0, mine, mate), jnp.where(core == 0, mate, mine)], axis=0).astype(F32)
    new_state = adagrad_state + jnp.mean(row_grad * row_grad, axis=1)
    new_table = emb_table - LEARN_RATE * row_grad / jnp.sqrt(new_state)[:, None]
    return (weight_grad, bias_grad, new_table, new_state)


def solution(mesh):
    in_specs = (
        P("wide", None),
        P("wide", "narrow"),
        P(None, "narrow"),
        P("narrow"),
        P("wide", None),
        P("narrow", "wide", None, None),
        P("narrow", "wide", None),
        P("wide", None),
        P("wide"),
    )
    out_specs = (P("wide", "narrow"), P("narrow"), P("wide", None), P("wide"))
    return jax.shard_map(body, mesh=mesh, in_specs=in_specs, out_specs=out_specs, check_vma=False)
```

```python
import functools
import math

import jax
import jax.numpy as jnp
from jax import lax
from jax.experimental import pallas as pl
from jax.experimental.pallas import tpu as pltpu
from jax.sharding import PartitionSpec as P

LEARN_RATE = 0.3
E = 128
N_WIDE = 32
CAP = 512
TAIL = 16
BLOCK = CAP + TAIL
N_ROWS = 2048
HI = 4
LO = N_ROWS // HI
F32 = jnp.float32
BF16 = jnp.bfloat16
LIGHT = pl.CostEstimate(flops=1, bytes_accessed=1, transcendentals=0)
VMEM_BYTES = 56 << 20
VMEM_MOST = 63 << 20
NT = (((1,), (1,)), ((), ()))


def z_perm(d):
    return [(i, ((i // 8 + d) % 4) * 8 + i % 8) for i in range(N_WIDE)]


def y_perm(d):
    return [(i, (i // 8) * 8 + (((i // 2) % 4 + d) % 4) * 2 + i % 2) for i in range(N_WIDE)]


def y_flip(m):
    return [(i, i ^ (2 * m)) for i in range(N_WIDE)]


def z_flip(m):
    return [(i, i ^ (8 * m)) for i in range(N_WIDE)]


X_LO = [(i, i ^ 1) for i in range(N_WIDE)]
CORE = [(i, i ^ 1) for i in range(4)]
X_HI = [(i, i ^ 2) for i in range(4)]


def find_slots(panel, owner_ref, row_ref, bag_ref, slots_ref, ids_ref, onehots):
    depth, samples = owner_ref.shape
    feats = depth // 2
    bag = bag_ref[pl.ds(pl.multiple_of(panel * feats, feats), feats), :]
    bag = jnp.concatenate([bag[k // 2 : k // 2 + 1, :] for k in range(depth)], axis=0)
    live = (lax.broadcasted_iota(jnp.int32, (depth, samples), 0) & 1) < bag
    owner = jnp.where(live, owner_ref[...], N_WIDE)
    for t in range(N_WIDE):
        onehots[t * depth : (t + 1) * depth, :] = jnp.where(owner == t, 1.0, 0.0).astype(BF16)

    size = N_WIDE * depth
    first = lax.broadcasted_iota(jnp.int32, (samples, samples), 0)
    second = lax.broadcasted_iota(jnp.int32, (samples, samples), 1)
    before = jnp.where(first < second, 1.0, 0.0).astype(BF16)
    within = jnp.dot(onehots[...], before, preferred_element_type=F32)
    in_row = jnp.dot(onehots[...], jnp.ones((samples, E), BF16), preferred_element_type=F32)
    top = jnp.floor(in_row * (1.0 / 16.0))
    low = (in_row - 16.0 * top).astype(BF16)
    top = top.astype(BF16)
    r = lax.broadcasted_iota(jnp.int32, (size, size), 0)
    c = lax.broadcasted_iota(jnp.int32, (size, size), 1)
    shift = depth.bit_length() - 1
    earlier = jnp.where((r >> shift == c >> shift) & (c < r), 1.0, 0.0).astype(BF16)
    rows_before = 16.0 * jnp.dot(earlier, top, preferred_element_type=F32) + jnp.dot(
        earlier, low, preferred_element_type=F32
    )
    place = jnp.zeros((depth, samples), F32)
    for t in range(N_WIDE):
        at = slice(t * depth, (t + 1) * depth)
        ahead = jnp.concatenate([rows_before[at, :]] * (samples // E), axis=1)
        place = place + jnp.where(owner == t, within[at, :] + ahead, 0.0)
    place = place.astype(jnp.int32)
    slots = jnp.where(live, owner * CAP + place, N_WIDE * CAP)
    for k in range(samples // E):
        slots_ref[k * depth : (k + 1) * depth, :] = slots[:, k * E : (k + 1) * E]

    marked = row_ref[...] + 1
    top = (marked >> 6).astype(F32)
    low = (marked & 63).astype(F32)
    owners = lax.broadcasted_iota(jnp.int32, (N_WIDE, samples), 0)
    places = lax.broadcasted_iota(jnp.int32, (CAP, samples), 0)
    ids = jnp.zeros((2 * N_WIDE, CAP), F32)
    for k in range(depth):
        at = slice(k, k + 1)
        mine = owners == owner[at, :]
        marks = jnp.concatenate([jnp.where(mine, top[at, :], 0.0), jnp.where(mine, low[at, :], 0.0)], axis=0)
        there = jnp.where(places == place[at, :], 1.0, 0.0).astype(BF16)
        ids = ids + lax.dot_general(
            marks.astype(BF16), there, (((1,), (1,)), ((), ())), preferred_element_type=F32
        )
    ids_ref[...] = ids


def place_kernel(
    slots_ref, base_hbm, mate_hbm, far_hbm, ids_ref, bias_ref, out_ref, base, mate, far, rows, blocks, sems, sems_in
):
    depth = 16
    dump = N_WIDE * CAP
    loads = [
        pltpu.make_async_copy(src, dst, sems_in.at[k])
        for k, (src, dst) in enumerate(((base_hbm, base), (mate_hbm, mate), (far_hbm, far)))
    ]
    for load in loads:
        load.start()

    def clear(i, _):
        rows[pl.ds(pl.multiple_of(i * 256, 256), 256), :] = jnp.zeros((256, E), F32)
        return 0

    lax.fori_loop(0, dump // 256, clear, 0)
    for load in loads:
        load.wait()

    def place(i, _):
        first = pl.multiple_of(i * 16, 16)
        at = (first // E) * (depth * E) + first % E
        for f in range(8):
            cols = slice(f * E, (f + 1) * E)
            tile = base[pl.ds(first, 16), cols] + (
                mate[pl.ds(first, 16), cols].astype(F32) + far[pl.ds(first, 16), cols].astype(F32)
            )
            for b in range(16):
                row = tile[b : b + 1, :]
                for j in range(2):
                    slot = slots_ref[at + (2 * f + j) * E + b]
                    rows[pl.ds(slot, 1), :] = row
        return 0

    lax.fori_loop(0, base.shape[0] // 16, place, 0)

    bias = bias_ref[...]

    def copy_out(w):
        return pltpu.make_async_copy(blocks.at[w], out_ref.at[w], sems.at[w])

    def narrow_down(w, _):
        blocks[w, :CAP, :] = rows[pl.ds(pl.multiple_of(w * CAP, CAP), CAP), :].astype(BF16)
        top = ids_ref[pl.ds(w, 1), :]
        low = ids_ref[pl.ds(N_WIDE + w, 1), :]
        parts = [top[:, k * E : (k + 1) * E] for k in range(4)] + [low[:, k * E : (k + 1) * E] for k in range(4)]
        blocks[w, CAP:, :] = jnp.concatenate(parts + [bias], axis=0).astype(BF16)
        copy_out(w).start()
        return 0

    lax.fori_loop(0, N_WIDE, narrow_down, 0)

    def finish(w, _):
        copy_out(w).wait()
        return 0

    lax.fori_loop(0, N_WIDE, finish, 0)


def place_entries(slots, base, mate, far, ids, bias):
    vmem = pl.BlockSpec(memory_space=pltpu.VMEM)
    hbm = pl.BlockSpec(memory_space=pltpu.HBM)
    return pl.pallas_call(
        place_kernel,
        out_shape=jax.ShapeDtypeStruct((N_WIDE, BLOCK, E), BF16),
        in_specs=[pl.BlockSpec(memory_space=pltpu.SMEM)] + [pl.BlockSpec(memory_space=pl.ANY)] * 3 + [vmem] * 2,
        out_specs=hbm,
        scratch_shapes=[
            pltpu.VMEM(base.shape, F32),
            pltpu.VMEM(base.shape, BF16),
            pltpu.VMEM(base.shape, BF16),
            pltpu.VMEM((N_WIDE * CAP + 8, E), F32),
            pltpu.VMEM((N_WIDE, BLOCK, E), BF16),
            pltpu.SemaphoreType.DMA((N_WIDE,)),
            pltpu.SemaphoreType.DMA((3,)),
        ],
        compiler_params=pltpu.CompilerParams(vmem_limit_bytes=VMEM_MOST),
        cost_estimate=LIGHT,
        name="place_entries",
    )(slots, base, mate, far, ids, bias)


def sums_kernel(
    norm_factor, core_ref, recv_hbm, keep_ref, send_ref, bias_ref, recv_ref, tails, total, left, right, todo, sems
):
    get_tails = pltpu.make_async_copy(recv_hbm.at[:, pl.ds(CAP, TAIL), :], tails, sems.at[0])
    get_values = pltpu.make_async_copy(recv_hbm.at[:, pl.ds(0, CAP), :], recv_ref, sems.at[1])
    get_tails.start()
    get_values.start()
    get_tails.wait()
    lane_rows = lax.broadcasted_iota(jnp.int32, (LO, E), 0)

    n = 0
    for w in range(N_WIDE):
        ids = tails[w].astype(F32)
        ids = ids[0:4, :] + ids[4:8, :]
        halves = jnp.max(jnp.where(ids[2:3, :] > 0.0, 2.0, jnp.where(ids[0:1, :] > 0.0, 1.0, 0.0)))
        todo[n] = 2 * w
        n = n + jnp.where(halves > 0.5, 1, 0)
        todo[n] = 2 * w + 1
        n = n + jnp.where(halves > 1.5, 1, 0)
    for k in range(12):
        todo[n + k] = -1
    total[...] = jnp.zeros_like(total)
    bias_ref[...] = jnp.sum(tails[:, 8:, :].astype(F32), axis=0) * norm_factor
    get_values.wait()

    def build(i, buf):
        for p in range(4):
            item = todo[i * 4 + p]
            w = jnp.maximum(item, 0) // 2
            half = jnp.maximum(item, 0) % 2
            ids = tails[w].astype(F32)
            row = (ids[0:4, :] * 64.0 + ids[4:8, :]).astype(jnp.int32) - 1
            row = jnp.where(half == 0, row[0:2, :], row[2:4, :])
            row = jnp.where(item < 0, -1, row)
            hi = row >> (LO.bit_length() - 1)
            lo = jnp.where(row < 0, -1, row & (LO - 1))
            hi_col = jnp.transpose(jnp.concatenate([hi] * 4, axis=0).astype(F32), (1, 0))
            for j in range(2):
                at = (2 * p + j) * E
                left[buf, :, at : at + E] = jnp.where(lane_rows == lo[j : j + 1, :], 1.0, 0.0).astype(BF16)
                v = recv_ref[w, pl.ds(pl.multiple_of(half * (CAP // 2), CAP // 2) + j * E, E), :]
                own = jnp.broadcast_to(hi_col[:, j : j + 1], (E, E)).astype(BF16)
                for h in range(HI):
                    right[buf, at : at + E, h * E : (h + 1) * E] = jnp.where(own == BF16(h), v, BF16(0))

    build(0, 0)

    def step(i, _):
        for b in range(2):
            build(2 * i + b + 1, 1 - b)
            total[...] += jnp.dot(left[b], right[b], preferred_element_type=F32)
        return 0

    lax.fori_loop(0, (n + 7) // 8, step, 0)
    for k in range(HI // 2):
        for out_ref, half in ((keep_ref, core_ref[0]), (send_ref, 1 - core_ref[0])):
            at = pl.multiple_of((half * (HI // 2) + k) * E, E)
            out_ref[k * LO : (k + 1) * LO, :] = total[:, pl.ds(at, E)].astype(BF16)


def owned_sums(norm_factor, core, recv):
    vmem = pl.BlockSpec(memory_space=pltpu.VMEM)
    return pl.pallas_call(
        functools.partial(sums_kernel, norm_factor),
        out_shape=[jax.ShapeDtypeStruct((N_ROWS // 2, E), BF16)] * 2 + [jax.ShapeDtypeStruct((8, E), F32)],
        in_specs=[pl.BlockSpec(memory_space=pltpu.SMEM), pl.BlockSpec(memory_space=pltpu.HBM)],
        out_specs=[vmem] * 3,
        scratch_shapes=[
            pltpu.VMEM((N_WIDE, CAP, E), BF16),
            pltpu.VMEM((N_WIDE, TAIL, E), BF16),
            pltpu.VMEM((LO, HI * E), F32),
            pltpu.VMEM((2, LO, 2 * CAP), BF16),
            pltpu.VMEM((2, 2 * CAP, HI * E), BF16),
            pltpu.SMEM((2 * N_WIDE + 16,), jnp.int32),
            pltpu.SemaphoreType.DMA((2,)),
        ],
        compiler_params=pltpu.CompilerParams(vmem_limit_bytes=VMEM_BYTES),
        cost_estimate=LIGHT,
        name="owned_sums",
    )(core, recv)


def summed(own, others):
    total = own.astype(F32)
    for other in others:
        total = total + other.astype(F32)
    return total


def own_chunk(a):
    return pl.multiple_of(a * 1024, 1024)


def ring_terms(route, part, embedded, z, y, d):
    if route == 0:
        rows = embedded[:, pl.ds(own_chunk((z + d) % 4), 1024)]
        yield slice(0, 1024), jnp.dot(part, rows, preferred_element_type=F32)
        return
    start = ((y + d) % 4) * 256
    for k in range(4):
        rows = embedded[:, pl.ds(pl.multiple_of(k * 1024 + start, 256), 256)]
        yield slice(k * 256, (k + 1) * 256), jnp.dot(part, rows, preferred_element_type=F32)


def sent_kernel(n_ref, z_ref, y_ref, cot_hbm, embedded_hbm, weight_hbm, *refs):
    parts_hbm, first_hbm, (scaled_hbm, turned_hbm) = refs[:2], refs[2:6], refs[6:8]
    cot, embedded, weight, scaled, turned, parts, first, sems, sems_out = refs[8:]
    n, z, y = n_ref[0], z_ref[0], y_ref[0]

    def columns(q):
        at = pl.ds(own_chunk(n ^ q), 1024)
        return pltpu.make_async_copy(embedded_hbm.at[:, at], embedded.at[:, at], sems.at[q])

    def rows(q):
        at = pl.ds(own_chunk(n ^ q), 1024)
        return pltpu.make_async_copy(weight_hbm.at[at, :], weight.at[q - 2], sems.at[2 + q])

    outs = [(parts.at[q], parts_hbm[q]) for q in range(2)]
    outs += [(first.at[q], first_hbm[q]) for q in range(4)]
    outs += [(scaled, scaled_hbm), (turned, turned_hbm)]
    outs = [pltpu.make_async_copy(src, dst, sems_out.at[k]) for k, (src, dst) in enumerate(outs)]

    get_cot = pltpu.make_async_copy(cot_hbm, cot, sems.at[6])
    get_cot.start()
    columns(0).start()
    rows(3).start()
    get_cot.wait()
    columns(0).wait()
    rows(2).start()
    for q in (1, 2, 3):
        columns(q).start()
    grads = (cot[...].astype(F32) * embedded[:, pl.ds(own_chunk(n), 1024)].astype(F32)).astype(BF16)
    scaled[...] = grads
    outs[6].start()
    rows(3).wait()
    parts[0] = lax.dot_general(scaled[...], weight[1], NT, preferred_element_type=F32).astype(BF16)
    turned[...] = jnp.transpose(grads, (1, 0))
    outs[0].start()
    outs[7].start()
    rows(2).wait()
    parts[1] = lax.dot_general(scaled[...], weight[0], NT, preferred_element_type=F32).astype(BF16)
    outs[1].start()
    for q in (1, 2, 3):
        columns(q).wait()
    for route in range(2):
        low = route * 512
        for at, term in ring_terms(route, turned[low : low + 512, :], embedded, z, y, 2):
            term = term.astype(BF16)
            for way in range(2):
                first[2 * route + way, :256, at] = term[way * 256 : (way + 1) * 256, :]
        for way in range(2):
            q = 2 * route + way
            other = turned[low + (1 - way) * 256 : low + (2 - way) * 256, :]
            for at, term in ring_terms(route, other, embedded, z, y, 3 if way else 1):
                first[q, 256:, at] = term.astype(BF16)
            outs[2 + q].start()
    for copy in outs:
        copy.wait()


def sent_terms(n, z, y, cotangent, embedded, weight):
    hbm = pl.BlockSpec(memory_space=pltpu.HBM)
    smem = pl.BlockSpec(memory_space=pltpu.SMEM)
    samples, width = cotangent.shape
    shape = jax.ShapeDtypeStruct
    full = shape((samples, width), BF16)
    results = pl.pallas_call(
        sent_kernel,
        out_shape=[full] * 2 + [shape((512, 1024), BF16)] * 4 + [full, shape((width, samples), BF16)],
        in_specs=[smem] * 3 + [hbm] * 3,
        out_specs=[hbm] * 8,
        scratch_shapes=[
            pltpu.VMEM(cotangent.shape, BF16),
            pltpu.VMEM(embedded.shape, BF16),
            pltpu.VMEM((2, 1024, 1024), BF16),
            pltpu.VMEM((samples, width), BF16),
            pltpu.VMEM((width, samples), BF16),
            pltpu.VMEM((2, samples, width), BF16),
            pltpu.VMEM((4, 512, 1024), BF16),
            pltpu.SemaphoreType.DMA((7,)),
            pltpu.SemaphoreType.DMA((8,)),
        ],
        compiler_params=pltpu.CompilerParams(vmem_limit_bytes=VMEM_MOST),
        cost_estimate=LIGHT,
        name="sent_terms",
    )(n, z, y, cotangent, embedded, weight)
    return results[:2], results[2:6], *results[6:]


def pass_kernel(*refs):
    passed_hbm, mine_hbm, sent_hbm, (passed, mine, sent, sems, sems_out) = refs[:4], refs[4:8], refs[8:12], refs[12:]
    loads, outs = [], []
    for q in range(4):
        loads.append(pltpu.make_async_copy(passed_hbm[q].at[pl.ds(0, 256), :], passed.at[q], sems.at[2 * q]))
        loads.append(pltpu.make_async_copy(mine_hbm[q], mine.at[q], sems.at[2 * q + 1]))
        outs.append(pltpu.make_async_copy(sent.at[q], sent_hbm[q], sems_out.at[q]))
    for load in loads:
        load.start()
    for q in range(4):
        loads[2 * q].wait()
        loads[2 * q + 1].wait()
        sent[q] = (passed[q].astype(F32) + mine[q].astype(F32)).astype(BF16)
        outs[q].start()
    for copy in outs:
        copy.wait()


def passed_on(first, second):
    hbm = pl.BlockSpec(memory_space=pltpu.HBM)
    return pl.pallas_call(
        pass_kernel,
        out_shape=[jax.ShapeDtypeStruct((256, 1024), BF16)] * 4,
        in_specs=[pl.BlockSpec(memory_space=pl.ANY)] * 8,
        out_specs=[hbm] * 4,
        scratch_shapes=[
            pltpu.VMEM((4, 256, 1024), BF16),
            pltpu.VMEM((4, 256, 1024), BF16),
            pltpu.VMEM((4, 256, 1024), BF16),
            pltpu.SemaphoreType.DMA((8,)),
            pltpu.SemaphoreType.DMA((4,)),
        ],
        compiler_params=pltpu.CompilerParams(vmem_limit_bytes=VMEM_MOST),
        cost_estimate=LIGHT,
        name="passed_on",
    )(*first, *second)


def kept_kernel(
    n_ref, z_ref, y_ref, cot_hbm, embedded_hbm, weight_hbm, bias_ref, scaled_hbm, turned_hbm, owner_ref, row_ref, bag_ref, *refs
):
    base_ref, slots_ref, ids_ref, bias_sum_ref, mate_hbm, second_hbm = *refs[:5], refs[5:9]
    cot, embedded, weight, scaled, turned, cross, onehots, mate, second, sems, sems_out = refs[9:]
    n, z, y = n_ref[0], z_ref[0], y_ref[0]

    def columns(q):
        at = pl.ds(own_chunk(n ^ q), 1024)
        return pltpu.make_async_copy(embedded_hbm.at[:, at], embedded.at[:, at], sems.at[q])

    def rows(q):
        at = pl.ds(own_chunk(n ^ q), 1024)
        return pltpu.make_async_copy(weight_hbm.at[at, :], weight.at[q], sems.at[4 + q])

    get_scaled = pltpu.make_async_copy(scaled_hbm, scaled, sems.at[8])
    get_cot = pltpu.make_async_copy(cot_hbm, cot, sems.at[9])
    get_turned = pltpu.make_async_copy(turned_hbm, turned, sems.at[10])
    outs = [(mate, mate_hbm)] + [(second.at[q], second_hbm[q]) for q in range(4)]
    outs = [pltpu.make_async_copy(src, dst, sems_out.at[k]) for k, (src, dst) in enumerate(outs)]
    rows(0).start()
    columns(0).start()
    get_scaled.start()
    for q in (1, 2, 3):
        rows(q).start()
        columns(q).start()
    get_cot.start()
    get_turned.start()
    find_slots(n, owner_ref, row_ref, bag_ref, slots_ref, ids_ref, onehots)
    get_scaled.wait()
    rows(1).wait()
    mate[...] = lax.dot_general(scaled[...], weight[1], NT, preferred_element_type=F32).astype(BF16)
    outs[0].start()
    for q in range(4):
        columns(q).wait()
    get_turned.wait()
    for route in range(2):
        for way in range(2):
            q = 2 * route + way
            low = route * 512 + way * 256
            for at, term in ring_terms(route, turned[low : low + 256, :], embedded, z, y, 3 if way else 1):
                second[q, :, at] = term.astype(BF16)
            outs[1 + q].start()
    sums = jnp.sum(scaled[...].astype(F32), axis=0, keepdims=True)
    bias_sum_ref[...] = jnp.concatenate([sums[:, k * E : (k + 1) * E] for k in range(8)], axis=0)
    rows(0).wait()
    cross[...] = jnp.dot(embedded[:, pl.ds(own_chunk(n), 1024)], weight[0], preferred_element_type=F32)
    base_ref[...] = lax.dot_general(scaled[...], weight[0], NT, preferred_element_type=F32)
    for q in (1, 2):
        if q > 1:
            rows(q).wait()
        cross[...] += jnp.dot(embedded[:, pl.ds(own_chunk(n ^ q), 1024)], weight[q], preferred_element_type=F32)
    rows(3).wait()
    get_cot.wait()
    grad = cot[...].astype(F32)
    last = jnp.dot(embedded[:, pl.ds(own_chunk(n ^ 3), 1024)], weight[3], preferred_element_type=F32)
    base_ref[...] += grad + grad * (cross[...] + last + bias_ref[...])
    for copy in outs:
        copy.wait()


def kept_terms(n, z, y, cotangent, embedded, weight, bias, scaled, turned, owner, row, bag):
    hbm = pl.BlockSpec(memory_space=pltpu.HBM)
    vmem = pl.BlockSpec(memory_space=pltpu.VMEM)
    samples, width = cotangent.shape
    depth = owner.shape[0]
    shape = jax.ShapeDtypeStruct
    results = pl.pallas_call(
        kept_kernel,
        out_shape=[
            shape((samples, width), F32),
            shape((depth * samples // E, E), jnp.int32),
            shape((2 * N_WIDE, CAP), F32),
            shape((8, E), F32),
            shape((samples, width), BF16),
        ]
        + [shape((256, 1024), BF16)] * 4,
        in_specs=[pl.BlockSpec(memory_space=pltpu.SMEM)] * 3 + [hbm] * 3 + [vmem, hbm, hbm] + [vmem] * 3,
        out_specs=[vmem] * 4 + [hbm] * 5,
        scratch_shapes=[
            pltpu.VMEM(cotangent.shape, BF16),
            pltpu.VMEM(embedded.shape, BF16),
            pltpu.VMEM((4, 1024, 1024), BF16),
            pltpu.VMEM((samples, width), BF16),
            pltpu.VMEM((width, samples), BF16),
            pltpu.VMEM((samples, width), F32),
            pltpu.VMEM((N_WIDE * depth, samples), BF16),
            pltpu.VMEM((samples, width), BF16),
            pltpu.VMEM((4, 256, 1024), BF16),
            pltpu.SemaphoreType.DMA((11,)),
            pltpu.SemaphoreType.DMA((5,)),
        ],
        compiler_params=pltpu.CompilerParams(vmem_limit_bytes=VMEM_MOST),
        cost_estimate=LIGHT,
        name="kept_terms",
    )(n, z, y, cotangent, embedded, weight, bias.reshape(1, -1), scaled, turned, owner, row, bag)
    return *results[:5], results[5:]


def own_kernel(z_ref, y_ref, embedded_hbm, turned_hbm, *refs):
    got_hbm, results, (embedded, turned, got, sems) = refs[:8], refs[8:12], refs[12:]
    z, y = z_ref[0], y_ref[0]
    loads = [(embedded_hbm, embedded), (turned_hbm, turned)]
    loads += [(got_hbm[k].at[pl.ds(256, 256), :], got.at[k]) for k in range(4)]
    loads += [(got_hbm[k], got.at[k]) for k in range(4, 8)]
    loads = [pltpu.make_async_copy(src, dst, sems.at[k]) for k, (src, dst) in enumerate(loads)]
    for load in loads:
        load.start()
    for load in loads:
        load.wait()
    for route, place in ((0, y), (1, z)):
        term = jnp.concatenate([term for _, term in ring_terms(route, turned[route * 512 : (route + 1) * 512, :], embedded, z, y, 0)], axis=1)
        up, down = 2 * route, 2 * route + 1
        total = jnp.concatenate(
            [
                term[:256, :] + got[4 + up].astype(F32) + got[down].astype(F32),
                term[256:, :] + got[4 + down].astype(F32) + got[up].astype(F32),
            ],
            axis=0,
        ).astype(BF16)
        high = place >= 2
        results[2 * route][...] = jnp.where(high, total[:, 512:], total[:, :512])
        results[2 * route + 1][...] = jnp.where(high, total[:, :512], total[:, 512:])


def own_terms(z, y, embedded, turned, first, second):
    hbm = pl.BlockSpec(memory_space=pltpu.HBM)
    vmem = pl.BlockSpec(memory_space=pltpu.VMEM)
    return pl.pallas_call(
        own_kernel,
        out_shape=[jax.ShapeDtypeStruct((512, 512), BF16)] * 4,
        in_specs=[pl.BlockSpec(memory_space=pltpu.SMEM)] * 2 + [hbm] + [pl.BlockSpec(memory_space=pl.ANY)] * 9,
        out_specs=[vmem] * 4,
        scratch_shapes=[
            pltpu.VMEM(embedded.shape, BF16),
            pltpu.VMEM(turned.shape, BF16),
            pltpu.VMEM((8, 256, 1024), BF16),
            pltpu.SemaphoreType.DMA((10,)),
        ],
        compiler_params=pltpu.CompilerParams(vmem_limit_bytes=VMEM_BYTES),
        cost_estimate=LIGHT,
        name="own_terms",
    )(z, y, embedded, turned, *first, *second)


def halves_of(array, bit, axis):
    size = array.shape[axis] // 2
    return (
        lax.dynamic_slice_in_dim(array, bit * size, size, axis),
        lax.dynamic_slice_in_dim(array, (1 - bit) * size, size, axis),
    )


def body(
    embedded,
    cotangent,
    cross_weight,
    cross_bias,
    bag_size,
    row_owner,
    row_id,
    emb_table,
    adagrad_state,
):
    panel = lax.axis_index("narrow")
    wide = lax.axis_index("wide")
    z, y, x_lo = wide // 8, (wide // 2) % 4, wide % 2
    core = panel % 2
    batch_rows = cotangent.shape[0]
    norm_factor = 1.0 / math.sqrt(batch_rows * N_WIDE)

    at = (panel.reshape(1), z.reshape(1), y.reshape(1))

    parts, first, scaled, turned = sent_terms(*at, cotangent, embedded, cross_weight)
    from_mate_far = lax.ppermute(parts[0], "narrow", CORE)
    ways = [z_perm(1), z_perm(3), y_perm(1), y_perm(3)]
    first = [lax.ppermute(first[q], "wide", ways[q]) for q in range(4)]
    chip_far = (parts[1].astype(F32) + from_mate_far.astype(F32)).astype(BF16)
    chip_far, scaled, turned = lax.optimization_barrier((chip_far, scaled, turned))
    far = lax.ppermute(chip_far, "narrow", X_HI)

    entries = (row_owner.reshape(row_owner.shape[1:3]).T, row_id.reshape(row_id.shape[1:]).T, bag_size.T)
    base, slots, ids, bias_part, part, second = kept_terms(
        *at, cotangent, embedded, cross_weight, cross_bias, scaled, turned, *entries
    )
    slots, ids, part, *first = lax.optimization_barrier((slots, ids, part, *first))
    from_mate = lax.ppermute(part, "narrow", CORE)
    second = passed_on(first, second)
    slots, far, *second = lax.optimization_barrier((slots, far, *second))
    second = [lax.ppermute(second[q], "wide", ways[q]) for q in range(4)]

    payload = place_entries(slots.reshape(-1), base, from_mate, far, ids, bias_part)
    payload, *second = lax.optimization_barrier((payload, *second))
    recv = lax.all_to_all(payload, "wide", split_axis=0, concat_axis=0, tiled=True)

    keep_y, send_y, keep_z, send_z = own_terms(at[1], at[2], embedded, turned, first, second)
    recv, send_y, send_z = lax.optimization_barrier((recv, send_y, send_z))
    got = [lax.ppermute(send_y, "wide", y_flip(2)), lax.ppermute(send_z, "wide", z_flip(2))]
    keep, send, bias_sums = owned_sums(norm_factor, core.reshape(1), recv)
    from_core = lax.ppermute(send, "narrow", CORE)
    keep, *got = lax.optimization_barrier((keep, *got))
    quarters = []
    for half, other, place in ((keep_y, got[0], y), (keep_z, got[1], z)):
        quarters.append([part.astype(BF16) for part in halves_of(summed(half, [other]), place % 2, 1)])
    got = [lax.ppermute(quarters[0][1], "wide", y_flip(1)), lax.ppermute(quarters[1][1], "wide", z_flip(1))]
    keep, from_core, *_ = lax.optimization_barrier((keep, from_core, quarters[0][1], quarters[1][1]))
    chip = summed(keep, [from_core]).astype(BF16)
    pair = jnp.concatenate([summed(quarters[0][0], got[:1]), summed(quarters[1][0], got[1:])], axis=0).astype(BF16)
    x_keep, x_send = halves_of(pair, x_lo, 1)
    other_chip, _ = lax.optimization_barrier((lax.ppermute(chip, "narrow", X_HI), x_send))
    x_got = lax.ppermute(jnp.pad(x_send, ((0, 16), (0, 0))), "wide", X_LO)[:1024]

    bias_grad = bias_sums.reshape(-1)
    mine = summed(chip, [other_chip]).astype(BF16)
    mate, x_got = lax.optimization_barrier((lax.ppermute(mine, "narrow", CORE), x_got))
    weight_grad = summed(x_keep, [x_got]).T * norm_factor
    row_grad = jnp.concatenate([jnp.where(core == 0, mine, mate), jnp.where(core == 0, mate, mine)], axis=0).astype(F32)
    new_state = adagrad_state + jnp.mean(row_grad * row_grad, axis=1)
    new_table = emb_table - LEARN_RATE * row_grad / jnp.sqrt(new_state)[:, None]
    return (weight_grad, bias_grad, new_table, new_state)


def solution(mesh):
    in_specs = (
        P("wide", None),
        P("wide", "narrow"),
        P(None, "narrow"),
        P("narrow"),
        P("wide", None),
        P("narrow", "wide", None, None),
        P("narrow", "wide", None),
        P("wide", None),
        P("wide"),
    )
    out_specs = (P("wide", "narrow"), P("narrow"), P("wide", None), P("wide"))
    return jax.shard_map(body, mesh=mesh, in_specs=in_specs, out_specs=out_specs, check_vma=False)
```

```python
import functools
import math

import jax
import jax.numpy as jnp
from jax import lax
from jax.experimental import pallas as pl
from jax.experimental.pallas import tpu as pltpu
from jax.sharding import PartitionSpec as P

LEARN_RATE = 0.3
E = 128
N_WIDE = 32
CAP = 512
TAIL = 16
BLOCK = CAP + TAIL
N_ROWS = 2048
HI = 4
LO = N_ROWS // HI
F32 = jnp.float32
BF16 = jnp.bfloat16
LIGHT = pl.CostEstimate(flops=1, bytes_accessed=1, transcendentals=0)
VMEM_BYTES = 56 << 20
VMEM_MOST = 63 << 20
NT = (((1,), (1,)), ((), ()))


def z_perm(d):
    return [(i, ((i // 8 + d) % 4) * 8 + i % 8) for i in range(N_WIDE)]


def y_perm(d):
    return [(i, (i // 8) * 8 + (((i // 2) % 4 + d) % 4) * 2 + i % 2) for i in range(N_WIDE)]


def y_flip(m):
    return [(i, i ^ (2 * m)) for i in range(N_WIDE)]


def z_flip(m):
    return [(i, i ^ (8 * m)) for i in range(N_WIDE)]


X_LO = [(i, i ^ 1) for i in range(N_WIDE)]
CORE = [(i, i ^ 1) for i in range(4)]
X_HI = [(i, i ^ 2) for i in range(4)]


def find_slots(panel, owner_ref, row_ref, bag_ref, slots_ref, ids_ref, onehots):
    depth, samples = owner_ref.shape
    feats = depth // 2
    bag = bag_ref[pl.ds(pl.multiple_of(panel * feats, feats), feats), :]
    bag = jnp.concatenate([bag[k // 2 : k // 2 + 1, :] for k in range(depth)], axis=0)
    live = (lax.broadcasted_iota(jnp.int32, (depth, samples), 0) & 1) < bag
    owner = jnp.where(live, owner_ref[...], N_WIDE)
    for t in range(N_WIDE):
        onehots[t * depth : (t + 1) * depth, :] = jnp.where(owner == t, 1.0, 0.0).astype(BF16)

    size = N_WIDE * depth
    first = lax.broadcasted_iota(jnp.int32, (samples, samples), 0)
    second = lax.broadcasted_iota(jnp.int32, (samples, samples), 1)
    before = jnp.where(first < second, 1.0, 0.0).astype(BF16)
    within = jnp.dot(onehots[...], before, preferred_element_type=F32)
    in_row = jnp.dot(onehots[...], jnp.ones((samples, E), BF16), preferred_element_type=F32)
    top = jnp.floor(in_row * (1.0 / 16.0))
    low = (in_row - 16.0 * top).astype(BF16)
    top = top.astype(BF16)
    r = lax.broadcasted_iota(jnp.int32, (size, size), 0)
    c = lax.broadcasted_iota(jnp.int32, (size, size), 1)
    shift = depth.bit_length() - 1
    earlier = jnp.where((r >> shift == c >> shift) & (c < r), 1.0, 0.0).astype(BF16)
    rows_before = 16.0 * jnp.dot(earlier, top, preferred_element_type=F32) + jnp.dot(
        earlier, low, preferred_element_type=F32
    )
    place = jnp.zeros((depth, samples), F32)
    for t in range(N_WIDE):
        at = slice(t * depth, (t + 1) * depth)
        ahead = jnp.concatenate([rows_before[at, :]] * (samples // E), axis=1)
        place = place + jnp.where(owner == t, within[at, :] + ahead, 0.0)
    place = place.astype(jnp.int32)
    slots = jnp.where(live, owner * CAP + place, N_WIDE * CAP)
    for k in range(samples // E):
        slots_ref[k * depth : (k + 1) * depth, :] = slots[:, k * E : (k + 1) * E]

    marked = row_ref[...] + 1
    top = (marked >> 6).astype(F32)
    low = (marked & 63).astype(F32)
    owners = lax.broadcasted_iota(jnp.int32, (N_WIDE, samples), 0)
    places = lax.broadcasted_iota(jnp.int32, (CAP, samples), 0)
    ids = jnp.zeros((2 * N_WIDE, CAP), F32)
    for k in range(depth):
        at = slice(k, k + 1)
        mine = owners == owner[at, :]
        marks = jnp.concatenate([jnp.where(mine, top[at, :], 0.0), jnp.where(mine, low[at, :], 0.0)], axis=0)
        there = jnp.where(places == place[at, :], 1.0, 0.0).astype(BF16)
        ids = ids + lax.dot_general(
            marks.astype(BF16), there, (((1,), (1,)), ((), ())), preferred_element_type=F32
        )
    ids_ref[...] = ids


def place_kernel(
    slots_ref, base_hbm, mate_hbm, far_hbm, ids_ref, bias_ref, out_ref, base, mate, far, rows, blocks, sems, sems_in
):
    depth = 16
    dump = N_WIDE * CAP
    loads = [
        pltpu.make_async_copy(src, dst, sems_in.at[k])
        for k, (src, dst) in enumerate(((base_hbm, base), (mate_hbm, mate), (far_hbm, far)))
    ]
    for load in loads:
        load.start()

    def clear(i, _):
        rows[pl.ds(pl.multiple_of(i * 256, 256), 256), :] = jnp.zeros((256, E), F32)
        return 0

    lax.fori_loop(0, dump // 256, clear, 0)
    for load in loads:
        load.wait()

    def place(i, _):
        first = pl.multiple_of(i * 16, 16)
        at = (first // E) * (depth * E) + first % E
        for f in range(8):
            cols = slice(f * E, (f + 1) * E)
            tile = base[pl.ds(first, 16), cols] + (
                mate[pl.ds(first, 16), cols].astype(F32) + far[pl.ds(first, 16), cols].astype(F32)
            )
            for b in range(16):
                row = tile[b : b + 1, :]
                for j in range(2):
                    slot = slots_ref[at + (2 * f + j) * E + b]
                    rows[pl.ds(slot, 1), :] = row
        return 0

    lax.fori_loop(0, base.shape[0] // 16, place, 0)

    bias = bias_ref[...]

    def copy_out(w):
        return pltpu.make_async_copy(blocks.at[w], out_ref.at[w], sems.at[w])

    def narrow_down(w, _):
        blocks[w, :CAP, :] = rows[pl.ds(pl.multiple_of(w * CAP, CAP), CAP), :].astype(BF16)
        top = ids_ref[pl.ds(w, 1), :]
        low = ids_ref[pl.ds(N_WIDE + w, 1), :]
        parts = [top[:, k * E : (k + 1) * E] for k in range(4)] + [low[:, k * E : (k + 1) * E] for k in range(4)]
        blocks[w, CAP:, :] = jnp.concatenate(parts + [bias], axis=0).astype(BF16)
        copy_out(w).start()
        return 0

    lax.fori_loop(0, N_WIDE, narrow_down, 0)

    def finish(w, _):
        copy_out(w).wait()
        return 0

    lax.fori_loop(0, N_WIDE, finish, 0)


def place_entries(slots, base, mate, far, ids, bias):
    vmem = pl.BlockSpec(memory_space=pltpu.VMEM)
    hbm = pl.BlockSpec(memory_space=pltpu.HBM)
    return pl.pallas_call(
        place_kernel,
        out_shape=jax.ShapeDtypeStruct((N_WIDE, BLOCK, E), BF16),
        in_specs=[pl.BlockSpec(memory_space=pltpu.SMEM)] + [pl.BlockSpec(memory_space=pl.ANY)] * 3 + [vmem] * 2,
        out_specs=hbm,
        scratch_shapes=[
            pltpu.VMEM(base.shape, F32),
            pltpu.VMEM(base.shape, BF16),
            pltpu.VMEM(base.shape, BF16),
            pltpu.VMEM((N_WIDE * CAP + 8, E), F32),
            pltpu.VMEM((N_WIDE, BLOCK, E), BF16),
            pltpu.SemaphoreType.DMA((N_WIDE,)),
            pltpu.SemaphoreType.DMA((3,)),
        ],
        compiler_params=pltpu.CompilerParams(vmem_limit_bytes=VMEM_MOST),
        cost_estimate=LIGHT,
        name="place_entries",
    )(slots, base, mate, far, ids, bias)


def sums_kernel(
    norm_factor, core_ref, recv_hbm, keep_ref, send_ref, bias_ref, recv_ref, tails, total, left, right, todo, sems
):
    get_tails = pltpu.make_async_copy(recv_hbm.at[:, pl.ds(CAP, TAIL), :], tails, sems.at[0])
    get_values = pltpu.make_async_copy(recv_hbm.at[:, pl.ds(0, CAP), :], recv_ref, sems.at[1])
    get_tails.start()
    get_values.start()
    get_tails.wait()
    lane_rows = lax.broadcasted_iota(jnp.int32, (LO, E), 0)

    n = 0
    for w in range(N_WIDE):
        ids = tails[w].astype(F32)
        ids = ids[0:4, :] + ids[4:8, :]
        halves = jnp.max(jnp.where(ids[2:3, :] > 0.0, 2.0, jnp.where(ids[0:1, :] > 0.0, 1.0, 0.0)))
        todo[n] = 2 * w
        n = n + jnp.where(halves > 0.5, 1, 0)
        todo[n] = 2 * w + 1
        n = n + jnp.where(halves > 1.5, 1, 0)
    for k in range(12):
        todo[n + k] = -1
    total[...] = jnp.zeros_like(total)
    bias_ref[...] = jnp.sum(tails[:, 8:, :].astype(F32), axis=0) * norm_factor
    get_values.wait()

    def build(i, buf):
        for p in range(4):
            item = todo[i * 4 + p]
            w = jnp.maximum(item, 0) // 2
            half = jnp.maximum(item, 0) % 2
            ids = tails[w].astype(F32)
            row = (ids[0:4, :] * 64.0 + ids[4:8, :]).astype(jnp.int32) - 1
            row = jnp.where(half == 0, row[0:2, :], row[2:4, :])
            row = jnp.where(item < 0, -1, row)
            hi = row >> (LO.bit_length() - 1)
            lo = jnp.where(row < 0, -1, row & (LO - 1))
            hi_col = jnp.transpose(jnp.concatenate([hi] * 4, axis=0).astype(F32), (1, 0))
            for j in range(2):
                at = (2 * p + j) * E
                left[buf, :, at : at + E] = jnp.where(lane_rows == lo[j : j + 1, :], 1.0, 0.0).astype(BF16)
                v = recv_ref[w, pl.ds(pl.multiple_of(half * (CAP // 2), CAP // 2) + j * E, E), :]
                own = jnp.broadcast_to(hi_col[:, j : j + 1], (E, E)).astype(BF16)
                for h in range(HI):
                    right[buf, at : at + E, h * E : (h + 1) * E] = jnp.where(own == BF16(h), v, BF16(0))

    build(0, 0)

    def step(i, _):
        for b in range(2):
            build(2 * i + b + 1, 1 - b)
            total[...] += jnp.dot(left[b], right[b], preferred_element_type=F32)
        return 0

    lax.fori_loop(0, (n + 7) // 8, step, 0)
    for k in range(HI // 2):
        for out_ref, half in ((keep_ref, core_ref[0]), (send_ref, 1 - core_ref[0])):
            at = pl.multiple_of((half * (HI // 2) + k) * E, E)
            out_ref[k * LO : (k + 1) * LO, :] = total[:, pl.ds(at, E)].astype(BF16)


def owned_sums(norm_factor, core, recv):
    vmem = pl.BlockSpec(memory_space=pltpu.VMEM)
    return pl.pallas_call(
        functools.partial(sums_kernel, norm_factor),
        out_shape=[jax.ShapeDtypeStruct((N_ROWS // 2, E), BF16)] * 2 + [jax.ShapeDtypeStruct((8, E), F32)],
        in_specs=[pl.BlockSpec(memory_space=pltpu.SMEM), pl.BlockSpec(memory_space=pltpu.HBM)],
        out_specs=[vmem] * 3,
        scratch_shapes=[
            pltpu.VMEM((N_WIDE, CAP, E), BF16),
            pltpu.VMEM((N_WIDE, TAIL, E), BF16),
            pltpu.VMEM((LO, HI * E), F32),
            pltpu.VMEM((2, LO, 2 * CAP), BF16),
            pltpu.VMEM((2, 2 * CAP, HI * E), BF16),
            pltpu.SMEM((2 * N_WIDE + 16,), jnp.int32),
            pltpu.SemaphoreType.DMA((2,)),
        ],
        compiler_params=pltpu.CompilerParams(vmem_limit_bytes=VMEM_BYTES),
        cost_estimate=LIGHT,
        name="owned_sums",
    )(core, recv)


def summed(own, others):
    total = own.astype(F32)
    for other in others:
        total = total + other.astype(F32)
    return total


def own_chunk(a):
    return pl.multiple_of(a * 1024, 1024)


def ring_terms(route, part, embedded, z, y, d):
    if route == 0:
        rows = embedded[:, pl.ds(own_chunk((z + d) % 4), 1024)]
        yield slice(0, 1024), jnp.dot(part, rows, preferred_element_type=F32)
        return
    start = ((y + d) % 4) * 256
    for k in range(4):
        rows = embedded[:, pl.ds(pl.multiple_of(k * 1024 + start, 256), 256)]
        yield slice(k * 256, (k + 1) * 256), jnp.dot(part, rows, preferred_element_type=F32)


def sent_kernel(n_ref, z_ref, y_ref, cot_hbm, embedded_hbm, weight_hbm, *refs):
    parts_hbm, first_hbm, (scaled_hbm, turned_hbm) = refs[:2], refs[2:6], refs[6:8]
    cot, embedded, weight, scaled, turned, parts, first, sems, sems_out = refs[8:]
    n, z, y = n_ref[0], z_ref[0], y_ref[0]

    def columns(q):
        at = pl.ds(own_chunk(n ^ q), 1024)
        return pltpu.make_async_copy(embedded_hbm.at[:, at], embedded.at[:, at], sems.at[q])

    def rows(q):
        at = pl.ds(own_chunk(n ^ q), 1024)
        return pltpu.make_async_copy(weight_hbm.at[at, :], weight.at[q - 2], sems.at[2 + q])

    outs = [(parts.at[q], parts_hbm[q]) for q in range(2)]
    outs += [(first.at[q], first_hbm[q]) for q in range(4)]
    outs += [(scaled, scaled_hbm), (turned, turned_hbm)]
    outs = [pltpu.make_async_copy(src, dst, sems_out.at[k]) for k, (src, dst) in enumerate(outs)]

    get_cot = pltpu.make_async_copy(cot_hbm, cot, sems.at[6])
    get_cot.start()
    columns(0).start()
    rows(3).start()
    get_cot.wait()
    columns(0).wait()
    rows(2).start()
    for q in (1, 2, 3):
        columns(q).start()
    grads = (cot[...].astype(F32) * embedded[:, pl.ds(own_chunk(n), 1024)].astype(F32)).astype(BF16)
    scaled[...] = grads
    outs[6].start()
    rows(3).wait()
    parts[0] = lax.dot_general(scaled[...], weight[1], NT, preferred_element_type=F32).astype(BF16)
    turned[...] = jnp.transpose(grads, (1, 0))
    outs[0].start()
    outs[7].start()
    rows(2).wait()
    parts[1] = lax.dot_general(scaled[...], weight[0], NT, preferred_element_type=F32).astype(BF16)
    outs[1].start()
    for q in (1, 2, 3):
        columns(q).wait()
    for route in range(2):
        low = route * 512
        for at, term in ring_terms(route, turned[low : low + 512, :], embedded, z, y, 2):
            term = term.astype(BF16)
            for way in range(2):
                first[2 * route + way, :256, at] = term[way * 256 : (way + 1) * 256, :]
        for way in range(2):
            q = 2 * route + way
            other = turned[low + (1 - way) * 256 : low + (2 - way) * 256, :]
            for at, term in ring_terms(route, other, embedded, z, y, 3 if way else 1):
                first[q, 256:, at] = term.astype(BF16)
            outs[2 + q].start()
    for copy in outs:
        copy.wait()


def sent_terms(n, z, y, cotangent, embedded, weight):
    hbm = pl.BlockSpec(memory_space=pltpu.HBM)
    smem = pl.BlockSpec(memory_space=pltpu.SMEM)
    samples, width = cotangent.shape
    shape = jax.ShapeDtypeStruct
    full = shape((samples, width), BF16)
    results = pl.pallas_call(
        sent_kernel,
        out_shape=[full] * 2 + [shape((512, 1024), BF16)] * 4 + [full, shape((width, samples), BF16)],
        in_specs=[smem] * 3 + [hbm] * 3,
        out_specs=[hbm] * 8,
        scratch_shapes=[
            pltpu.VMEM(cotangent.shape, BF16),
            pltpu.VMEM(embedded.shape, BF16),
            pltpu.VMEM((2, 1024, 1024), BF16),
            pltpu.VMEM((samples, width), BF16),
            pltpu.VMEM((width, samples), BF16),
            pltpu.VMEM((2, samples, width), BF16),
            pltpu.VMEM((4, 512, 1024), BF16),
            pltpu.SemaphoreType.DMA((7,)),
            pltpu.SemaphoreType.DMA((8,)),
        ],
        compiler_params=pltpu.CompilerParams(vmem_limit_bytes=VMEM_MOST),
        cost_estimate=LIGHT,
        name="sent_terms",
    )(n, z, y, cotangent, embedded, weight)
    return results[:2], results[2:6], *results[6:]


def pass_kernel(*refs):
    passed_hbm, mine_hbm, sent_hbm, (passed, mine, sent, sems, sems_out) = refs[:4], refs[4:8], refs[8:12], refs[12:]
    loads, outs = [], []
    for q in range(4):
        loads.append(pltpu.make_async_copy(passed_hbm[q].at[pl.ds(0, 256), :], passed.at[q], sems.at[2 * q]))
        loads.append(pltpu.make_async_copy(mine_hbm[q], mine.at[q], sems.at[2 * q + 1]))
        outs.append(pltpu.make_async_copy(sent.at[q], sent_hbm[q], sems_out.at[q]))
    for load in loads:
        load.start()
    for q in range(4):
        loads[2 * q].wait()
        loads[2 * q + 1].wait()
        sent[q] = (passed[q].astype(F32) + mine[q].astype(F32)).astype(BF16)
        outs[q].start()
    for copy in outs:
        copy.wait()


def passed_on(first, second):
    hbm = pl.BlockSpec(memory_space=pltpu.HBM)
    return pl.pallas_call(
        pass_kernel,
        out_shape=[jax.ShapeDtypeStruct((256, 1024), BF16)] * 4,
        in_specs=[pl.BlockSpec(memory_space=pl.ANY)] * 8,
        out_specs=[hbm] * 4,
        scratch_shapes=[
            pltpu.VMEM((4, 256, 1024), BF16),
            pltpu.VMEM((4, 256, 1024), BF16),
            pltpu.VMEM((4, 256, 1024), BF16),
            pltpu.SemaphoreType.DMA((8,)),
            pltpu.SemaphoreType.DMA((4,)),
        ],
        compiler_params=pltpu.CompilerParams(vmem_limit_bytes=VMEM_MOST),
        cost_estimate=LIGHT,
        name="passed_on",
    )(*first, *second)


def kept_kernel(
    n_ref, z_ref, y_ref, cot_hbm, embedded_hbm, weight_hbm, bias_ref, scaled_hbm, turned_hbm, owner_ref, row_ref, bag_ref, *refs
):
    base_ref, slots_ref, ids_ref, bias_sum_ref, mate_hbm, second_hbm = *refs[:5], refs[5:9]
    cot, embedded, weight, scaled, turned, cross, onehots, mate, second, sems, sems_out = refs[9:]
    n, z, y = n_ref[0], z_ref[0], y_ref[0]

    def columns(q):
        at = pl.ds(own_chunk(n ^ q), 1024)
        return pltpu.make_async_copy(embedded_hbm.at[:, at], embedded.at[:, at], sems.at[q])

    def rows(q):
        at = pl.ds(own_chunk(n ^ q), 1024)
        return pltpu.make_async_copy(weight_hbm.at[at, :], weight.at[q], sems.at[4 + q])

    get_scaled = pltpu.make_async_copy(scaled_hbm, scaled, sems.at[8])
    get_cot = pltpu.make_async_copy(cot_hbm, cot, sems.at[9])
    get_turned = pltpu.make_async_copy(turned_hbm, turned, sems.at[10])
    outs = [(mate, mate_hbm)] + [(second.at[q], second_hbm[q]) for q in range(4)]
    outs = [pltpu.make_async_copy(src, dst, sems_out.at[k]) for k, (src, dst) in enumerate(outs)]
    rows(0).start()
    columns(0).start()
    get_scaled.start()
    for q in (1, 2, 3):
        rows(q).start()
        columns(q).start()
    get_cot.start()
    get_turned.start()
    find_slots(n, owner_ref, row_ref, bag_ref, slots_ref, ids_ref, onehots)
    get_scaled.wait()
    rows(1).wait()
    mate[...] = lax.dot_general(scaled[...], weight[1], NT, preferred_element_type=F32).astype(BF16)
    outs[0].start()
    for q in range(4):
        columns(q).wait()
    get_turned.wait()
    for route in range(2):
        for way in range(2):
            q = 2 * route + way
            low = route * 512 + way * 256
            for at, term in ring_terms(route, turned[low : low + 256, :], embedded, z, y, 3 if way else 1):
                second[q, :, at] = term.astype(BF16)
            outs[1 + q].start()
    sums = jnp.sum(scaled[...].astype(F32), axis=0, keepdims=True)
    bias_sum_ref[...] = jnp.concatenate([sums[:, k * E : (k + 1) * E] for k in range(8)], axis=0)
    rows(0).wait()
    cross[...] = jnp.dot(embedded[:, pl.ds(own_chunk(n), 1024)], weight[0], preferred_element_type=F32)
    base_ref[...] = lax.dot_general(scaled[...], weight[0], NT, preferred_element_type=F32)
    for q in (1, 2):
        if q > 1:
            rows(q).wait()
        cross[...] += jnp.dot(embedded[:, pl.ds(own_chunk(n ^ q), 1024)], weight[q], preferred_element_type=F32)
    rows(3).wait()
    get_cot.wait()
    grad = cot[...].astype(F32)
    last = jnp.dot(embedded[:, pl.ds(own_chunk(n ^ 3), 1024)], weight[3], preferred_element_type=F32)
    base_ref[...] += grad + grad * (cross[...] + last + bias_ref[...])
    for copy in outs:
        copy.wait()


def kept_terms(n, z, y, cotangent, embedded, weight, bias, scaled, turned, owner, row, bag):
    hbm = pl.BlockSpec(memory_space=pltpu.HBM)
    vmem = pl.BlockSpec(memory_space=pltpu.VMEM)
    samples, width = cotangent.shape
    depth = owner.shape[0]
    shape = jax.ShapeDtypeStruct
    results = pl.pallas_call(
        kept_kernel,
        out_shape=[
            shape((samples, width), F32),
            shape((depth * samples // E, E), jnp.int32),
            shape((2 * N_WIDE, CAP), F32),
            shape((8, E), F32),
            shape((samples, width), BF16),
        ]
        + [shape((256, 1024), BF16)] * 4,
        in_specs=[pl.BlockSpec(memory_space=pltpu.SMEM)] * 3 + [hbm] * 3 + [vmem, hbm, hbm] + [vmem] * 3,
        out_specs=[vmem] * 4 + [hbm] * 5,
        scratch_shapes=[
            pltpu.VMEM(cotangent.shape, BF16),
            pltpu.VMEM(embedded.shape, BF16),
            pltpu.VMEM((4, 1024, 1024), BF16),
            pltpu.VMEM((samples, width), BF16),
            pltpu.VMEM((width, samples), BF16),
            pltpu.VMEM((samples, width), F32),
            pltpu.VMEM((N_WIDE * depth, samples), BF16),
            pltpu.VMEM((samples, width), BF16),
            pltpu.VMEM((4, 256, 1024), BF16),
            pltpu.SemaphoreType.DMA((11,)),
            pltpu.SemaphoreType.DMA((5,)),
        ],
        compiler_params=pltpu.CompilerParams(vmem_limit_bytes=VMEM_MOST),
        cost_estimate=LIGHT,
        name="kept_terms",
    )(n, z, y, cotangent, embedded, weight, bias.reshape(1, -1), scaled, turned, owner, row, bag)
    return *results[:5], results[5:]


def own_kernel(z_ref, y_ref, embedded_hbm, turned_hbm, *refs):
    got_hbm, results, (embedded, turned, got, sems) = refs[:8], refs[8:12], refs[12:]
    z, y = z_ref[0], y_ref[0]
    loads = [(embedded_hbm, embedded), (turned_hbm, turned)]
    loads += [(got_hbm[k].at[pl.ds(256, 256), :], got.at[k]) for k in range(4)]
    loads += [(got_hbm[k], got.at[k]) for k in range(4, 8)]
    loads = [pltpu.make_async_copy(src, dst, sems.at[k]) for k, (src, dst) in enumerate(loads)]
    for load in loads:
        load.start()
    for load in loads:
        load.wait()
    for route, place in ((0, y), (1, z)):
        term = jnp.concatenate([term for _, term in ring_terms(route, turned[route * 512 : (route + 1) * 512, :], embedded, z, y, 0)], axis=1)
        up, down = 2 * route, 2 * route + 1
        total = jnp.concatenate(
            [
                term[:256, :] + got[4 + up].astype(F32) + got[down].astype(F32),
                term[256:, :] + got[4 + down].astype(F32) + got[up].astype(F32),
            ],
            axis=0,
        ).astype(BF16)
        total = jnp.transpose(total, (1, 0))
        high = place >= 2
        results[2 * route][...] = jnp.where(high, total[512:, :], total[:512, :])
        results[2 * route + 1][...] = jnp.where(high, total[:512, :], total[512:, :])


def own_terms(z, y, embedded, turned, first, second):
    hbm = pl.BlockSpec(memory_space=pltpu.HBM)
    vmem = pl.BlockSpec(memory_space=pltpu.VMEM)
    return pl.pallas_call(
        own_kernel,
        out_shape=[jax.ShapeDtypeStruct((512, 512), BF16)] * 4,
        in_specs=[pl.BlockSpec(memory_space=pltpu.SMEM)] * 2 + [hbm] + [pl.BlockSpec(memory_space=pl.ANY)] * 9,
        out_specs=[vmem] * 4,
        scratch_shapes=[
            pltpu.VMEM(embedded.shape, BF16),
            pltpu.VMEM(turned.shape, BF16),
            pltpu.VMEM((8, 256, 1024), BF16),
            pltpu.SemaphoreType.DMA((10,)),
        ],
        compiler_params=pltpu.CompilerParams(vmem_limit_bytes=VMEM_BYTES),
        cost_estimate=LIGHT,
        name="own_terms",
    )(z, y, embedded, turned, *first, *second)


def halves_of(array, bit, axis):
    size = array.shape[axis] // 2
    return (
        lax.dynamic_slice_in_dim(array, bit * size, size, axis),
        lax.dynamic_slice_in_dim(array, (1 - bit) * size, size, axis),
    )


def body(
    embedded,
    cotangent,
    cross_weight,
    cross_bias,
    bag_size,
    row_owner,
    row_id,
    emb_table,
    adagrad_state,
):
    panel = lax.axis_index("narrow")
    wide = lax.axis_index("wide")
    z, y, x_lo = wide // 8, (wide // 2) % 4, wide % 2
    core = panel % 2
    batch_rows = cotangent.shape[0]
    norm_factor = 1.0 / math.sqrt(batch_rows * N_WIDE)

    at = (panel.reshape(1), z.reshape(1), y.reshape(1))

    parts, first, scaled, turned = sent_terms(*at, cotangent, embedded, cross_weight)
    from_mate_far = lax.ppermute(parts[0], "narrow", CORE)
    ways = [z_perm(1), z_perm(3), y_perm(1), y_perm(3)]
    first = [lax.ppermute(first[q], "wide", ways[q]) for q in range(4)]
    chip_far = (parts[1].astype(F32) + from_mate_far.astype(F32)).astype(BF16)
    chip_far, scaled, turned = lax.optimization_barrier((chip_far, scaled, turned))
    far = lax.ppermute(chip_far, "narrow", X_HI)

    entries = (row_owner.reshape(row_owner.shape[1:3]).T, row_id.reshape(row_id.shape[1:]).T, bag_size.T)
    base, slots, ids, bias_part, part, second = kept_terms(
        *at, cotangent, embedded, cross_weight, cross_bias, scaled, turned, *entries
    )
    slots, ids, part, *first = lax.optimization_barrier((slots, ids, part, *first))
    from_mate = lax.ppermute(part, "narrow", CORE)
    second = passed_on(first, second)
    slots, far, *second = lax.optimization_barrier((slots, far, *second))
    second = [lax.ppermute(second[q], "wide", ways[q]) for q in range(4)]

    payload = place_entries(slots.reshape(-1), base, from_mate, far, ids, bias_part)
    payload, *second = lax.optimization_barrier((payload, *second))
    recv = lax.all_to_all(payload, "wide", split_axis=0, concat_axis=0, tiled=True)

    keep_y, send_y, keep_z, send_z = own_terms(at[1], at[2], embedded, turned, first, second)
    recv, send_y, send_z = lax.optimization_barrier((recv, send_y, send_z))
    got = [lax.ppermute(send_y, "wide", y_flip(2)), lax.ppermute(send_z, "wide", z_flip(2))]
    keep, send, bias_sums = owned_sums(norm_factor, core.reshape(1), recv)
    from_core = lax.ppermute(send, "narrow", CORE)
    keep, *got = lax.optimization_barrier((keep, *got))
    quarters = []
    for half, other, place in ((keep_y, got[0], y), (keep_z, got[1], z)):
        quarters.append([part.astype(BF16) for part in halves_of(summed(half, [other]), place % 2, 0)])
    got = [lax.ppermute(quarters[0][1], "wide", y_flip(1)), lax.ppermute(quarters[1][1], "wide", z_flip(1))]
    keep, from_core, *_ = lax.optimization_barrier((keep, from_core, quarters[0][1], quarters[1][1]))
    chip = summed(keep, [from_core]).astype(BF16)
    pair = jnp.concatenate([summed(quarters[0][0], got[:1]), summed(quarters[1][0], got[1:])], axis=1).astype(BF16)
    x_keep, x_send = halves_of(pair, x_lo, 0)
    other_chip, _ = lax.optimization_barrier((lax.ppermute(chip, "narrow", X_HI), x_send))
    x_got = lax.ppermute(jnp.pad(x_send, ((0, 8), (0, 0))), "wide", X_LO)[:E]

    bias_grad = bias_sums.reshape(-1)
    mine = summed(chip, [other_chip]).astype(BF16)
    mate, x_got = lax.optimization_barrier((lax.ppermute(mine, "narrow", CORE), x_got))
    weight_grad = summed(x_keep, [x_got]) * norm_factor
    row_grad = jnp.concatenate([jnp.where(core == 0, mine, mate), jnp.where(core == 0, mate, mine)], axis=0).astype(F32)
    new_state = adagrad_state + jnp.mean(row_grad * row_grad, axis=1)
    new_table = emb_table - LEARN_RATE * row_grad / jnp.sqrt(new_state)[:, None]
    return (weight_grad, bias_grad, new_table, new_state)


def solution(mesh):
    in_specs = (
        P("wide", None),
        P("wide", "narrow"),
        P(None, "narrow"),
        P("narrow"),
        P("wide", None),
        P("narrow", "wide", None, None),
        P("narrow", "wide", None),
        P("wide", None),
        P("wide"),
    )
    out_specs = (P("wide", "narrow"), P("narrow"), P("wide", None), P("wide"))
    return jax.shard_map(body, mesh=mesh, in_specs=in_specs, out_specs=out_specs, check_vma=False)
```

```python
import functools
import math

import jax
import jax.numpy as jnp
from jax import lax
from jax.experimental import pallas as pl
from jax.experimental.pallas import tpu as pltpu
from jax.sharding import PartitionSpec as P

LEARN_RATE = 0.3
E = 128
N_WIDE = 32
CAP = 512
TAIL = 16
BLOCK = CAP + TAIL
N_ROWS = 2048
HI = 4
LO = N_ROWS // HI
F32 = jnp.float32
BF16 = jnp.bfloat16
LIGHT = pl.CostEstimate(flops=1, bytes_accessed=1, transcendentals=0)
VMEM_BYTES = 56 << 20
VMEM_MOST = 127 << 19
NT = (((1,), (1,)), ((), ()))


def z_perm(d):
    return [(i, ((i // 8 + d) % 4) * 8 + i % 8) for i in range(N_WIDE)]


def y_perm(d):
    return [(i, (i // 8) * 8 + (((i // 2) % 4 + d) % 4) * 2 + i % 2) for i in range(N_WIDE)]


def y_flip(m):
    return [(i, i ^ (2 * m)) for i in range(N_WIDE)]


def z_flip(m):
    return [(i, i ^ (8 * m)) for i in range(N_WIDE)]


X_LO = [(i, i ^ 1) for i in range(N_WIDE)]
CORE = [(i, i ^ 1) for i in range(4)]
X_HI = [(i, i ^ 2) for i in range(4)]


def find_slots(panel, owner_ref, row_ref, bag_ref, slots_ref, ids_ref, onehots):
    depth, samples = owner_ref.shape
    feats = depth // 2
    bag = bag_ref[pl.ds(pl.multiple_of(panel * feats, feats), feats), :]
    bag = jnp.concatenate([bag[k // 2 : k // 2 + 1, :] for k in range(depth)], axis=0)
    live = (lax.broadcasted_iota(jnp.int32, (depth, samples), 0) & 1) < bag
    owner = jnp.where(live, owner_ref[...], N_WIDE)
    for t in range(N_WIDE):
        onehots[t * depth : (t + 1) * depth, :] = jnp.where(owner == t, 1.0, 0.0).astype(BF16)

    size = N_WIDE * depth
    first = lax.broadcasted_iota(jnp.int32, (samples, samples), 0)
    second = lax.broadcasted_iota(jnp.int32, (samples, samples), 1)
    before = jnp.where(first < second, 1.0, 0.0).astype(BF16)
    within = jnp.dot(onehots[...], before, preferred_element_type=F32)
    in_row = jnp.dot(onehots[...], jnp.ones((samples, E), BF16), preferred_element_type=F32)
    top = jnp.floor(in_row * (1.0 / 16.0))
    low = (in_row - 16.0 * top).astype(BF16)
    top = top.astype(BF16)
    r = lax.broadcasted_iota(jnp.int32, (size, size), 0)
    c = lax.broadcasted_iota(jnp.int32, (size, size), 1)
    shift = depth.bit_length() - 1
    earlier = jnp.where((r >> shift == c >> shift) & (c < r), 1.0, 0.0).astype(BF16)
    rows_before = 16.0 * jnp.dot(earlier, top, preferred_element_type=F32) + jnp.dot(
        earlier, low, preferred_element_type=F32
    )
    place = jnp.zeros((depth, samples), F32)
    for t in range(N_WIDE):
        at = slice(t * depth, (t + 1) * depth)
        ahead = jnp.concatenate([rows_before[at, :]] * (samples // E), axis=1)
        place = place + jnp.where(owner == t, within[at, :] + ahead, 0.0)
    place = place.astype(jnp.int32)
    slots = jnp.where(live, owner * CAP + place, N_WIDE * CAP)
    for k in range(samples // E):
        slots_ref[k * depth : (k + 1) * depth, :] = slots[:, k * E : (k + 1) * E]

    marked = row_ref[...] + 1
    top = (marked >> 6).astype(F32)
    low = (marked & 63).astype(F32)
    owners = lax.broadcasted_iota(jnp.int32, (N_WIDE, samples), 0)
    places = lax.broadcasted_iota(jnp.int32, (CAP, samples), 0)
    ids = jnp.zeros((2 * N_WIDE, CAP), F32)
    for k in range(depth):
        at = slice(k, k + 1)
        mine = owners == owner[at, :]
        marks = jnp.concatenate([jnp.where(mine, top[at, :], 0.0), jnp.where(mine, low[at, :], 0.0)], axis=0)
        there = jnp.where(places == place[at, :], 1.0, 0.0).astype(BF16)
        ids = ids + lax.dot_general(
            marks.astype(BF16), there, (((1,), (1,)), ((), ())), preferred_element_type=F32
        )
    ids_ref[...] = ids


def place_kernel(
    slots_ref, base_hbm, mate_hbm, far_hbm, ids_ref, bias_ref, out_ref, base, mate, far, rows, blocks, sems, sems_in
):
    depth = 16
    dump = N_WIDE * CAP
    loads = [
        pltpu.make_async_copy(src, dst, sems_in.at[k])
        for k, (src, dst) in enumerate(((base_hbm, base), (mate_hbm, mate), (far_hbm, far)))
    ]
    for load in loads:
        load.start()

    def clear(i, _):
        rows[pl.ds(pl.multiple_of(i * 256, 256), 256), :] = jnp.zeros((256, E), F32)
        return 0

    lax.fori_loop(0, dump // 256, clear, 0)
    for load in loads:
        load.wait()

    def place(i, _):
        first = pl.multiple_of(i * 16, 16)
        at = (first // E) * (depth * E) + first % E
        for f in range(8):
            cols = slice(f * E, (f + 1) * E)
            tile = base[pl.ds(first, 16), cols] + (
                mate[pl.ds(first, 16), cols].astype(F32) + far[pl.ds(first, 16), cols].astype(F32)
            )
            for b in range(16):
                row = tile[b : b + 1, :]
                for j in range(2):
                    slot = slots_ref[at + (2 * f + j) * E + b]
                    rows[pl.ds(slot, 1), :] = row
        return 0

    lax.fori_loop(0, base.shape[0] // 16, place, 0)

    bias = bias_ref[...]

    def copy_out(w):
        return pltpu.make_async_copy(blocks.at[w], out_ref.at[w], sems.at[w])

    def narrow_down(w, _):
        blocks[w, :CAP, :] = rows[pl.ds(pl.multiple_of(w * CAP, CAP), CAP), :].astype(BF16)
        top = ids_ref[pl.ds(w, 1), :]
        low = ids_ref[pl.ds(N_WIDE + w, 1), :]
        parts = [top[:, k * E : (k + 1) * E] for k in range(4)] + [low[:, k * E : (k + 1) * E] for k in range(4)]
        blocks[w, CAP:, :] = jnp.concatenate(parts + [bias], axis=0).astype(BF16)
        copy_out(w).start()
        return 0

    lax.fori_loop(0, N_WIDE, narrow_down, 0)

    def finish(w, _):
        copy_out(w).wait()
        return 0

    lax.fori_loop(0, N_WIDE, finish, 0)


def place_entries(slots, base, mate, far, ids, bias):
    vmem = pl.BlockSpec(memory_space=pltpu.VMEM)
    hbm = pl.BlockSpec(memory_space=pltpu.HBM)
    return pl.pallas_call(
        place_kernel,
        out_shape=jax.ShapeDtypeStruct((N_WIDE, BLOCK, E), BF16),
        in_specs=[pl.BlockSpec(memory_space=pltpu.SMEM)] + [pl.BlockSpec(memory_space=pl.ANY)] * 3 + [vmem] * 2,
        out_specs=hbm,
        scratch_shapes=[
            pltpu.VMEM(base.shape, F32),
            pltpu.VMEM(base.shape, BF16),
            pltpu.VMEM(base.shape, BF16),
            pltpu.VMEM((N_WIDE * CAP + 8, E), F32),
            pltpu.VMEM((N_WIDE, BLOCK, E), BF16),
            pltpu.SemaphoreType.DMA((N_WIDE,)),
            pltpu.SemaphoreType.DMA((3,)),
        ],
        compiler_params=pltpu.CompilerParams(vmem_limit_bytes=VMEM_MOST),
        cost_estimate=LIGHT,
        name="place_entries",
    )(slots, base, mate, far, ids, bias)


def sums_kernel(
    norm_factor, core_ref, recv_hbm, keep_ref, send_ref, bias_ref, recv_ref, tails, total, left, right, todo, sems
):
    get_tails = pltpu.make_async_copy(recv_hbm.at[:, pl.ds(CAP, TAIL), :], tails, sems.at[0])
    get_values = pltpu.make_async_copy(recv_hbm.at[:, pl.ds(0, CAP), :], recv_ref, sems.at[1])
    get_tails.start()
    get_values.start()
    get_tails.wait()
    lane_rows = lax.broadcasted_iota(jnp.int32, (LO, E), 0)

    n = 0
    for w in range(N_WIDE):
        ids = tails[w].astype(F32)
        ids = ids[0:4, :] + ids[4:8, :]
        halves = jnp.max(jnp.where(ids[2:3, :] > 0.0, 2.0, jnp.where(ids[0:1, :] > 0.0, 1.0, 0.0)))
        todo[n] = 2 * w
        n = n + jnp.where(halves > 0.5, 1, 0)
        todo[n] = 2 * w + 1
        n = n + jnp.where(halves > 1.5, 1, 0)
    for k in range(12):
        todo[n + k] = -1
    total[...] = jnp.zeros_like(total)
    bias_ref[...] = jnp.sum(tails[:, 8:, :].astype(F32), axis=0) * norm_factor
    get_values.wait()

    def build(i, buf):
        for p in range(4):
            item = todo[i * 4 + p]
            w = jnp.maximum(item, 0) // 2
            half = jnp.maximum(item, 0) % 2
            ids = tails[w].astype(F32)
            row = (ids[0:4, :] * 64.0 + ids[4:8, :]).astype(jnp.int32) - 1
            row = jnp.where(half == 0, row[0:2, :], row[2:4, :])
            row = jnp.where(item < 0, -1, row)
            hi = row >> (LO.bit_length() - 1)
            lo = jnp.where(row < 0, -1, row & (LO - 1))
            hi_col = jnp.transpose(jnp.concatenate([hi] * 4, axis=0).astype(F32), (1, 0))
            for j in range(2):
                at = (2 * p + j) * E
                left[buf, :, at : at + E] = jnp.where(lane_rows == lo[j : j + 1, :], 1.0, 0.0).astype(BF16)
                v = recv_ref[w, pl.ds(pl.multiple_of(half * (CAP // 2), CAP // 2) + j * E, E), :]
                own = jnp.broadcast_to(hi_col[:, j : j + 1], (E, E)).astype(BF16)
                for h in range(HI):
                    right[buf, at : at + E, h * E : (h + 1) * E] = jnp.where(own == BF16(h), v, BF16(0))

    build(0, 0)

    def step(i, _):
        for b in range(2):
            build(2 * i + b + 1, 1 - b)
            total[...] += jnp.dot(left[b], right[b], preferred_element_type=F32)
        return 0

    lax.fori_loop(0, (n + 7) // 8, step, 0)
    for k in range(HI // 2):
        for out_ref, half in ((keep_ref, core_ref[0]), (send_ref, 1 - core_ref[0])):
            at = pl.multiple_of((half * (HI // 2) + k) * E, E)
            out_ref[k * LO : (k + 1) * LO, :] = total[:, pl.ds(at, E)].astype(BF16)


def owned_sums(norm_factor, core, recv):
    vmem = pl.BlockSpec(memory_space=pltpu.VMEM)
    return pl.pallas_call(
        functools.partial(sums_kernel, norm_factor),
        out_shape=[jax.ShapeDtypeStruct((N_ROWS // 2, E), BF16)] * 2 + [jax.ShapeDtypeStruct((8, E), F32)],
        in_specs=[pl.BlockSpec(memory_space=pltpu.SMEM), pl.BlockSpec(memory_space=pltpu.HBM)],
        out_specs=[vmem] * 3,
        scratch_shapes=[
            pltpu.VMEM((N_WIDE, CAP, E), BF16),
            pltpu.VMEM((N_WIDE, TAIL, E), BF16),
            pltpu.VMEM((LO, HI * E), F32),
            pltpu.VMEM((2, LO, 2 * CAP), BF16),
            pltpu.VMEM((2, 2 * CAP, HI * E), BF16),
            pltpu.SMEM((2 * N_WIDE + 16,), jnp.int32),
            pltpu.SemaphoreType.DMA((2,)),
        ],
        compiler_params=pltpu.CompilerParams(vmem_limit_bytes=VMEM_BYTES),
        cost_estimate=LIGHT,
        name="owned_sums",
    )(core, recv)


def summed(own, others):
    total = own.astype(F32)
    for other in others:
        total = total + other.astype(F32)
    return total


def own_chunk(a):
    return pl.multiple_of(a * 1024, 1024)


def ring_terms(route, part, embedded, z, y, d):
    if route == 0:
        rows = embedded[:, pl.ds(own_chunk((z + d) % 4), 1024)]
        yield slice(0, 1024), jnp.dot(part, rows, preferred_element_type=F32)
        return
    start = ((y + d) % 4) * 256
    for k in range(4):
        rows = embedded[:, pl.ds(pl.multiple_of(k * 1024 + start, 256), 256)]
        yield slice(k * 256, (k + 1) * 256), jnp.dot(part, rows, preferred_element_type=F32)


def sent_kernel(n_ref, z_ref, y_ref, cot_hbm, embedded_hbm, weight_hbm, *refs):
    parts_hbm, first_hbm, (scaled_hbm, turned_hbm) = refs[:2], refs[2:6], refs[6:8]
    cot, embedded, weight, scaled, turned, parts, first, sems, sems_out = refs[8:]
    n, z, y = n_ref[0], z_ref[0], y_ref[0]

    def columns(q):
        at = pl.ds(own_chunk(n ^ q), 1024)
        return pltpu.make_async_copy(embedded_hbm.at[:, at], embedded.at[:, at], sems.at[q])

    def rows(q):
        at = pl.ds(own_chunk(n ^ q), 1024)
        return pltpu.make_async_copy(weight_hbm.at[at, :], weight.at[q - 2], sems.at[2 + q])

    outs = [(parts.at[q], parts_hbm[q]) for q in range(2)]
    outs += [(first.at[q], first_hbm[q]) for q in range(4)]
    outs += [(scaled, scaled_hbm), (turned, turned_hbm)]
    outs = [pltpu.make_async_copy(src, dst, sems_out.at[k]) for k, (src, dst) in enumerate(outs)]

    get_cot = pltpu.make_async_copy(cot_hbm, cot, sems.at[6])
    get_cot.start()
    columns(0).start()
    rows(3).start()
    get_cot.wait()
    columns(0).wait()
    rows(2).start()
    for q in (1, 2, 3):
        columns(q).start()
    grads = (cot[...].astype(F32) * embedded[:, pl.ds(own_chunk(n), 1024)].astype(F32)).astype(BF16)
    scaled[...] = grads
    outs[6].start()
    rows(3).wait()
    parts[0] = lax.dot_general(scaled[...], weight[1], NT, preferred_element_type=F32).astype(BF16)
    turned[...] = jnp.transpose(grads, (1, 0))
    outs[0].start()
    outs[7].start()
    rows(2).wait()
    parts[1] = lax.dot_general(scaled[...], weight[0], NT, preferred_element_type=F32).astype(BF16)
    outs[1].start()
    for q in (1, 2, 3):
        columns(q).wait()
    for route in range(2):
        low = route * 512
        for at, term in ring_terms(route, turned[low : low + 512, :], embedded, z, y, 2):
            term = term.astype(BF16)
            for way in range(2):
                first[2 * route + way, :256, at] = term[way * 256 : (way + 1) * 256, :]
        for way in range(2):
            q = 2 * route + way
            other = turned[low + (1 - way) * 256 : low + (2 - way) * 256, :]
            for at, term in ring_terms(route, other, embedded, z, y, 3 if way else 1):
                first[q, 256:, at] = term.astype(BF16)
            outs[2 + q].start()
    for copy in outs:
        copy.wait()


def sent_terms(n, z, y, cotangent, embedded, weight):
    hbm = pl.BlockSpec(memory_space=pltpu.HBM)
    smem = pl.BlockSpec(memory_space=pltpu.SMEM)
    samples, width = cotangent.shape
    shape = jax.ShapeDtypeStruct
    full = shape((samples, width), BF16)
    results = pl.pallas_call(
        sent_kernel,
        out_shape=[full] * 2 + [shape((512, 1024), BF16)] * 4 + [full, shape((width, samples), BF16)],
        in_specs=[smem] * 3 + [hbm] * 3,
        out_specs=[hbm] * 8,
        scratch_shapes=[
            pltpu.VMEM(cotangent.shape, BF16),
            pltpu.VMEM(embedded.shape, BF16),
            pltpu.VMEM((2, 1024, 1024), BF16),
            pltpu.VMEM((samples, width), BF16),
            pltpu.VMEM((width, samples), BF16),
            pltpu.VMEM((2, samples, width), BF16),
            pltpu.VMEM((4, 512, 1024), BF16),
            pltpu.SemaphoreType.DMA((7,)),
            pltpu.SemaphoreType.DMA((8,)),
        ],
        compiler_params=pltpu.CompilerParams(vmem_limit_bytes=VMEM_MOST),
        cost_estimate=LIGHT,
        name="sent_terms",
    )(n, z, y, cotangent, embedded, weight)
    return results[:2], results[2:6], *results[6:]


def pass_kernel(*refs):
    passed_hbm, mine_hbm, sent_hbm, (passed, mine, sent, sems, sems_out) = refs[:4], refs[4:8], refs[8:12], refs[12:]
    loads, outs = [], []
    for q in range(4):
        loads.append(pltpu.make_async_copy(passed_hbm[q].at[pl.ds(0, 256), :], passed.at[q], sems.at[2 * q]))
        loads.append(pltpu.make_async_copy(mine_hbm[q], mine.at[q], sems.at[2 * q + 1]))
        outs.append(pltpu.make_async_copy(sent.at[q], sent_hbm[q], sems_out.at[q]))
    for load in loads:
        load.start()
    for q in range(4):
        loads[2 * q].wait()
        loads[2 * q + 1].wait()
        sent[q] = (passed[q].astype(F32) + mine[q].astype(F32)).astype(BF16)
        outs[q].start()
    for copy in outs:
        copy.wait()


def passed_on(first, second):
    hbm = pl.BlockSpec(memory_space=pltpu.HBM)
    return pl.pallas_call(
        pass_kernel,
        out_shape=[jax.ShapeDtypeStruct((256, 1024), BF16)] * 4,
        in_specs=[pl.BlockSpec(memory_space=pl.ANY)] * 8,
        out_specs=[hbm] * 4,
        scratch_shapes=[
            pltpu.VMEM((4, 256, 1024), BF16),
            pltpu.VMEM((4, 256, 1024), BF16),
            pltpu.VMEM((4, 256, 1024), BF16),
            pltpu.SemaphoreType.DMA((8,)),
            pltpu.SemaphoreType.DMA((4,)),
        ],
        compiler_params=pltpu.CompilerParams(vmem_limit_bytes=VMEM_MOST),
        cost_estimate=LIGHT,
        name="passed_on",
    )(*first, *second)


def kept_kernel(
    n_ref, z_ref, y_ref, cot_hbm, embedded_hbm, weight_hbm, bias_ref, scaled_hbm, turned_hbm, owner_ref, row_ref, bag_ref, *refs
):
    base_ref, slots_ref, ids_ref, bias_sum_ref, mate_hbm, second_hbm = *refs[:5], refs[5:9]
    cot, embedded, weight, scaled, turned, cross, onehots, mate, second, sems, sems_out = refs[9:]
    n, z, y = n_ref[0], z_ref[0], y_ref[0]

    def columns(q):
        at = pl.ds(own_chunk(n ^ q), 1024)
        return pltpu.make_async_copy(embedded_hbm.at[:, at], embedded.at[:, at], sems.at[q])

    def rows(q):
        at = pl.ds(own_chunk(n ^ q), 1024)
        return pltpu.make_async_copy(weight_hbm.at[at, :], weight.at[q], sems.at[4 + q])

    get_scaled = pltpu.make_async_copy(scaled_hbm, scaled, sems.at[8])
    get_cot = pltpu.make_async_copy(cot_hbm, cot, sems.at[9])
    get_turned = pltpu.make_async_copy(turned_hbm, turned, sems.at[10])
    outs = [(mate, mate_hbm)] + [(second.at[q], second_hbm[q]) for q in range(4)]
    outs = [pltpu.make_async_copy(src, dst, sems_out.at[k]) for k, (src, dst) in enumerate(outs)]
    rows(0).start()
    columns(0).start()
    get_scaled.start()
    for q in (1, 2, 3):
        rows(q).start()
        columns(q).start()
    get_cot.start()
    get_turned.start()
    find_slots(n, owner_ref, row_ref, bag_ref, slots_ref, ids_ref, onehots)
    get_scaled.wait()
    rows(1).wait()
    mate[...] = lax.dot_general(scaled[...], weight[1], NT, preferred_element_type=F32).astype(BF16)
    outs[0].start()
    for q in range(4):
        columns(q).wait()
    get_turned.wait()
    for route in range(2):
        for way in range(2):
            q = 2 * route + way
            low = route * 512 + way * 256
            for at, term in ring_terms(route, turned[low : low + 256, :], embedded, z, y, 3 if way else 1):
                second[q, :, at] = term.astype(BF16)
            outs[1 + q].start()
    sums = jnp.sum(scaled[...].astype(F32), axis=0, keepdims=True)
    bias_sum_ref[...] = jnp.concatenate([sums[:, k * E : (k + 1) * E] for k in range(8)], axis=0)
    rows(0).wait()
    cross[...] = jnp.dot(embedded[:, pl.ds(own_chunk(n), 1024)], weight[0], preferred_element_type=F32)
    base_ref[...] = lax.dot_general(scaled[...], weight[0], NT, preferred_element_type=F32)
    for q in (1, 2):
        if q > 1:
            rows(q).wait()
        cross[...] += jnp.dot(embedded[:, pl.ds(own_chunk(n ^ q), 1024)], weight[q], preferred_element_type=F32)
    rows(3).wait()
    get_cot.wait()
    grad = cot[...].astype(F32)
    last = jnp.dot(embedded[:, pl.ds(own_chunk(n ^ 3), 1024)], weight[3], preferred_element_type=F32)
    base_ref[...] += grad + grad * (cross[...] + last + bias_ref[...])
    for copy in outs:
        copy.wait()


def kept_terms(n, z, y, cotangent, embedded, weight, bias, scaled, turned, owner, row, bag):
    hbm = pl.BlockSpec(memory_space=pltpu.HBM)
    vmem = pl.BlockSpec(memory_space=pltpu.VMEM)
    samples, width = cotangent.shape
    depth = owner.shape[0]
    shape = jax.ShapeDtypeStruct
    results = pl.pallas_call(
        kept_kernel,
        out_shape=[
            shape((samples, width), F32),
            shape((depth * samples // E, E), jnp.int32),
            shape((2 * N_WIDE, CAP), F32),
            shape((8, E), F32),
            shape((samples, width), BF16),
        ]
        + [shape((256, 1024), BF16)] * 4,
        in_specs=[pl.BlockSpec(memory_space=pltpu.SMEM)] * 3 + [hbm] * 3 + [vmem, hbm, hbm] + [vmem] * 3,
        out_specs=[vmem] * 4 + [hbm] * 5,
        scratch_shapes=[
            pltpu.VMEM(cotangent.shape, BF16),
            pltpu.VMEM(embedded.shape, BF16),
            pltpu.VMEM((4, 1024, 1024), BF16),
            pltpu.VMEM((samples, width), BF16),
            pltpu.VMEM((width, samples), BF16),
            pltpu.VMEM((samples, width), F32),
            pltpu.VMEM((N_WIDE * depth, samples), BF16),
            pltpu.VMEM((samples, width), BF16),
            pltpu.VMEM((4, 256, 1024), BF16),
            pltpu.SemaphoreType.DMA((11,)),
            pltpu.SemaphoreType.DMA((5,)),
        ],
        compiler_params=pltpu.CompilerParams(vmem_limit_bytes=VMEM_MOST),
        cost_estimate=LIGHT,
        name="kept_terms",
    )(n, z, y, cotangent, embedded, weight, bias.reshape(1, -1), scaled, turned, owner, row, bag)
    return *results[:5], results[5:]


def own_kernel(z_ref, y_ref, embedded_hbm, turned_hbm, *refs):
    got_hbm, results, (embedded, turned, got, sems) = refs[:8], refs[8:12], refs[12:]
    z, y = z_ref[0], y_ref[0]
    loads = [(embedded_hbm, embedded), (turned_hbm, turned)]
    loads += [(got_hbm[k].at[pl.ds(256, 256), :], got.at[k]) for k in range(4)]
    loads += [(got_hbm[k], got.at[k]) for k in range(4, 8)]
    loads = [pltpu.make_async_copy(src, dst, sems.at[k]) for k, (src, dst) in enumerate(loads)]
    for load in loads:
        load.start()
    for load in loads:
        load.wait()
    for route, place in ((0, y), (1, z)):
        term = jnp.concatenate([term for _, term in ring_terms(route, turned[route * 512 : (route + 1) * 512, :], embedded, z, y, 0)], axis=1)
        up, down = 2 * route, 2 * route + 1
        total = jnp.concatenate(
            [
                term[:256, :] + got[4 + up].astype(F32) + got[down].astype(F32),
                term[256:, :] + got[4 + down].astype(F32) + got[up].astype(F32),
            ],
            axis=0,
        ).astype(BF16)
        total = jnp.transpose(total, (1, 0))
        high = place >= 2
        results[2 * route][...] = jnp.where(high, total[512:, :], total[:512, :])
        results[2 * route + 1][...] = jnp.where(high, total[:512, :], total[512:, :])


def own_terms(z, y, embedded, turned, first, second):
    hbm = pl.BlockSpec(memory_space=pltpu.HBM)
    vmem = pl.BlockSpec(memory_space=pltpu.VMEM)
    return pl.pallas_call(
        own_kernel,
        out_shape=[jax.ShapeDtypeStruct((512, 512), BF16)] * 4,
        in_specs=[pl.BlockSpec(memory_space=pltpu.SMEM)] * 2 + [hbm] + [pl.BlockSpec(memory_space=pl.ANY)] * 9,
        out_specs=[vmem] * 4,
        scratch_shapes=[
            pltpu.VMEM(embedded.shape, BF16),
            pltpu.VMEM(turned.shape, BF16),
            pltpu.VMEM((8, 256, 1024), BF16),
            pltpu.SemaphoreType.DMA((10,)),
        ],
        compiler_params=pltpu.CompilerParams(vmem_limit_bytes=VMEM_BYTES),
        cost_estimate=LIGHT,
        name="own_terms",
    )(z, y, embedded, turned, *first, *second)


def halves_of(array, bit, axis):
    size = array.shape[axis] // 2
    return (
        lax.dynamic_slice_in_dim(array, bit * size, size, axis),
        lax.dynamic_slice_in_dim(array, (1 - bit) * size, size, axis),
    )


def body(
    embedded,
    cotangent,
    cross_weight,
    cross_bias,
    bag_size,
    row_owner,
    row_id,
    emb_table,
    adagrad_state,
):
    panel = lax.axis_index("narrow")
    wide = lax.axis_index("wide")
    z, y, x_lo = wide // 8, (wide // 2) % 4, wide % 2
    core = panel % 2
    batch_rows = cotangent.shape[0]
    norm_factor = 1.0 / math.sqrt(batch_rows * N_WIDE)

    at = (panel.reshape(1), z.reshape(1), y.reshape(1))

    parts, first, scaled, turned = sent_terms(*at, cotangent, embedded, cross_weight)
    from_mate_far = lax.ppermute(parts[0], "narrow", CORE)
    ways = [z_perm(1), z_perm(3), y_perm(1), y_perm(3)]
    first = [lax.ppermute(first[q], "wide", ways[q]) for q in range(4)]
    chip_far = (parts[1].astype(F32) + from_mate_far.astype(F32)).astype(BF16)
    chip_far, scaled, turned = lax.optimization_barrier((chip_far, scaled, turned))
    far = lax.ppermute(chip_far, "narrow", X_HI)

    entries = (row_owner.reshape(row_owner.shape[1:3]).T, row_id.reshape(row_id.shape[1:]).T, bag_size.T)
    base, slots, ids, bias_part, part, second = kept_terms(
        *at, cotangent, embedded, cross_weight, cross_bias, scaled, turned, *entries
    )
    slots, ids, part, *first = lax.optimization_barrier((slots, ids, part, *first))
    from_mate = lax.ppermute(part, "narrow", CORE)
    second = passed_on(first, second)
    slots, far, *second = lax.optimization_barrier((slots, far, *second))
    second = [lax.ppermute(second[q], "wide", ways[q]) for q in range(4)]

    payload = place_entries(slots.reshape(-1), base, from_mate, far, ids, bias_part)
    payload, *second = lax.optimization_barrier((payload, *second))
    recv = lax.all_to_all(payload, "wide", split_axis=0, concat_axis=0, tiled=True)

    keep_y, send_y, keep_z, send_z = own_terms(at[1], at[2], embedded, turned, first, second)
    recv, send_y, send_z = lax.optimization_barrier((recv, send_y, send_z))
    got = [lax.ppermute(send_y, "wide", y_flip(2)), lax.ppermute(send_z, "wide", z_flip(2))]
    keep, send, bias_sums = owned_sums(norm_factor, core.reshape(1), recv)
    from_core = lax.ppermute(send, "narrow", CORE)
    keep, *got = lax.optimization_barrier((keep, *got))
    quarters = []
    for half, other, place in ((keep_y, got[0], y), (keep_z, got[1], z)):
        quarters.append([part.astype(BF16) for part in halves_of(summed(half, [other]), place % 2, 0)])
    got = [lax.ppermute(quarters[0][1], "wide", y_flip(1)), lax.ppermute(quarters[1][1], "wide", z_flip(1))]
    keep, from_core, *_ = lax.optimization_barrier((keep, from_core, quarters[0][1], quarters[1][1]))
    chip = summed(keep, [from_core]).astype(BF16)
    pair = jnp.concatenate([summed(quarters[0][0], got[:1]), summed(quarters[1][0], got[1:])], axis=1).astype(BF16)
    x_keep, x_send = halves_of(pair, x_lo, 0)
    other_chip, _ = lax.optimization_barrier((lax.ppermute(chip, "narrow", X_HI), x_send))
    x_got = lax.ppermute(jnp.pad(x_send, ((0, 8), (0, 0))), "wide", X_LO)[:E]

    bias_grad = bias_sums.reshape(-1)
    mine = summed(chip, [other_chip]).astype(BF16)
    mate, x_got = lax.optimization_barrier((lax.ppermute(mine, "narrow", CORE), x_got))
    weight_grad = summed(x_keep, [x_got]) * norm_factor
    row_grad = jnp.concatenate([jnp.where(core == 0, mine, mate), jnp.where(core == 0, mate, mine)], axis=0).astype(F32)
    new_state = adagrad_state + jnp.mean(row_grad * row_grad, axis=1)
    new_table = emb_table - LEARN_RATE * row_grad / jnp.sqrt(new_state)[:, None]
    return (weight_grad, bias_grad, new_table, new_state)


def solution(mesh):
    in_specs = (
        P("wide", None),
        P("wide", "narrow"),
        P(None, "narrow"),
        P("narrow"),
        P("wide", None),
        P("narrow", "wide", None, None),
        P("narrow", "wide", None),
        P("wide", None),
        P("wide"),
    )
    out_specs = (P("wide", "narrow"), P("narrow"), P("wide", None), P("wide"))
    return jax.shard_map(body, mesh=mesh, in_specs=in_specs, out_specs=out_specs, check_vma=False)
```
